32 devices in a mesh: heads: 16 (over z, x, core), frames: 2 (over y).
Axes of the slice: x: 2, y: 2, z: 4, core: 2. Of those that a mesh axis runs over, the one named last changes fastest.
Arguments:
- query: bfloat16 [4096, 2048], P(('frames', 'heads'))
- keys: bfloat16 [4096, 2048], P(('frames', 'heads'))
- values: bfloat16 [4096, 2048], P(('frames', 'heads')), may hold values from -6 to 6
- query_tan: bfloat16 [4096, 2048], P(('frames', 'heads')), may hold values from -6 to 6
- keys_tan: bfloat16 [4096, 2048], P(('frames', 'heads')), may hold values from -6 to 6
- values_tan: bfloat16 [4096, 2048], P(('frames', 'heads')), may hold values from -6 to 6
- neighbors: int32 [16, 4], P('frames'), may hold values from 0 to 15, as said below
Outputs:
- attended: bfloat16 [4096, 2048], P(('frames', 'heads'))
- attended_tan: bfloat16 [4096, 2048], P(('frames', 'heads'))
The draws below stay inside these ranges and needn't reach their ends.
Inputs may be any that keep to these rules, and one draw needn't show every extreme that they name: `neighbors`: entry 0 of row b is b itself; the other entries are min(max(b + o, 0), 15) for distinct nonzero offsets o between -4 and 4.
All inputs are finite; a program needn't handle non-finite values.
Results may differ from the reference program's by a relative error of at most 0.028.
Values may be sent and summed in bfloat16 or wider, within the bound.
No kernel may reach another device: no remote copies, remote signals or barrier semaphores. Data moves between devices by JAX's collectives and lax.ppermute only.
A program may use at most 192 MiB of HBM per device.

```python
import jax
import jax.numpy as jnp
from jax import lax

HD = 128
HEADS = 16
BQ = 256
WK = 4
HB = 4
TOKENS = 4096
NBLK = 16


def draw_query(key, part):
    key = jax.random.fold_in(key, 1)
    own = jax.random.normal(key, (TOKENS, HEADS * HD), jnp.float32)
    return jnp.clip(own, -6.0, 6.0).astype(jnp.bfloat16)


def draw_keys(key, part):
    key = jax.random.fold_in(key, 2)
    own = jax.random.normal(key, (TOKENS, HEADS * HD), jnp.float32)
    return jnp.clip(own, -6.0, 6.0).astype(jnp.bfloat16)


def draw_neighbors(key, part):
    key = jax.random.fold_in(key, 3)
    ranks = jax.random.randint(key, (NBLK, 2 * HB), 0, 1000, jnp.int32)
    ranks = ranks * (2 * HB) + jnp.arange(2 * HB, dtype=jnp.int32)[None, :]
    order = jnp.argsort(ranks, axis=1, stable=True).astype(jnp.int32)
    offsets = jnp.where(order < HB, order - HB, order - HB + 1)[:, :WK - 1]
    blocks = jnp.arange(NBLK, dtype=jnp.int32)[:, None]
    others = jnp.clip(blocks + offsets, 0, NBLK - 1)
    return jnp.concatenate([blocks, others], axis=1).astype(jnp.int32)


def steps_of(rng, shape, cuts, smallest, largest):
    factor_of = 1.0
    for position, shards_of in cuts:
        draws = jax.random.uniform(jax.random.fold_in(jax.random.fold_in(rng, 6), position), (shards_of,), jnp.float32, smallest / len(cuts), largest / len(cuts))
        factor_of = factor_of * jnp.repeat(jnp.exp(draws), shape[position] // shards_of).reshape((-1,) + (1,) * (len(shape) - 1 - position))
    return factor_of


def bell_draw(stream_key, shape, spread, most, cuts=(), kind=jnp.bfloat16):
    values = jax.random.normal(stream_key, shape, jnp.float32) * spread
    if len(cuts) > 0:
        values = steps_of(stream_key, shape, cuts, -0.22, 0.18) * values
    return jnp.clip(values, min=-most, max=most).astype(kind)


def setup_inputs(seed: int = 0) -> dict:
    key_of = jax.random.split(jax.random.key(seed), 8)
    return {
        "query": draw_query(jax.random.fold_in(key_of[7], 71), 0),
        "keys": draw_keys(jax.random.fold_in(key_of[7], 71), 0),
        "values": bell_draw(key_of[2], (TOKENS, HEADS * HD), 1.0, 6.0, ((0, 32),)),
        "query_tan": bell_draw(key_of[3], (TOKENS, HEADS * HD), 1.0, 6.0, ((0, 32),)),
        "keys_tan": bell_draw(key_of[4], (TOKENS, HEADS * HD), 1.0, 6.0, ((0, 32),)),
        "values_tan": bell_draw(key_of[5], (TOKENS, HEADS * HD), 1.0, 6.0, ((0, 32),)),
        "neighbors": draw_neighbors(jax.random.fold_in(key_of[7], 71), 0),
    }


def one_head(head, query, keys, values, query_tan, keys_tan, values_tan, neighbors):
    start = (head * HD).astype(jnp.int32)

    def cut(array):
        return lax.dynamic_slice_in_dim(array, start, HD, 1)

    def window(array):
        return cut(array).reshape(NBLK, BQ, HD)[neighbors].reshape(NBLK, WK * BQ, HD)

    scale = HD ** -0.5
    q_rows = cut(query).reshape(NBLK, BQ, HD).astype(jnp.float32)
    qt_rows = cut(query_tan).reshape(NBLK, BQ, HD).astype(jnp.float32)
    k_win = window(keys).astype(jnp.float32)
    kt_win = window(keys_tan).astype(jnp.float32)
    v_win = window(values).astype(jnp.float32)
    vt_win = window(values_tan).astype(jnp.float32)
    scores = jnp.einsum("nqd,nkd->nqk", q_rows, k_win) * scale
    probs = jax.nn.softmax(scores, axis=-1)
    probs16 = probs.astype(jnp.bfloat16).astype(jnp.float32)
    out = jnp.einsum("nqk,nkd->nqd", probs16, v_win)
    score_tan = (jnp.einsum("nqd,nkd->nqk", qt_rows, k_win) + jnp.einsum("nqd,nkd->nqk", q_rows, kt_win)) * scale
    weighted = probs * score_tan
    mean_tan = jnp.sum(weighted, axis=-1, keepdims=True)
    weighted16 = weighted.astype(jnp.bfloat16).astype(jnp.float32)
    tan = jnp.einsum("nqk,nkd->nqd", probs16, vt_win) + jnp.einsum("nqk,nkd->nqd", weighted16, v_win) - mean_tan * out
    return out.reshape(TOKENS, HD).astype(jnp.bfloat16), tan.reshape(TOKENS, HD).astype(jnp.bfloat16)


def reference(query, keys, values, query_tan, keys_tan, values_tan, neighbors):
    def step(head):
        return one_head(head, query, keys, values, query_tan, keys_tan, values_tan, neighbors)

    outs, tans = lax.map(step, jnp.arange(HEADS, dtype=jnp.int32))
    attended = jnp.transpose(outs, (1, 0, 2)).reshape(TOKENS, HEADS * HD)
    attended_tan = jnp.transpose(tans, (1, 0, 2)).reshape(TOKENS, HEADS * HD)
    return attended, attended_tan
```

```python
import functools
import math

import jax
import jax.numpy as jnp
from jax import lax
from jax.experimental import pallas as pl
from jax.experimental.pallas import tpu as pltpu
from jax.sharding import PartitionSpec as P

BQ = 256
WK = 4
HB = 4
HALO = HB * BQ


def attend_kernel(table, q_ref, kv_hbm, *rest, halos, hd):
    halo_hbm, (o_ref, kv, sem) = rest[:halos], rest[halos:]
    step = pl.program_id(0)
    rows = kv_hbm.shape[0]

    @pl.when(step == 0)
    def load():
        copies = [pltpu.make_async_copy(kv_hbm, kv.at[pl.ds(0, rows)], sem.at[0])]
        for i, ref in enumerate(halo_hbm):
            copies.append(
                pltpu.make_async_copy(ref, kv.at[pl.ds(rows + i * HALO, HALO)], sem.at[1 + i])
            )
        for copy in copies:
            copy.start()
        for copy in copies:
            copy.wait()

    scale = hd ** (-0.5)
    factor = scale * math.log2(math.e)
    trans = (((1,), (1,)), ((), ()))
    both = q_ref[...]
    query = both[:, :hd]
    starts = [pl.multiple_of(table[step * WK + w] * BQ, BQ) for w in range(WK)]
    scores, tans = [], []
    for start in starts:
        keys = kv[pl.ds(start, BQ), : 2 * hd]
        scores.append(
            lax.dot_general(query, keys[:, hd:], trans, preferred_element_type=jnp.float32)
        )
        tans.append(lax.dot_general(both, keys, trans, preferred_element_type=jnp.float32))
    top = functools.reduce(jnp.maximum, scores)
    top = jnp.max(top, axis=1, keepdims=True) * factor
    probs = [jnp.exp2(s * factor - top) for s in scores]
    weighted = [p * t for p, t in zip(probs, tans)]
    total = jnp.sum(functools.reduce(jnp.add, probs), axis=1, keepdims=True)
    mean = jnp.sum(functools.reduce(jnp.add, weighted), axis=1, keepdims=True)
    main, side = 0.0, 0.0
    for start, p, w in zip(starts, probs, weighted):
        vals = kv[pl.ds(start, BQ), 2 * hd :]
        main += jnp.dot(p.astype(jnp.bfloat16), vals, preferred_element_type=jnp.float32)
        side += jnp.dot(w.astype(jnp.bfloat16), vals[:, :hd], preferred_element_type=jnp.float32)
    inverse = 1.0 / total
    out = main[:, :hd] * inverse
    tan = (main[:, hd:] + scale * side) * inverse - (scale * mean * inverse) * out
    o_ref[:, :hd] = out.astype(jnp.bfloat16)
    o_ref[:, hd:] = tan.astype(jnp.bfloat16)


def attend(table, q_pair, kv, halos):
    rows, width = q_pair.shape
    hd = width // 2
    blocks = rows // BQ
    total = rows + len(halos) * HALO
    elements = rows * WK * BQ
    return pl.pallas_call(
        functools.partial(attend_kernel, halos=len(halos), hd=hd),
        grid_spec=pltpu.PrefetchScalarGridSpec(
            num_scalar_prefetch=1,
            grid=(blocks,),
            in_specs=[pl.BlockSpec((BQ, width), lambda i, t: (i, 0))]
            + [pl.BlockSpec(memory_space=pl.ANY)] * (1 + len(halos)),
            out_specs=pl.BlockSpec((BQ, width), lambda i, t: (i, 0)),
            scratch_shapes=[
                pltpu.VMEM((total, 4 * hd), jnp.bfloat16),
                pltpu.SemaphoreType.DMA((1 + len(halos),)),
            ],
        ),
        out_shape=jax.ShapeDtypeStruct((rows, width), jnp.bfloat16),
        compiler_params=pltpu.CompilerParams(vmem_limit_bytes=32 * 1024 * 1024),
        cost_estimate=pl.CostEstimate(
            flops=12 * elements * hd,
            bytes_accessed=2 * (total * 4 * hd + 2 * rows * width),
            transcendentals=elements,
        ),
    )(table, q_pair, kv, *halos)


def to_heads(arrays, devices):
    tokens, columns = arrays[0].shape
    hd = columns // devices
    parts = [a.reshape(tokens, devices, hd).transpose(1, 0, 2) for a in arrays]
    sent = jnp.concatenate(parts, axis=2)
    got = lax.all_to_all(sent, "heads", split_axis=0, concat_axis=0, tiled=True)
    return got.reshape(devices * tokens, len(arrays) * hd)


def exchange(kv, frame, frames):
    rows = kv.shape[0]
    halos = []
    for first in (0, 1):
        pairs = [(i, i + 1) for i in range(first, frames - 1, 2)]
        if not pairs:
            continue
        start = jnp.where(frame % 2 == first, rows - HALO, 0)
        edge = lax.dynamic_slice_in_dim(kv, start, HALO, axis=0)
        halos.append(lax.ppermute(edge, "frames", pairs + [(j, i) for i, j in pairs]))
    return halos


def slots(neighbors, frame, blocks):
    local = neighbors - frame * blocks
    even = frame % 2 == 0
    before = blocks + jnp.where(even, HB, 0) + local + HB
    after = blocks + jnp.where(even, 0, HB) + local - blocks
    return jnp.where(local < 0, before, jnp.where(local >= blocks, after, local)).reshape(-1)


def per_device(query, keys, values, query_tan, keys_tan, values_tan, neighbors):
    devices, frames = lax.axis_size("heads"), lax.axis_size("frames")
    frame = lax.axis_index("frames")
    tokens, columns = query.shape
    hd = columns // devices
    kv = to_heads([keys_tan, keys, values, values_tan], devices)
    halos = exchange(kv, frame, frames)
    q_pair = to_heads([query, query_tan], devices)
    table = slots(neighbors, frame, neighbors.shape[0])
    pair = attend(table, q_pair, kv, halos).reshape(devices, tokens, 2 * hd)
    back = lax.all_to_all(pair, "heads", split_axis=0, concat_axis=0, tiled=True)
    back = back.reshape(devices, tokens, 2, hd).transpose(2, 1, 0, 3)
    back = back.reshape(2, tokens, columns)
    return back[0], back[1]


def solution(mesh):
    own = P(("frames", "heads"), None)
    return jax.shard_map(
        per_device,
        mesh=mesh,
        in_specs=(own,) * 6 + (P("frames", None),),
        out_specs=(own, own),
        check_vma=False,
    )
```

```python
import functools
import math

import jax
import jax.numpy as jnp
from jax import lax
from jax.experimental import pallas as pl
from jax.experimental.pallas import tpu as pltpu
from jax.sharding import PartitionSpec as P

BQ = 256
WK = 4
HB = 4
VMEM_LIMIT = 32 * 1024 * 1024
ANY = pl.BlockSpec(memory_space=pl.ANY)
VMEM = pl.BlockSpec(memory_space=pltpu.VMEM)
SMEM = pl.BlockSpec(memory_space=pltpu.SMEM)


def finish(copies):
    for copy in copies:
        copy.start()
    for copy in copies:
        copy.wait()


def pack_kernel(me, *refs, count, hd):
    arrays, pieces, sems = refs[:count], refs[count:-1], refs[-1]
    copies = []
    for k, piece in enumerate(pieces):
        column = pl.multiple_of((me[0] ^ k) * hd, hd)
        for a, array in enumerate(arrays):
            source = array.at[:, pl.ds(column, hd)]
            copies.append(
                pltpu.make_async_copy(source, piece.at[:, pl.ds(a * hd, hd)], sems.at[k, a])
            )
    finish(copies)


def pack(me, arrays, devices):
    tokens, columns = arrays[0].shape
    hd, count = columns // devices, len(arrays)
    piece = jax.ShapeDtypeStruct((tokens, count * hd), jnp.bfloat16)
    size = 2 * tokens * columns * count
    return pl.pallas_call(
        functools.partial(pack_kernel, count=count, hd=hd),
        in_specs=[SMEM] + [ANY] * count,
        out_specs=[ANY] * devices,
        out_shape=[piece] * devices,
        scratch_shapes=[pltpu.SemaphoreType.DMA((devices, count))],
        cost_estimate=pl.CostEstimate(flops=0, bytes_accessed=2 * size, transcendentals=0),
    )(me, *arrays)


def unpack_kernel(me, *refs, count, hd):
    pieces, arrays, sems = refs[: -count - 1], refs[-count - 1 : -1], refs[-1]
    copies = []
    for k, piece in enumerate(pieces):
        column = pl.multiple_of((me[0] ^ k) * hd, hd)
        for a, array in enumerate(arrays):
            target = array.at[:, pl.ds(column, hd)]
            copies.append(
                pltpu.make_async_copy(piece.at[:, pl.ds(a * hd, hd)], target, sems.at[k, a])
            )
    finish(copies)


def unpack(me, pieces, count):
    tokens, width = pieces[0].shape
    devices, hd = len(pieces), width // count
    array = jax.ShapeDtypeStruct((tokens, devices * hd), jnp.bfloat16)
    size = 2 * tokens * width * devices
    return pl.pallas_call(
        functools.partial(unpack_kernel, count=count, hd=hd),
        in_specs=[SMEM] + [ANY] * devices,
        out_specs=[ANY] * count,
        out_shape=[array] * count,
        scratch_shapes=[pltpu.SemaphoreType.DMA((devices, count))],
        cost_estimate=pl.CostEstimate(flops=0, bytes_accessed=2 * size, transcendentals=0),
    )(me, *pieces)


def edge_kernel(group, *refs):
    pieces, out, sems = refs[:-2], refs[-2], refs[-1]
    tokens = pieces[0].shape[0]
    per = out.shape[0] // tokens
    for g in range(len(pieces) // per):

        @pl.when(group[0] == g)
        def copy(g=g):
            finish(
                [
                    pltpu.make_async_copy(
                        pieces[g * per + i], out.at[pl.ds(i * tokens, tokens)], sems.at[i]
                    )
                    for i in range(per)
                ]
            )


def edge(group, pieces):
    tokens, width = pieces[0].shape
    rows = HB * BQ
    return pl.pallas_call(
        edge_kernel,
        in_specs=[SMEM] + [ANY] * len(pieces),
        out_specs=ANY,
        out_shape=jax.ShapeDtypeStruct((rows, width), jnp.bfloat16),
        scratch_shapes=[pltpu.SemaphoreType.DMA((rows // tokens,))],
        cost_estimate=pl.CostEstimate(
            flops=0, bytes_accessed=4 * rows * width, transcendentals=0
        ),
    )(group, *pieces)


def attend_kernel(table, *refs, count, own, halos, hd, first):
    q_refs, refs = refs[:count], refs[count:]
    pieces, refs = refs[:own], refs[own:]
    halo_refs, refs = refs[:halos], refs[halos:]
    outs, kv, sems = refs[:count], refs[count], refs[count + 1]
    tokens = q_refs[0].shape[0]
    per = BQ // tokens
    copies, row = [], 0
    for i, ref in enumerate(pieces + halo_refs):
        rows = ref.shape[0]
        copies.append(pltpu.make_async_copy(ref, kv.at[pl.ds(row, rows)], sems.at[i]))
        row += rows
    finish(copies)

    scale = hd ** (-0.5)
    factor = scale * math.log2(math.e)
    trans = (((1,), (1,)), ((), ()))
    for b in range(count // per):
        both = jnp.concatenate([q_refs[b * per + i][...] for i in range(per)], axis=0)
        query = both[:, :hd]
        starts = [pl.multiple_of(table[first + b, w] * BQ, BQ) for w in range(WK)]
        scores, tans = [], []
        for start in starts:
            keys = kv[pl.ds(start, BQ), : 2 * hd]
            scores.append(
                lax.dot_general(query, keys[:, hd:], trans, preferred_element_type=jnp.float32)
            )
            tans.append(lax.dot_general(both, keys, trans, preferred_element_type=jnp.float32))
        top = functools.reduce(jnp.maximum, scores)
        top = jnp.max(top, axis=1, keepdims=True) * factor
        probs = [jnp.exp2(s * factor - top) for s in scores]
        weighted = [p * t for p, t in zip(probs, tans)]
        total = jnp.sum(functools.reduce(jnp.add, probs), axis=1, keepdims=True)
        mean = jnp.sum(functools.reduce(jnp.add, weighted), axis=1, keepdims=True)
        main, side = 0.0, 0.0
        for start, p, w in zip(starts, probs, weighted):
            vals = kv[pl.ds(start, BQ), 2 * hd :]
            main += jnp.dot(p.astype(jnp.bfloat16), vals, preferred_element_type=jnp.float32)
            side += jnp.dot(
                w.astype(jnp.bfloat16), vals[:, :hd], preferred_element_type=jnp.float32
            )
        inverse = 1.0 / total
        out = main[:, :hd] * inverse
        tan = (main[:, hd:] + scale * side) * inverse - (scale * mean * inverse) * out
        out, tan = out.astype(jnp.bfloat16), tan.astype(jnp.bfloat16)
        for i in range(per):
            outs[b * per + i][:, :hd] = out[i * tokens : (i + 1) * tokens]
            outs[b * per + i][:, hd:] = tan[i * tokens : (i + 1) * tokens]


def attend(table, first, queries, pieces, halos):
    tokens, width = queries[0].shape
    hd = width // 2
    total = sum(a.shape[0] for a in pieces) + sum(a.shape[0] for a in halos)
    rows = tokens * len(queries)
    elements = rows * WK * BQ
    return pl.pallas_call(
        functools.partial(
            attend_kernel,
            count=len(queries),
            own=len(pieces),
            halos=len(halos),
            hd=hd,
            first=first,
        ),
        in_specs=[SMEM] + [VMEM] * len(queries) + [ANY] * (len(pieces) + len(halos)),
        out_specs=[VMEM] * len(queries),
        out_shape=[jax.ShapeDtypeStruct((tokens, width), jnp.bfloat16)] * len(queries),
        scratch_shapes=[
            pltpu.VMEM((total, 4 * hd), jnp.bfloat16),
            pltpu.SemaphoreType.DMA((len(pieces) + len(halos),)),
        ],
        compiler_params=pltpu.CompilerParams(vmem_limit_bytes=VMEM_LIMIT),
        cost_estimate=pl.CostEstimate(
            flops=12 * elements * hd,
            bytes_accessed=2 * (total * 4 * hd + 2 * rows * width),
            transcendentals=elements,
        ),
    )(table, *queries, *pieces, *halos)


def send(pieces, slots, devices):
    got = {}
    for k in slots:
        pairs = [(i, i ^ k) for i in range(devices)]
        got[k] = lax.ppermute(pieces[k], "heads", pairs) if k else pieces[k]
    return got


def per_device(query, keys, values, query_tan, keys_tan, values_tan, neighbors):
    devices, frames = lax.axis_size("heads"), lax.axis_size("frames")
    index, frame = lax.axis_index("heads"), lax.axis_index("frames")
    tokens = query.shape[0]
    blocks = neighbors.shape[0]
    per = BQ // tokens
    me = index.reshape(1).astype(jnp.int32)
    chip = index // per
    far = list(range(devices // 2, devices))
    near = list(range(devices // 2 - 1, -1, -1))

    sent = pack(me, [keys_tan, keys, values, values_tan], devices)
    got = send(sent, far + near, devices)
    kv = [got[k] for k in range(devices)]
    q_sent = pack(me, [query, query_tan], devices)
    q_got = send(q_sent, far + near, devices)

    halos = []
    for first in (0, 1):
        pairs = [(i, i + 1) for i in range(first, frames - 1, 2)]
        if not pairs:
            continue
        group = jnp.where(frame % 2 == first, blocks // HB - 1, 0) ^ (chip // HB)
        outer = edge(group.reshape(1).astype(jnp.int32), kv)
        halos.append(lax.ppermute(outer, "frames", pairs + [(j, i) for i, j in pairs]))

    local = neighbors - frame * blocks
    even = frame % 2 == 0
    before = blocks + jnp.where(even, HB, 0) + ((local + blocks) ^ chip) % HB
    after = blocks + jnp.where(even, 0, HB) + ((local - blocks) ^ chip) % HB
    table = jnp.where(local < 0, before, jnp.where(local >= blocks, after, local ^ chip))
    table = table[jnp.arange(blocks) ^ chip]

    half = blocks // 2
    outs = {}
    for low, high in ((half, half + half // 2), (half + half // 2, blocks), (0, half)):
        slots = range(low * per, high * per)
        done = attend(table, low, [q_got[k] for k in slots], kv, halos)
        outs.update(send(dict(zip(slots, done)), slots, devices))
    return unpack(me, [outs[k] for k in range(devices)], 2)


def solution(mesh):
    own = P(("frames", "heads"), None)
    return jax.shard_map(
        per_device,
        mesh=mesh,
        in_specs=(own,) * 6 + (P("frames", None),),
        out_specs=(own, own),
        check_vma=False,
    )
```

```python
import functools
import math

import jax
import jax.numpy as jnp
from jax import lax
from jax.experimental import pallas as pl
from jax.experimental.pallas import tpu as pltpu
from jax.sharding import PartitionSpec as P

BQ = 256
WK = 4
HB = 4
PAIR = 2
PARAMS = pltpu.CompilerParams(vmem_limit_bytes=32 * 1024 * 1024)
ANY = pl.BlockSpec(memory_space=pl.ANY)
VMEM = pl.BlockSpec(memory_space=pltpu.VMEM)
SMEM = pl.BlockSpec(memory_space=pltpu.SMEM)


def moves(size):
    return pl.CostEstimate(flops=0, bytes_accessed=2 * size, transcendentals=0)


def pack_kernel(chip, *refs, counts, slots, hd):
    total = sum(counts)
    arrays, pieces = refs[:total], refs[total : total + slots * len(counts)]
    held, sems = refs[-2], refs[-1]
    copies = [pltpu.make_async_copy(a, held.at[i], sems.at[i]) for i, a in enumerate(arrays)]
    for copy in copies:
        copy.start()
    base = 0
    for g, count in enumerate(counts):
        for a in range(count):
            copies[base + a].wait()
            for k in range(slots):
                for h in range(PAIR):
                    column = pl.multiple_of(((chip[0] ^ k) * PAIR + h) * hd, hd)
                    target = (h * count + a) * hd
                    pieces[g * slots + k][:, target : target + hd] = held[
                        base + a, :, pl.ds(column, hd)
                    ]
        base += count


def pack(chip, groups, devices):
    arrays = [a for group in groups for a in group]
    tokens, columns = arrays[0].shape
    hd, slots = columns // devices, devices // PAIR
    counts = tuple(len(group) for group in groups)
    shapes = [
        jax.ShapeDtypeStruct((tokens, PAIR * count * hd), jnp.bfloat16)
        for count in counts
        for _ in range(slots)
    ]
    done = pl.pallas_call(
        functools.partial(pack_kernel, counts=counts, slots=slots, hd=hd),
        in_specs=[SMEM] + [ANY] * len(arrays),
        out_specs=[VMEM] * len(shapes),
        out_shape=shapes,
        scratch_shapes=[
            pltpu.VMEM((len(arrays), tokens, columns), jnp.bfloat16),
            pltpu.SemaphoreType.DMA((len(arrays),)),
        ],
        compiler_params=PARAMS,
        cost_estimate=moves(2 * tokens * columns * len(arrays)),
    )(chip, *arrays)
    return [done[g * slots : (g + 1) * slots] for g in range(len(groups))]


def unpack_kernel(chip, *refs, count, hd):
    pieces, arrays = refs[:-count], refs[-count:]
    for k, piece in enumerate(pieces):
        for h in range(PAIR):
            column = pl.multiple_of(((chip[0] ^ k) * PAIR + h) * hd, hd)
            for a, array in enumerate(arrays):
                source = (h * count + a) * hd
                array[:, pl.ds(column, hd)] = piece[:, source : source + hd]


def unpack(chip, pieces, count):
    tokens, width = pieces[0].shape
    hd = width // (PAIR * count)
    array = jax.ShapeDtypeStruct((tokens, len(pieces) * PAIR * hd), jnp.bfloat16)
    return pl.pallas_call(
        functools.partial(unpack_kernel, count=count, hd=hd),
        in_specs=[SMEM] + [VMEM] * len(pieces),
        out_specs=[VMEM] * count,
        out_shape=[array] * count,
        compiler_params=PARAMS,
        cost_estimate=moves(2 * tokens * width * len(pieces)),
    )(chip, *pieces)


def join_kernel(groups, *refs, slots):
    pieces, own, edges = refs[:slots], refs[slots], refs[slots + 1 :]
    for k, piece in enumerate(pieces):
        own[k] = piece[...]
    for e, out in enumerate(edges):
        for i in range(HB):
            out[i] = own[groups[e] * HB + i]


def join(groups, pieces):
    tokens, width = pieces[0].shape
    count = groups.shape[0]
    return pl.pallas_call(
        functools.partial(join_kernel, slots=len(pieces)),
        in_specs=[SMEM] + [VMEM] * len(pieces),
        out_specs=[VMEM] * (1 + count),
        out_shape=[jax.ShapeDtypeStruct((len(pieces), tokens, width), jnp.bfloat16)]
        + [jax.ShapeDtypeStruct((HB, tokens, width), jnp.bfloat16)] * count,
        compiler_params=PARAMS,
        cost_estimate=moves(2 * (len(pieces) + count * HB) * tokens * width),
    )(groups, *pieces)


def attend_slot(table, slot, q_ref, kv, out_ref, hd):
    tokens = q_ref.shape[0]
    scale = hd ** (-0.5)
    factor = scale * math.log2(math.e)
    trans = (((1,), (1,)), ((), ()))
    blocks = [table[slot, w] for w in range(WK)]
    for h in range(PAIR):
        both = q_ref[:, 2 * h * hd : 2 * (h + 1) * hd]
        query = both[:, :hd]
        left = jnp.concatenate([jnp.zeros_like(query), query], axis=1)
        left = jnp.concatenate([left, both], axis=0)
        low = 4 * h * hd
        scores, tans = [], []
        for block in blocks:
            keys = kv[block, :, :, low : low + 2 * hd].reshape(BQ, 2 * hd)
            product = lax.dot_general(left, keys, trans, preferred_element_type=jnp.float32)
            scores.append(product[:tokens])
            tans.append(product[tokens:])
        top = functools.reduce(jnp.maximum, scores)
        top = jnp.max(top, axis=1, keepdims=True) * factor
        probs = [jnp.exp2(s * factor - top) for s in scores]
        weighted = [p * t for p, t in zip(probs, tans)]
        total = jnp.sum(functools.reduce(jnp.add, probs), axis=1, keepdims=True)
        mean = jnp.sum(functools.reduce(jnp.add, weighted), axis=1, keepdims=True)
        mixed = jnp.zeros((2 * tokens, 2 * hd), jnp.float32)
        for block, p, w in zip(blocks, probs, weighted):
            vals = kv[block, :, :, low + 2 * hd : low + 4 * hd].reshape(BQ, 2 * hd)
            right = jnp.concatenate([p.astype(jnp.bfloat16), w.astype(jnp.bfloat16)], axis=0)
            mixed += jnp.dot(right, vals, preferred_element_type=jnp.float32)
        inverse = 1.0 / total
        out = mixed[:tokens, :hd] * inverse
        tan = (mixed[:tokens, hd:] + scale * mixed[tokens:, :hd]) * inverse
        tan = tan - (scale * mean * inverse) * out
        out_ref[:, 2 * h * hd : (2 * h + 1) * hd] = out.astype(jnp.bfloat16)
        out_ref[:, (2 * h + 1) * hd : 2 * (h + 1) * hd] = tan.astype(jnp.bfloat16)


def first_kernel(table, *refs, count, sources, hd, first):
    q_refs, refs = refs[:count], refs[count:]
    mine, other, refs = refs[:sources], refs[sources : 2 * sources], refs[2 * sources :]
    outs, kv = refs[:count], refs[count]
    row = 0
    for a, b in zip(mine, other):
        for i in range(a.shape[0]):
            kv[row + i, 0] = a[i]
            kv[row + i, 1] = b[i]
        row += a.shape[0]
    for i in range(count):
        attend_slot(table, first + i, q_refs[i], kv, outs[i], hd)


def next_kernel(table, *refs, count, hd, first):
    q_refs, kv, outs = refs[:count], refs[count], refs[count + 1 :]
    for i in range(count):
        attend_slot(table, first + i, q_refs[i], kv, outs[i], hd)


def hold_kernel(*refs):
    del refs


def hold(array, others):
    return pl.pallas_call(
        hold_kernel,
        in_specs=[ANY] * (1 + len(others)),
        out_specs=ANY,
        out_shape=jax.ShapeDtypeStruct(array.shape, array.dtype),
        input_output_aliases={0: 0},
        cost_estimate=moves(0),
    )(array, *others)


def cost(slots, tokens, hd, size):
    elements = slots * PAIR * tokens * WK * BQ
    return pl.CostEstimate(
        flops=16 * elements * hd, bytes_accessed=size, transcendentals=elements
    )


def attend_first(table, first, queries, mine, other):
    tokens, width = queries[0].shape
    hd = width // (2 * PAIR)
    total = sum(a.shape[0] for a in mine)
    count = len(queries)
    kv = jax.ShapeDtypeStruct((total, PAIR, tokens, 2 * width), jnp.bfloat16)
    done = pl.pallas_call(
        functools.partial(first_kernel, count=count, sources=len(mine), hd=hd, first=first),
        in_specs=[SMEM] + [VMEM] * (count + 2 * len(mine)),
        out_specs=[VMEM] * (count + 1),
        out_shape=[jax.ShapeDtypeStruct((tokens, width), jnp.bfloat16)] * count + [kv],
        compiler_params=PARAMS,
        cost_estimate=cost(count, tokens, hd, 2 * kv.size * 2),
    )(table, *queries, *mine, *other)
    return done[:count], done[count]


def attend_next(table, first, queries, kv):
    tokens, width = queries[0].shape
    hd = width // (2 * PAIR)
    count = len(queries)
    return pl.pallas_call(
        functools.partial(next_kernel, count=count, hd=hd, first=first),
        in_specs=[SMEM] + [VMEM] * (count + 1),
        out_specs=[VMEM] * count,
        out_shape=[jax.ShapeDtypeStruct((tokens, width), jnp.bfloat16)] * count,
        compiler_params=PARAMS,
        cost_estimate=cost(count, tokens, hd, 2 * kv.size),
    )(table, *queries, kv)


def send(pieces, order, devices):
    got = {}
    for k in order:
        pairs = [(i, i ^ (k * PAIR)) for i in range(devices)]
        got[k] = lax.ppermute(pieces[k], "heads", pairs) if k else pieces[k]
    return got


def per_device(query, keys, values, query_tan, keys_tan, values_tan, neighbors):
    devices, frames = lax.axis_size("heads"), lax.axis_size("frames")
    frame = lax.axis_index("frames")
    chip = lax.axis_index("heads") // PAIR
    blocks = neighbors.shape[0]
    half = blocks // 2
    far, near = list(range(half, blocks)), list(range(1, half))
    order = [k for pair in zip(far, near + [0]) for k in pair]

    groups = [[keys_tan, keys, values, values_tan], [query, query_tan]]
    chip_ref = chip.reshape(1).astype(jnp.int32)
    kv_sent, q_sent = pack(chip_ref, groups, devices)
    got = send(kv_sent, order, devices)
    q_got = send(q_sent, order, devices)

    rounds = []
    for first in (0, 1):
        pairs = [(i, i + 1) for i in range(first, frames - 1, 2)]
        if pairs:
            rounds.append((first, pairs + [(j, i) for i, j in pairs]))
    outer = [
        jnp.where(frame % 2 == first, blocks // HB - 1, 0) ^ (chip // HB) for first, _ in rounds
    ]
    joined = join(jnp.stack(outer).astype(jnp.int32), [got[k] for k in range(blocks)])
    mine = [joined[0]]
    for (_, pairs), edge in zip(rounds, joined[1:]):
        halo = lax.ppermute(edge, "frames", pairs)
        mine.append(hold(halo, [q_got[k] for k in range(1, blocks)]))
    swap = [(i, i ^ 1) for i in range(devices)]
    other = [lax.ppermute(a, "heads", swap) for a in mine]

    local = neighbors - frame * blocks
    even = frame % 2 == 0
    before = blocks + jnp.where(even, HB, 0) + ((local + blocks) ^ chip) % HB
    after = blocks + jnp.where(even, 0, HB) + ((local - blocks) ^ chip) % HB
    table = jnp.where(local < 0, before, jnp.where(local >= blocks, after, local ^ chip))
    table = table[jnp.arange(blocks) ^ chip]

    quarter = half // 2
    queries = [q_got[k] for k in range(blocks)]
    outs = {}
    done, kv = attend_first(table, half, queries[half : half + quarter], mine, other)
    outs.update(enumerate(done, half))
    done = attend_next(table, half + quarter, queries[half + quarter :], kv)
    outs.update(enumerate(done, half + quarter))
    done = attend_next(table, 0, queries[:half], kv)
    outs.update(enumerate(done))
    back = send(outs, far + near + [0], devices)
    return unpack(chip_ref, [back[k] for k in range(blocks)], 2)


def solution(mesh):
    own = P(("frames", "heads"), None)
    return jax.shard_map(
        per_device,
        mesh=mesh,
        in_specs=(own,) * 6 + (P("frames", None),),
        out_specs=(own, own),
        check_vma=False,
    )
```

```python
import functools
import math

import jax
import jax.numpy as jnp
from jax import lax
from jax.experimental import pallas as pl
from jax.experimental.pallas import tpu as pltpu
from jax.sharding import PartitionSpec as P

BQ = 256
WK = 4
HB = 4
PAIR = 2
PARAMS = pltpu.CompilerParams(vmem_limit_bytes=40 * 1024 * 1024)
ANY = pl.BlockSpec(memory_space=pl.ANY)
HBM = pl.BlockSpec(memory_space=pltpu.HBM)
SMEM = pl.BlockSpec(memory_space=pltpu.SMEM)
FREE = pl.CostEstimate(flops=0, bytes_accessed=0, transcendentals=0)


def half(*shape):
    return pltpu.HBM(shape, jnp.bfloat16)


def pin(*arrays):
    return [pltpu.with_memory_space_constraint(a, pltpu.HBM) for a in arrays]


def hold_kernel(*refs):
    del refs


def hold(array, others, micros=0):
    return pl.pallas_call(
        hold_kernel,
        in_specs=[ANY] * (1 + len(others)),
        out_specs=ANY,
        out_shape=jax.ShapeDtypeStruct(array.shape, array.dtype),
        input_output_aliases={0: 0},
        cost_estimate=pl.CostEstimate(
            flops=0, bytes_accessed=3_000_000 * micros, transcendentals=0
        ),
    )(array, *others)


def pack_kernel(chip, *refs, count, slots, hd):
    arrays, pieces = refs[:count], refs[count : count + slots]
    held, staged, sems, out_sems = refs[-4:]
    copies = [pltpu.make_async_copy(a, held.at[i], sems.at[i]) for i, a in enumerate(arrays)]
    for copy in copies:
        copy.start()
    for copy in copies:
        copy.wait()
    sends = []
    for k in range(slots):
        for h in range(PAIR):
            column = pl.multiple_of(((chip[0] ^ k) * PAIR + h) * hd, hd)
            for a in range(count):
                target = (h * count + a) * hd
                staged[k, :, target : target + hd] = held[a, :, pl.ds(column, hd)]
        sends.append(pltpu.make_async_copy(staged.at[k], pieces[k], out_sems.at[k]))
        sends[-1].start()
    for copy in sends:
        copy.wait()


def pack(chip, arrays, devices):
    tokens, columns = arrays[0].shape
    hd, slots, count = columns // devices, devices // PAIR, len(arrays)
    width = PAIR * count * hd
    return pl.pallas_call(
        functools.partial(pack_kernel, count=count, slots=slots, hd=hd),
        in_specs=[SMEM] + [HBM] * count,
        out_specs=[HBM] * slots,
        out_shape=[half(tokens, width)] * slots,
        scratch_shapes=[
            pltpu.VMEM((count, tokens, columns), jnp.bfloat16),
            pltpu.VMEM((slots, tokens, width), jnp.bfloat16),
            pltpu.SemaphoreType.DMA((count,)),
            pltpu.SemaphoreType.DMA((slots,)),
        ],
        compiler_params=PARAMS,
        cost_estimate=FREE,
    )(chip, *pin(*arrays))


def unpack_kernel(chip, *refs, order, count, hd):
    slots = len(order)
    pieces, arrays = refs[:slots], refs[slots : slots + count]
    held, staged, sems, out_sems = refs[-4:]
    copies = [pltpu.make_async_copy(p, held.at[k], sems.at[k]) for k, p in zip(order, pieces)]
    for copy in copies:
        copy.start()
    for k, copy in zip(order, copies):
        copy.wait()
        for h in range(PAIR):
            column = pl.multiple_of(((chip[0] ^ k) * PAIR + h) * hd, hd)
            for a in range(count):
                source = (h * count + a) * hd
                staged[a, :, pl.ds(column, hd)] = held[k, :, source : source + hd]
    sends = [pltpu.make_async_copy(staged.at[a], r, out_sems.at[a]) for a, r in enumerate(arrays)]
    for copy in sends:
        copy.start()
    for copy in sends:
        copy.wait()


def unpack(chip, pieces, count, order):
    tokens, width = pieces[0].shape
    slots, hd = len(pieces), width // (PAIR * count)
    columns = slots * PAIR * hd
    return pl.pallas_call(
        functools.partial(unpack_kernel, order=order, count=count, hd=hd),
        in_specs=[SMEM] + [ANY] * slots,
        out_specs=[HBM] * count,
        out_shape=[half(tokens, columns)] * count,
        scratch_shapes=[
            pltpu.VMEM((slots, tokens, width), jnp.bfloat16),
            pltpu.VMEM((count, tokens, columns), jnp.bfloat16),
            pltpu.SemaphoreType.DMA((slots,)),
            pltpu.SemaphoreType.DMA((count,)),
        ],
        compiler_params=PARAMS,
        cost_estimate=FREE,
    )(chip, *(pieces[k] for k in order))


def join_kernel(groups, *refs, order, edges):
    slots = len(order)
    pieces, outs = refs[:slots], refs[slots : slots + 1 + edges]
    held, sems, out_sems = refs[-3:]
    copies = [pltpu.make_async_copy(p, held.at[k], sems.at[k]) for k, p in zip(order, pieces)]
    for copy in copies:
        copy.start()
    for copy in copies:
        copy.wait()
    sends = [
        pltpu.make_async_copy(
            held.at[pl.ds(groups[e] * HB, HB)], outs[1 + e], out_sems.at[1 + e]
        )
        for e in range(edges)
    ]
    sends.append(pltpu.make_async_copy(held, outs[0], out_sems.at[0]))
    for copy in sends:
        copy.start()
    for copy in sends:
        copy.wait()


def join(groups, pieces, order):
    tokens, width = pieces[0].shape
    slots, edges = len(pieces), groups.shape[0]
    return pl.pallas_call(
        functools.partial(join_kernel, order=order, edges=edges),
        in_specs=[SMEM] + [ANY] * slots,
        out_specs=[HBM] * (1 + edges),
        out_shape=[half(slots, tokens, width)] + [half(HB, tokens, width)] * edges,
        scratch_shapes=[
            pltpu.VMEM((slots, tokens, width), jnp.bfloat16),
            pltpu.SemaphoreType.DMA((slots,)),
            pltpu.SemaphoreType.DMA((1 + edges,)),
        ],
        compiler_params=PARAMS,
        cost_estimate=FREE,
    )(groups, *(pieces[k] for k in order))


def attend_head(blocks, both, kv, low, hd):
    tokens = both.shape[0]
    scale = hd ** (-0.5)
    factor = scale * math.log2(math.e)
    trans = (((1,), (1,)), ((), ()))
    query = both[:, :hd]
    left = jnp.concatenate([jnp.zeros_like(query), query], axis=1)
    left = jnp.concatenate([left, both], axis=0)
    scores, tans = [], []
    for block in blocks:
        keys = kv[block, :, :, low : low + 2 * hd].reshape(BQ, 2 * hd)
        product = lax.dot_general(left, keys, trans, preferred_element_type=jnp.float32)
        scores.append(product[:tokens])
        tans.append(product[tokens:])
    top = functools.reduce(jnp.maximum, scores)
    top = jnp.max(top, axis=1, keepdims=True) * factor
    probs = [jnp.exp2(s * factor - top) for s in scores]
    weighted = [p * t for p, t in zip(probs, tans)]
    total = jnp.sum(functools.reduce(jnp.add, probs), axis=1, keepdims=True)
    mean = jnp.sum(functools.reduce(jnp.add, weighted), axis=1, keepdims=True)
    mixed = jnp.zeros((2 * tokens, 2 * hd), jnp.float32)
    for block, p, w in zip(blocks, probs, weighted):
        vals = kv[block, :, :, low + 2 * hd : low + 4 * hd].reshape(BQ, 2 * hd)
        right = jnp.concatenate([p.astype(jnp.bfloat16), w.astype(jnp.bfloat16)], axis=0)
        mixed += jnp.dot(right, vals, preferred_element_type=jnp.float32)
    inverse = 1.0 / total
    out = mixed[:tokens, :hd] * inverse
    tan = (mixed[:tokens, hd:] + scale * mixed[tokens:, :hd]) * inverse
    tan = tan - (scale * mean * inverse) * out
    return out.astype(jnp.bfloat16), tan.astype(jnp.bfloat16)


def attend_kernel(table, *refs, count, sources, hd, first):
    q_refs, refs = refs[:count], refs[count:]
    parts, refs = refs[: 2 * sources], refs[2 * sources :]
    outs = refs[-6 - count : -6]
    queries, kv, staged, q_sems, kv_sems, out_sems = refs[-6:]
    copies = []
    for i, ref in enumerate(q_refs):
        copies.append(pltpu.make_async_copy(ref, queries.at[i], q_sems.at[i]))
    for core in range(PAIR):
        row = 0
        for i in range(sources):
            ref = parts[core * sources + i]
            target = kv.at[pl.ds(row, ref.shape[0]), core]
            copies.append(
                pltpu.make_async_copy(ref, target, kv_sems.at[core * sources + i])
            )
            row += ref.shape[0]
    for copy in copies:
        copy.start()
    for copy in copies:
        copy.wait()
    sends = []
    for i in range(count):
        blocks = [table[first + i, w] for w in range(WK)]
        for h in range(PAIR):
            both = queries[i, :, 2 * h * hd : 2 * (h + 1) * hd]
            out, tan = attend_head(blocks, both, kv, 4 * h * hd, hd)
            staged[i, :, 2 * h * hd : (2 * h + 1) * hd] = out
            staged[i, :, (2 * h + 1) * hd : 2 * (h + 1) * hd] = tan
        sends.append(pltpu.make_async_copy(staged.at[i], outs[i], out_sems.at[i]))
        sends[-1].start()
    for copy in sends:
        copy.wait()


def attend(table, first, queries, mine, other, later):
    tokens, width = queries[0].shape
    hd, count, sources = width // (2 * PAIR), len(queries), len(mine)
    total = sum(a.shape[0] for a in mine)
    return pl.pallas_call(
        functools.partial(attend_kernel, count=count, sources=sources, hd=hd, first=first),
        in_specs=[SMEM] + [ANY] * (count + 2 * sources + len(later)),
        out_specs=[HBM] * count,
        out_shape=[half(tokens, width)] * count,
        scratch_shapes=[
            pltpu.VMEM((count, tokens, width), jnp.bfloat16),
            pltpu.VMEM((total, PAIR, tokens, 2 * width), jnp.bfloat16),
            pltpu.VMEM((count, tokens, width), jnp.bfloat16),
            pltpu.SemaphoreType.DMA((count,)),
            pltpu.SemaphoreType.DMA((2 * sources,)),
            pltpu.SemaphoreType.DMA((count,)),
        ],
        compiler_params=PARAMS,
        cost_estimate=FREE,
    )(table, *queries, *mine, *other, *later)


def send(pieces, devices):
    got = {}
    for k in range(devices // PAIR):
        pairs = [(i, i ^ (k * PAIR)) for i in range(devices)]
        got[k] = lax.ppermute(pieces[k], "heads", pairs) if k else pieces[k]
    return got


def per_device(query, keys, values, query_tan, keys_tan, values_tan, neighbors):
    devices, frames = lax.axis_size("heads"), lax.axis_size("frames")
    frame = lax.axis_index("frames")
    chip = lax.axis_index("heads") // PAIR
    blocks = neighbors.shape[0]
    middle = blocks // 2
    order = list(range(middle, blocks)) + list(range(middle))

    chip_ref = chip.reshape(1).astype(jnp.int32)
    got = send(pack(chip_ref, [keys_tan, keys, values, values_tan], devices), devices)
    q_got = send(pack(chip_ref, [query, query_tan], devices), devices)

    rounds = []
    for first in (0, 1):
        pairs = [(i, i + 1) for i in range(first, frames - 1, 2)]
        if pairs:
            rounds.append((first, pairs + [(j, i) for i, j in pairs]))
    outer = [
        jnp.where(frame % 2 == first, blocks // HB - 1, 0) ^ (chip // HB) for first, _ in rounds
    ]
    joined = join(jnp.stack(outer).astype(jnp.int32), got, order)
    mine = [joined[0]]
    for (_, pairs), edge in zip(rounds, joined[1:]):
        halo = lax.ppermute(edge, "frames", pairs)
        mine.append(hold(halo, [q_got[k] for k in order]))
    swap = [(i, i ^ 1) for i in range(devices)]
    other = [lax.ppermute(a, "heads", swap) for a in mine]

    local = neighbors - frame * blocks
    even = frame % 2 == 0
    before = blocks + jnp.where(even, HB, 0) + ((local + blocks) ^ chip) % HB
    after = blocks + jnp.where(even, 0, HB) + ((local - blocks) ^ chip) % HB
    table = jnp.where(local < 0, before, jnp.where(local >= blocks, after, local ^ chip))
    table = table[jnp.arange(blocks) ^ chip]

    far, near = range(middle, blocks), range(middle)
    outs, done = {}, []
    for part in (far, near):
        done = attend(table, part[0], [q_got[k] for k in part], mine, other, done)
        outs.update(zip(part, done))
    back = send(outs, devices)
    for k in near:
        back[k] = hold(back[k], [back[j] for j in far], 5)
    return unpack(chip_ref, back, 2, order)


def solution(mesh):
    own = P(("frames", "heads"), None)
    return jax.shard_map(
        per_device,
        mesh=mesh,
        in_specs=(own,) * 6 + (P("frames", None),),
        out_specs=(own, own),
        check_vma=False,
    )
```

```python
import functools
import math

import jax
import jax.numpy as jnp
from jax import lax
from jax.experimental import pallas as pl
from jax.experimental.pallas import tpu as pltpu
from jax.sharding import PartitionSpec as P

BQ = 256
WK = 4
HB = 4
HALO = HB * BQ
PARAMS = pltpu.CompilerParams(vmem_limit_bytes=32 * 1024 * 1024)
ANY = pl.BlockSpec(memory_space=pl.ANY)
HBM = pl.BlockSpec(memory_space=pltpu.HBM)
VMEM = pl.BlockSpec(memory_space=pltpu.VMEM)
SMEM = pl.BlockSpec(memory_space=pltpu.SMEM)


def pin(*arrays):
    return [pltpu.with_memory_space_constraint(a, pltpu.HBM) for a in arrays]


def moves(size):
    return pl.CostEstimate(flops=0, bytes_accessed=size, transcendentals=0)


def hold_kernel(*refs):
    del refs


def hold(array, others):
    return pl.pallas_call(
        hold_kernel,
        in_specs=[ANY] * (1 + len(others)),
        out_specs=ANY,
        out_shape=jax.ShapeDtypeStruct(array.shape, array.dtype),
        input_output_aliases={0: 0},
    )(array, *others)


def pack_kernel(*refs, count, devices):
    arrays, out, held, sems = refs[:count], refs[count], refs[-2], refs[-1]
    hd = held.shape[2] // devices
    copies = [pltpu.make_async_copy(a, held.at[i], sems.at[i]) for i, a in enumerate(arrays)]
    for copy in copies:
        copy.start()
    for a, copy in enumerate(copies):
        copy.wait()
        for h in range(devices):
            out[h, :, a * hd : (a + 1) * hd] = held[a, :, h * hd : (h + 1) * hd]


def to_heads(arrays, devices):
    tokens, columns = arrays[0].shape
    count, hd = len(arrays), columns // devices
    return pl.pallas_call(
        functools.partial(pack_kernel, count=count, devices=devices),
        in_specs=[HBM] * count,
        out_specs=VMEM,
        out_shape=jax.ShapeDtypeStruct((devices, tokens, count * hd), jnp.bfloat16),
        scratch_shapes=[
            pltpu.VMEM((count, tokens, columns), jnp.bfloat16),
            pltpu.SemaphoreType.DMA((count,)),
        ],
        compiler_params=PARAMS,
        cost_estimate=moves(4 * count * tokens * columns),
    )(*pin(*arrays))


def unpack_kernel(piece, *arrays):
    devices, tokens, width = piece.shape
    hd = width // len(arrays)
    for h in range(devices):
        for a, array in enumerate(arrays):
            array[:, h * hd : (h + 1) * hd] = piece[h, :, a * hd : (a + 1) * hd]


def from_heads(pieces, count):
    devices, tokens, width = pieces.shape
    columns = devices * width // count
    return pl.pallas_call(
        unpack_kernel,
        in_specs=[VMEM],
        out_specs=[VMEM] * count,
        out_shape=[jax.ShapeDtypeStruct((tokens, columns), jnp.bfloat16)] * count,
        compiler_params=PARAMS,
        cost_estimate=moves(4 * pieces.size),
    )(pieces)


def exchange(pieces):
    got = lax.all_to_all(pieces, "heads", split_axis=0, concat_axis=0, tiled=True)
    return got.reshape(-1, got.shape[2])


def attend_kernel(table, q_ref, *refs, sources, hd):
    parts, out_ref, kv, sems = refs[:sources], refs[sources], refs[-2], refs[-1]
    copies, row = [], 0
    for i, ref in enumerate(parts):
        rows = ref.shape[0]
        copies.append(pltpu.make_async_copy(ref, kv.at[pl.ds(row, rows)], sems.at[i]))
        row += rows
    for copy in copies:
        copy.start()
    for copy in copies:
        copy.wait()

    scale = hd ** (-0.5)
    factor = scale * math.log2(math.e)
    trans = (((1,), (1,)), ((), ()))
    for block in range(q_ref.shape[0] // BQ):
        both = q_ref[block * BQ : (block + 1) * BQ]
        query = both[:, :hd]
        starts = [pl.multiple_of(table[block * WK + w] * BQ, BQ) for w in range(WK)]
        scores, tans = [], []
        for start in starts:
            keys = kv[pl.ds(start, BQ), : 2 * hd]
            scores.append(
                lax.dot_general(query, keys[:, hd:], trans, preferred_element_type=jnp.float32)
            )
            tans.append(lax.dot_general(both, keys, trans, preferred_element_type=jnp.float32))
        top = functools.reduce(jnp.maximum, scores)
        top = jnp.max(top, axis=1, keepdims=True) * factor
        probs = [jnp.exp2(s * factor - top) for s in scores]
        weighted = [p * t for p, t in zip(probs, tans)]
        total = jnp.sum(functools.reduce(jnp.add, probs), axis=1, keepdims=True)
        mean = jnp.sum(functools.reduce(jnp.add, weighted), axis=1, keepdims=True)
        main, side = 0.0, 0.0
        for start, p, w in zip(starts, probs, weighted):
            vals = kv[pl.ds(start, BQ), 2 * hd :]
            main += jnp.dot(p.astype(jnp.bfloat16), vals, preferred_element_type=jnp.float32)
            side += jnp.dot(
                w.astype(jnp.bfloat16), vals[:, :hd], preferred_element_type=jnp.float32
            )
        inverse = 1.0 / total
        out = main[:, :hd] * inverse
        tan = (main[:, hd:] + scale * side) * inverse - (scale * mean * inverse) * out
        rows = slice(block * BQ, (block + 1) * BQ)
        out_ref[rows, :hd] = out.astype(jnp.bfloat16)
        out_ref[rows, hd:] = tan.astype(jnp.bfloat16)


def attend(table, q_pair, parts):
    rows, width = q_pair.shape
    hd = width // 2
    total = sum(a.shape[0] for a in parts)
    elements = rows * WK * BQ
    return pl.pallas_call(
        functools.partial(attend_kernel, sources=len(parts), hd=hd),
        in_specs=[SMEM, VMEM] + [ANY] * len(parts),
        out_specs=VMEM,
        out_shape=jax.ShapeDtypeStruct((rows, width), jnp.bfloat16),
        scratch_shapes=[
            pltpu.VMEM((total, 4 * hd), jnp.bfloat16),
            pltpu.SemaphoreType.DMA((len(parts),)),
        ],
        compiler_params=PARAMS,
        cost_estimate=pl.CostEstimate(
            flops=12 * elements * hd,
            bytes_accessed=2 * (total * 4 * hd + 2 * rows * width),
            transcendentals=elements,
        ),
    )(table, q_pair, *parts)


def slots(neighbors, frame, blocks):
    local = neighbors - frame * blocks
    even = frame % 2 == 0
    before = blocks + jnp.where(even, HB, 0) + local + HB
    after = blocks + jnp.where(even, 0, HB) + local - blocks
    return jnp.where(local < 0, before, jnp.where(local >= blocks, after, local)).reshape(-1)


def per_device(query, keys, values, query_tan, keys_tan, values_tan, neighbors):
    devices, frames = lax.axis_size("heads"), lax.axis_size("frames")
    frame = lax.axis_index("frames")
    tokens = query.shape[0]
    kv_sent = to_heads([keys_tan, keys, values, values_tan], devices)
    q_sent = to_heads([query, query_tan], devices)
    kv = hold(exchange(kv_sent), [q_sent])
    rows = kv.shape[0]

    edges, parts = [], [kv]
    for first in (0, 1):
        pairs = [(i, i + 1) for i in range(first, frames - 1, 2)]
        if not pairs:
            continue
        start = jnp.where(frame % 2 == first, rows - HALO, 0)
        edges.append(lax.dynamic_slice_in_dim(kv, start, HALO, axis=0))
        parts.append(lax.ppermute(edges[-1], "frames", pairs + [(j, i) for i, j in pairs]))

    q_pair = exchange(hold(q_sent, edges))
    table = slots(neighbors, frame, neighbors.shape[0])
    pair = attend(table, q_pair, parts).reshape(devices, tokens, -1)
    back = lax.all_to_all(pair, "heads", split_axis=0, concat_axis=0, tiled=True)
    return from_heads(back, 2)


def solution(mesh):
    own = P(("frames", "heads"), None)
    return jax.shard_map(
        per_device,
        mesh=mesh,
        in_specs=(own,) * 6 + (P("frames", None),),
        out_specs=(own, own),
        check_vma=False,
    )
```

```python
import functools
import math

import jax
import jax.numpy as jnp
from jax import lax
from jax.experimental import pallas as pl
from jax.experimental.pallas import tpu as pltpu
from jax.sharding import PartitionSpec as P

BQ = 256
WK = 4
HB = 4
HALO = HB * BQ
PARAMS = pltpu.CompilerParams(vmem_limit_bytes=32 * 1024 * 1024)
ANY = pl.BlockSpec(memory_space=pl.ANY)
HBM = pl.BlockSpec(memory_space=pltpu.HBM)
VMEM = pl.BlockSpec(memory_space=pltpu.VMEM)
SMEM = pl.BlockSpec(memory_space=pltpu.SMEM)


def pin(*arrays):
    return [pltpu.with_memory_space_constraint(a, pltpu.HBM) for a in arrays]


def moves(size):
    return pl.CostEstimate(flops=0, bytes_accessed=size, transcendentals=0)


def pack_kernel(*refs, count, chunks):
    arrays, out = refs[:count], refs[count]
    held, staged, sems, out_sems = refs[-4:]
    devices, columns = out.shape[0], held.shape[2]
    hd, heads, step = columns // devices, devices // chunks, columns // chunks
    copies = {}
    for c in range(chunks):
        lanes = pl.ds(c * step, step)
        for a, array in enumerate(arrays):
            copies[c, a] = pltpu.make_async_copy(
                array.at[:, lanes], held.at[a, :, lanes], sems.at[c, a]
            )
            copies[c, a].start()
    sends = []
    for c in range(chunks):
        for a in range(count):
            copies[c, a].wait()
        for h in range(c * heads, (c + 1) * heads):
            for a in range(count):
                staged[h, :, a * hd : (a + 1) * hd] = held[a, :, h * hd : (h + 1) * hd]
        part = pl.ds(c * heads, heads)
        sends.append(pltpu.make_async_copy(staged.at[part], out.at[part], out_sems.at[c]))
        sends[-1].start()
    for send in sends:
        send.wait()


def to_heads(arrays, devices, chunks=4):
    tokens, columns = arrays[0].shape
    count, hd = len(arrays), columns // devices
    shape = (devices, tokens, count * hd)
    return pl.pallas_call(
        functools.partial(pack_kernel, count=count, chunks=chunks),
        in_specs=[HBM] * count,
        out_specs=HBM,
        out_shape=pltpu.HBM(shape, jnp.bfloat16),
        scratch_shapes=[
            pltpu.VMEM((count, tokens, columns), jnp.bfloat16),
            pltpu.VMEM(shape, jnp.bfloat16),
            pltpu.SemaphoreType.DMA((chunks, count)),
            pltpu.SemaphoreType.DMA((chunks,)),
        ],
        compiler_params=PARAMS,
        cost_estimate=moves(4 * count * tokens * columns),
    )(*pin(*arrays))


def unpack_kernel(piece, *arrays):
    devices, tokens, width = piece.shape
    hd = width // len(arrays)
    for h in range(devices):
        for a, array in enumerate(arrays):
            array[:, h * hd : (h + 1) * hd] = piece[h, :, a * hd : (a + 1) * hd]


def from_heads(pieces, count):
    devices, tokens, width = pieces.shape
    columns = devices * width // count
    return pl.pallas_call(
        unpack_kernel,
        in_specs=[VMEM],
        out_specs=[VMEM] * count,
        out_shape=[jax.ShapeDtypeStruct((tokens, columns), jnp.bfloat16)] * count,
        compiler_params=PARAMS,
        cost_estimate=moves(4 * pieces.size),
    )(pieces)


def exchange(pieces):
    got = lax.all_to_all(pieces, "heads", split_axis=0, concat_axis=0, tiled=True)
    return got.reshape(-1, got.shape[2])


def edge_kernel(start, kv, q_sent, out, sem):
    del q_sent
    first = pl.multiple_of(start[0] * BQ, BQ)
    copy = pltpu.make_async_copy(kv.at[pl.ds(first, HALO)], out, sem)
    copy.start()
    copy.wait()


def edge(start, kv, q_sent):
    shape = (HALO, kv.shape[1])
    return pl.pallas_call(
        edge_kernel,
        in_specs=[SMEM, ANY, ANY],
        out_specs=HBM,
        out_shape=pltpu.HBM(shape, jnp.bfloat16),
        scratch_shapes=[pltpu.SemaphoreType.DMA(())],
        cost_estimate=moves(4 * HALO * kv.shape[1]),
    )(start, kv, q_sent)


def join_kernel(*refs, sources):
    parts, out, sems = refs[:sources], refs[sources], refs[-1]
    copies, row = [], 0
    for i, ref in enumerate(parts):
        rows = ref.shape[0]
        copies.append(pltpu.make_async_copy(ref, out.at[pl.ds(row, rows)], sems.at[i]))
        row += rows
    for copy in copies:
        copy.start()
    for copy in copies:
        copy.wait()


def join(parts):
    total, width = sum(a.shape[0] for a in parts), parts[0].shape[1]
    return pl.pallas_call(
        functools.partial(join_kernel, sources=len(parts)),
        in_specs=[ANY] * len(parts),
        out_specs=VMEM,
        out_shape=jax.ShapeDtypeStruct((total, width), jnp.bfloat16),
        scratch_shapes=[pltpu.SemaphoreType.DMA((len(parts),))],
        compiler_params=PARAMS,
        cost_estimate=moves(200_000_000),
    )(*parts)


def attend_kernel(table, q_ref, kv, out_ref, *, hd):
    scale = hd ** (-0.5)
    factor = scale * math.log2(math.e)
    trans = (((1,), (1,)), ((), ()))
    for block in range(q_ref.shape[0] // BQ):
        both = q_ref[block * BQ : (block + 1) * BQ]
        query = both[:, :hd]
        starts = [pl.multiple_of(table[block * WK + w] * BQ, BQ) for w in range(WK)]
        scores, tans = [], []
        for start in starts:
            keys = kv[pl.ds(start, BQ), : 2 * hd]
            scores.append(
                lax.dot_general(query, keys[:, hd:], trans, preferred_element_type=jnp.float32)
            )
            tans.append(lax.dot_general(both, keys, trans, preferred_element_type=jnp.float32))
        top = functools.reduce(jnp.maximum, scores)
        top = jnp.max(top, axis=1, keepdims=True) * factor
        probs = [jnp.exp2(s * factor - top) for s in scores]
        weighted = [p * t for p, t in zip(probs, tans)]
        total = jnp.sum(functools.reduce(jnp.add, probs), axis=1, keepdims=True)
        mean = jnp.sum(functools.reduce(jnp.add, weighted), axis=1, keepdims=True)
        main, side = 0.0, 0.0
        for start, p, w in zip(starts, probs, weighted):
            vals = kv[pl.ds(start, BQ), 2 * hd :]
            main += jnp.dot(p.astype(jnp.bfloat16), vals, preferred_element_type=jnp.float32)
            side += jnp.dot(
                w.astype(jnp.bfloat16), vals[:, :hd], preferred_element_type=jnp.float32
            )
        inverse = 1.0 / total
        out = main[:, :hd] * inverse
        tan = (main[:, hd:] + scale * side) * inverse - (scale * mean * inverse) * out
        rows = slice(block * BQ, (block + 1) * BQ)
        out_ref[rows, :hd] = out.astype(jnp.bfloat16)
        out_ref[rows, hd:] = tan.astype(jnp.bfloat16)


def attend(table, q_pair, kv):
    rows, width = q_pair.shape
    hd = width // 2
    elements = rows * WK * BQ
    return pl.pallas_call(
        functools.partial(attend_kernel, hd=hd),
        in_specs=[SMEM, VMEM, VMEM],
        out_specs=VMEM,
        out_shape=jax.ShapeDtypeStruct((rows, width), jnp.bfloat16),
        compiler_params=PARAMS,
        cost_estimate=pl.CostEstimate(
            flops=12 * elements * hd,
            bytes_accessed=2 * (kv.size + 2 * rows * width),
            transcendentals=elements,
        ),
    )(table, q_pair, kv)


def slots(neighbors, frame, blocks):
    local = neighbors - frame * blocks
    even = frame % 2 == 0
    before = blocks + jnp.where(even, HB, 0) + local + HB
    after = blocks + jnp.where(even, 0, HB) + local - blocks
    return jnp.where(local < 0, before, jnp.where(local >= blocks, after, local)).reshape(-1)


def per_device(query, keys, values, query_tan, keys_tan, values_tan, neighbors):
    devices, frames = lax.axis_size("heads"), lax.axis_size("frames")
    frame = lax.axis_index("frames")
    tokens = query.shape[0]
    kv = exchange(to_heads([keys_tan, keys, values, values_tan], devices))
    q_sent = to_heads([query, query_tan], devices)
    blocks = neighbors.shape[0]

    parts = [kv]
    for first in (0, 1):
        pairs = [(i, i + 1) for i in range(first, frames - 1, 2)]
        if pairs:
            start = jnp.where(frame % 2 == first, blocks - HB, 0).reshape(1).astype(jnp.int32)
            outer = edge(start, kv, q_sent)
            parts.append(lax.ppermute(outer, "frames", pairs + [(j, i) for i, j in pairs]))
    kv = join(parts)

    q_pair = exchange(q_sent)
    table = slots(neighbors, frame, blocks)
    pair = attend(table, q_pair, kv).reshape(devices, tokens, -1)
    back = lax.all_to_all(pair, "heads", split_axis=0, concat_axis=0, tiled=True)
    return from_heads(back, 2)


def solution(mesh):
    own = P(("frames", "heads"), None)
    return jax.shard_map(
        per_device,
        mesh=mesh,
        in_specs=(own,) * 6 + (P("frames", None),),
        out_specs=(own, own),
        check_vma=False,
    )
```

```python
import functools
import math

import jax
import jax.numpy as jnp
from jax import lax
from jax.experimental import pallas as pl
from jax.experimental.pallas import tpu as pltpu
from jax.sharding import PartitionSpec as P

BQ = 256
WK = 4
HB = 4
HALO = HB * BQ
PARAMS = pltpu.CompilerParams(vmem_limit_bytes=32 * 1024 * 1024)
ANY = pl.BlockSpec(memory_space=pl.ANY)
HBM = pl.BlockSpec(memory_space=pltpu.HBM)
VMEM = pl.BlockSpec(memory_space=pltpu.VMEM)
SMEM = pl.BlockSpec(memory_space=pltpu.SMEM)


def pin(*arrays):
    return [pltpu.with_memory_space_constraint(a, pltpu.HBM) for a in arrays]


def moves(size):
    return pl.CostEstimate(flops=0, bytes_accessed=size, transcendentals=0)


def pack_kernel(*refs, count, chunks):
    arrays, out = refs[:count], refs[count]
    held, staged, sems, out_sems = refs[-4:]
    devices, columns = out.shape[0], held.shape[2]
    hd, heads, step = columns // devices, devices // chunks, columns // chunks
    copies = {}
    for c in range(chunks):
        lanes = pl.ds(c * step, step)
        for a, array in enumerate(arrays):
            copies[c, a] = pltpu.make_async_copy(
                array.at[:, lanes], held.at[a, :, lanes], sems.at[c, a]
            )
            copies[c, a].start()
    sends = []
    for c in range(chunks):
        for a in range(count):
            copies[c, a].wait()
        for h in range(c * heads, (c + 1) * heads):
            for a in range(count):
                staged[h, :, a * hd : (a + 1) * hd] = held[a, :, h * hd : (h + 1) * hd]
        part = pl.ds(c * heads, heads)
        sends.append(pltpu.make_async_copy(staged.at[part], out.at[part], out_sems.at[c]))
        sends[-1].start()
    for send in sends:
        send.wait()


def to_heads(arrays, devices, chunks=4):
    tokens, columns = arrays[0].shape
    count, hd = len(arrays), columns // devices
    shape = (devices, tokens, count * hd)
    return pl.pallas_call(
        functools.partial(pack_kernel, count=count, chunks=chunks),
        in_specs=[HBM] * count,
        out_specs=HBM,
        out_shape=pltpu.HBM(shape, jnp.bfloat16),
        scratch_shapes=[
            pltpu.VMEM((count, tokens, columns), jnp.bfloat16),
            pltpu.VMEM(shape, jnp.bfloat16),
            pltpu.SemaphoreType.DMA((chunks, count)),
            pltpu.SemaphoreType.DMA((chunks,)),
        ],
        compiler_params=PARAMS,
        cost_estimate=moves(4 * count * tokens * columns),
    )(*pin(*arrays))


def unpack_kernel(piece, *arrays):
    devices, tokens, width = piece.shape
    hd = width // len(arrays)
    for h in range(devices):
        for a, array in enumerate(arrays):
            array[:, h * hd : (h + 1) * hd] = piece[h, :, a * hd : (a + 1) * hd]


def from_heads(pieces, count):
    devices, tokens, width = pieces.shape
    columns = devices * width // count
    return pl.pallas_call(
        unpack_kernel,
        in_specs=[VMEM],
        out_specs=[VMEM] * count,
        out_shape=[jax.ShapeDtypeStruct((tokens, columns), jnp.bfloat16)] * count,
        compiler_params=PARAMS,
        cost_estimate=moves(4 * pieces.size),
    )(pieces)


def exchange(pieces):
    got = lax.all_to_all(pieces, "heads", split_axis=0, concat_axis=0, tiled=True)
    return got.reshape(-1, got.shape[2])


def attend_kernel(table, q_ref, *refs, sources, hd):
    parts, out_ref, kv, sems = refs[:sources], refs[sources], refs[-2], refs[-1]
    copies, row = [], 0
    for i, ref in enumerate(parts):
        rows = ref.shape[0]
        copies.append(pltpu.make_async_copy(ref, kv.at[pl.ds(row, rows)], sems.at[i]))
        row += rows
    for copy in copies:
        copy.start()
    for copy in copies:
        copy.wait()

    scale = hd ** (-0.5)
    factor = scale * math.log2(math.e)
    trans = (((1,), (1,)), ((), ()))

    def products(block):
        both = q_ref[block * BQ : (block + 1) * BQ]
        query = both[:, :hd]
        starts = [pl.multiple_of(table[block * WK + w] * BQ, BQ) for w in range(WK)]
        scores, tans = [], []
        for start in starts:
            keys = kv[pl.ds(start, BQ), : 2 * hd]
            scores.append(
                lax.dot_general(query, keys[:, hd:], trans, preferred_element_type=jnp.float32)
            )
            tans.append(lax.dot_general(both, keys, trans, preferred_element_type=jnp.float32))
        return starts, scores, tans

    def finish(block, starts, scores, tans):
        top = functools.reduce(jnp.maximum, scores)
        top = jnp.max(top, axis=1, keepdims=True) * factor
        probs = [jnp.exp2(s * factor - top) for s in scores]
        weighted = [p * t for p, t in zip(probs, tans)]
        total = jnp.sum(functools.reduce(jnp.add, probs), axis=1, keepdims=True)
        mean = jnp.sum(functools.reduce(jnp.add, weighted), axis=1, keepdims=True)
        main, side = 0.0, 0.0
        for start, p, w in zip(starts, probs, weighted):
            vals = kv[pl.ds(start, BQ), 2 * hd :]
            main += jnp.dot(p.astype(jnp.bfloat16), vals, preferred_element_type=jnp.float32)
            side += jnp.dot(
                w.astype(jnp.bfloat16), vals[:, :hd], preferred_element_type=jnp.float32
            )
        inverse = 1.0 / total
        out = main[:, :hd] * inverse
        tan = (main[:, hd:] + scale * side) * inverse - (scale * mean * inverse) * out
        rows = slice(block * BQ, (block + 1) * BQ)
        out_ref[rows, :hd] = out.astype(jnp.bfloat16)
        out_ref[rows, hd:] = tan.astype(jnp.bfloat16)

    blocks = q_ref.shape[0] // BQ
    ahead = products(0)
    for block in range(blocks):
        current = ahead
        if block + 1 < blocks:
            ahead = products(block + 1)
        finish(block, *current)


def attend(table, q_pair, parts):
    rows, width = q_pair.shape
    hd = width // 2
    total = sum(a.shape[0] for a in parts)
    elements = rows * WK * BQ
    return pl.pallas_call(
        functools.partial(attend_kernel, sources=len(parts), hd=hd),
        in_specs=[SMEM, VMEM] + [ANY] * len(parts),
        out_specs=VMEM,
        out_shape=jax.ShapeDtypeStruct((rows, width), jnp.bfloat16),
        scratch_shapes=[
            pltpu.VMEM((total, 4 * hd), jnp.bfloat16),
            pltpu.SemaphoreType.DMA((len(parts),)),
        ],
        compiler_params=PARAMS,
        cost_estimate=pl.CostEstimate(
            flops=12 * elements * hd,
            bytes_accessed=2 * (total * 4 * hd + 2 * rows * width),
            transcendentals=elements,
        ),
    )(table, q_pair, *parts)


def slots(neighbors, frame, blocks):
    local = neighbors - frame * blocks
    even = frame % 2 == 0
    before = blocks + jnp.where(even, HB, 0) + local + HB
    after = blocks + jnp.where(even, 0, HB) + local - blocks
    return jnp.where(local < 0, before, jnp.where(local >= blocks, after, local)).reshape(-1)


def per_device(query, keys, values, query_tan, keys_tan, values_tan, neighbors):
    devices, frames = lax.axis_size("heads"), lax.axis_size("frames")
    frame = lax.axis_index("frames")
    tokens = query.shape[0]
    kv = exchange(to_heads([keys_tan, keys, values, values_tan], devices))
    rows = kv.shape[0]

    parts = [kv]
    for first in (0, 1):
        pairs = [(i, i + 1) for i in range(first, frames - 1, 2)]
        if pairs:
            start = jnp.where(frame % 2 == first, rows - HALO, 0)
            edge = lax.dynamic_slice_in_dim(kv, start, HALO, axis=0)
            parts.append(lax.ppermute(edge, "frames", pairs + [(j, i) for i, j in pairs]))

    q_pair = exchange(to_heads([query, query_tan], devices))
    table = slots(neighbors, frame, neighbors.shape[0])
    pair = attend(table, q_pair, parts).reshape(devices, tokens, -1)
    back = lax.all_to_all(pair, "heads", split_axis=0, concat_axis=0, tiled=True)
    return from_heads(back, 2)


def solution(mesh):
    own = P(("frames", "heads"), None)
    return jax.shard_map(
        per_device,
        mesh=mesh,
        in_specs=(own,) * 6 + (P("frames", None),),
        out_specs=(own, own),
        check_vma=False,
    )
```

```python
import functools
import math

import jax
import jax.numpy as jnp
from jax import lax
from jax.experimental import pallas as pl
from jax.experimental.pallas import tpu as pltpu
from jax.sharding import PartitionSpec as P

BQ = 256
WK = 4
HB = 4
HALO = HB * BQ
PARAMS = pltpu.CompilerParams(vmem_limit_bytes=32 * 1024 * 1024)
ANY = pl.BlockSpec(memory_space=pl.ANY)
HBM = pl.BlockSpec(memory_space=pltpu.HBM)
VMEM = pl.BlockSpec(memory_space=pltpu.VMEM)
SMEM = pl.BlockSpec(memory_space=pltpu.SMEM)


def pin(*arrays):
    return [pltpu.with_memory_space_constraint(a, pltpu.HBM) for a in arrays]


def moves(size):
    return pl.CostEstimate(flops=0, bytes_accessed=size, transcendentals=0)


def pack_kernel(*refs, count, chunks):
    arrays, out = refs[:count], refs[count]
    held, staged, sems, out_sems = refs[-4:]
    devices, columns = out.shape[0], held.shape[2]
    hd, heads, step = columns // devices, devices // chunks, columns // chunks
    copies = {}
    for c in range(chunks):
        lanes = pl.ds(c * step, step)
        for a, array in enumerate(arrays):
            copies[c, a] = pltpu.make_async_copy(
                array.at[:, lanes], held.at[a, :, lanes], sems.at[c, a]
            )
            copies[c, a].start()
    sends = []
    for c in range(chunks):
        for a in range(count):
            copies[c, a].wait()
        for h in range(c * heads, (c + 1) * heads):
            for a in range(count):
                staged[h, :, a * hd : (a + 1) * hd] = held[a, :, h * hd : (h + 1) * hd]
        part = pl.ds(c * heads, heads)
        sends.append(pltpu.make_async_copy(staged.at[part], out.at[part], out_sems.at[c]))
        sends[-1].start()
    for send in sends:
        send.wait()


def to_heads(arrays, devices, chunks=4):
    tokens, columns = arrays[0].shape
    count, hd = len(arrays), columns // devices
    shape = (devices, tokens, count * hd)
    return pl.pallas_call(
        functools.partial(pack_kernel, count=count, chunks=chunks),
        in_specs=[HBM] * count,
        out_specs=HBM,
        out_shape=pltpu.HBM(shape, jnp.bfloat16),
        scratch_shapes=[
            pltpu.VMEM((count, tokens, columns), jnp.bfloat16),
            pltpu.VMEM(shape, jnp.bfloat16),
            pltpu.SemaphoreType.DMA((chunks, count)),
            pltpu.SemaphoreType.DMA((chunks,)),
        ],
        compiler_params=PARAMS,
        cost_estimate=moves(4 * count * tokens * columns),
    )(*pin(*arrays))


def unpack_kernel(me, near, *refs):
    half, _, width = near.shape
    pieces, arrays = refs[:half], refs[half:]
    hd = width // len(arrays)
    heads = [((me[0] // half) * half + i, near.at[i]) for i in range(half)]
    heads += [(me[0] ^ (half + i), pieces[i]) for i in range(half)]
    for head, piece in heads:
        columns = pl.ds(pl.multiple_of(head * hd, hd), hd)
        for a, array in enumerate(arrays):
            array[:, columns] = piece[:, a * hd : (a + 1) * hd]


def from_heads(me, near, far, count):
    half, tokens, width = near.shape
    columns = 2 * half * width // count
    return pl.pallas_call(
        unpack_kernel,
        in_specs=[SMEM] + [VMEM] * (1 + half),
        out_specs=[VMEM] * count,
        out_shape=[jax.ShapeDtypeStruct((tokens, columns), jnp.bfloat16)] * count,
        compiler_params=PARAMS,
        cost_estimate=moves(8 * near.size),
    )(me, near, *far)


def exchange(pieces):
    got = lax.all_to_all(pieces, "heads", split_axis=0, concat_axis=0, tiled=True)
    return got.reshape(-1, got.shape[2])


def attend_kernel(me, table, q_ref, *refs, sources, later, tokens, far, hd):
    parts, outs = refs[:sources], refs[sources + later : -3]
    kv, held, sems = refs[-3:]
    count, per = q_ref.shape[0] // BQ // 2, BQ // tokens
    chip, core = me[0] // per, me[0] % per
    if far:
        blocks = [chip ^ (count + i) for i in range(count)]
    else:
        blocks = [(chip // count) * count + i for i in range(count)]
    copies, row = [], 0
    for i, ref in enumerate(parts):
        rows = ref.shape[0]
        copies.append(pltpu.make_async_copy(ref, kv.at[pl.ds(row, rows)], sems.at[i]))
        row += rows
    for copy in copies:
        copy.start()
    for copy in copies:
        copy.wait()

    scale = hd ** (-0.5)
    factor = scale * math.log2(math.e)
    trans = (((1,), (1,)), ((), ()))

    def products(block):
        both = q_ref[pl.ds(pl.multiple_of(block * BQ, BQ), BQ)]
        query = both[:, :hd]
        starts = [pl.multiple_of(table[block * WK + w] * BQ, BQ) for w in range(WK)]
        scores, tans = [], []
        for start in starts:
            keys = kv[pl.ds(start, BQ), : 2 * hd]
            scores.append(
                lax.dot_general(query, keys[:, hd:], trans, preferred_element_type=jnp.float32)
            )
            tans.append(lax.dot_general(both, keys, trans, preferred_element_type=jnp.float32))
        return starts, scores, tans

    def finish(i, starts, scores, tans):
        top = functools.reduce(jnp.maximum, scores)
        top = jnp.max(top, axis=1, keepdims=True) * factor
        probs = [jnp.exp2(s * factor - top) for s in scores]
        weighted = [p * t for p, t in zip(probs, tans)]
        total = jnp.sum(functools.reduce(jnp.add, probs), axis=1, keepdims=True)
        mean = jnp.sum(functools.reduce(jnp.add, weighted), axis=1, keepdims=True)
        main, side = 0.0, 0.0
        for start, p, w in zip(starts, probs, weighted):
            vals = kv[pl.ds(start, BQ), 2 * hd :]
            main += jnp.dot(p.astype(jnp.bfloat16), vals, preferred_element_type=jnp.float32)
            side += jnp.dot(
                w.astype(jnp.bfloat16), vals[:, :hd], preferred_element_type=jnp.float32
            )
        inverse = 1.0 / total
        out = main[:, :hd] * inverse
        tan = (main[:, hd:] + scale * side) * inverse - (scale * mean * inverse) * out
        rows = held.at[i] if far else outs[0].at[i * BQ : (i + 1) * BQ]
        rows[:, :hd] = out.astype(jnp.bfloat16)
        rows[:, hd:] = tan.astype(jnp.bfloat16)
        if far:
            for p in range(per):
                start = pl.multiple_of((core ^ p) * tokens, tokens)
                outs[i * per + p][...] = held[i, pl.ds(start, tokens)]

    ahead = products(blocks[0])
    for i in range(count):
        current = ahead
        if i + 1 < count:
            ahead = products(blocks[i + 1])
        finish(i, *current)


def attend(me, table, q_pair, parts, later, tokens, far):
    rows, width = q_pair.shape
    hd, half = width // 2, rows // 2
    total = sum(a.shape[0] for a in parts)
    elements = half * WK * BQ
    sizes = [tokens] * (half // tokens) if far else [half]
    return pl.pallas_call(
        functools.partial(
            attend_kernel, sources=len(parts), later=len(later), tokens=tokens, far=far, hd=hd
        ),
        in_specs=[SMEM, SMEM, VMEM] + [ANY] * (len(parts) + len(later)),
        out_specs=[VMEM] * len(sizes),
        out_shape=[jax.ShapeDtypeStruct((size, width), jnp.bfloat16) for size in sizes],
        scratch_shapes=[
            pltpu.VMEM((total, 4 * hd), jnp.bfloat16),
            pltpu.VMEM((half // BQ, BQ, width), jnp.bfloat16),
            pltpu.SemaphoreType.DMA((len(parts),)),
        ],
        compiler_params=PARAMS,
        cost_estimate=pl.CostEstimate(
            flops=12 * elements * hd,
            bytes_accessed=2 * (total * 4 * hd + 2 * rows * width),
            transcendentals=elements,
        ),
    )(me, table, q_pair, *parts, *later)


def slots(neighbors, frame, blocks):
    local = neighbors - frame * blocks
    even = frame % 2 == 0
    before = blocks + jnp.where(even, HB, 0) + local + HB
    after = blocks + jnp.where(even, 0, HB) + local - blocks
    return jnp.where(local < 0, before, jnp.where(local >= blocks, after, local)).reshape(-1)


def per_device(query, keys, values, query_tan, keys_tan, values_tan, neighbors):
    devices, frames = lax.axis_size("heads"), lax.axis_size("frames")
    frame = lax.axis_index("frames")
    tokens = query.shape[0]
    kv = exchange(to_heads([keys_tan, keys, values, values_tan], devices))
    rows = kv.shape[0]

    parts = [kv]
    for first in (0, 1):
        pairs = [(i, i + 1) for i in range(first, frames - 1, 2)]
        if pairs:
            start = jnp.where(frame % 2 == first, rows - HALO, 0)
            edge = lax.dynamic_slice_in_dim(kv, start, HALO, axis=0)
            parts.append(lax.ppermute(edge, "frames", pairs + [(j, i) for i, j in pairs]))

    q_pair = exchange(to_heads([query, query_tan], devices))
    table = slots(neighbors, frame, neighbors.shape[0])
    me = lax.axis_index("heads").reshape(1).astype(jnp.int32)
    half = devices // 2
    pieces = attend(me, table, q_pair, parts, [], tokens, True)
    far = []
    for i, piece in enumerate(pieces):
        far.append(lax.ppermute(piece, "heads", [(d, d ^ (half + i)) for d in range(devices)]))
    (near,) = attend(me, table, q_pair, parts, far[:2], tokens, False)
    near = lax.all_to_all(
        near.reshape(half, tokens, -1),
        "heads",
        split_axis=0,
        concat_axis=0,
        axis_index_groups=[list(range(half)), list(range(half, devices))],
        tiled=True,
    )
    return from_heads(me, near, far, 2)


def solution(mesh):
    own = P(("frames", "heads"), None)
    return jax.shard_map(
        per_device,
        mesh=mesh,
        in_specs=(own,) * 6 + (P("frames", None),),
        out_specs=(own, own),
        check_vma=False,
    )
```

```python
import functools
import math

import jax
import jax.numpy as jnp
from jax import lax
from jax.experimental import pallas as pl
from jax.experimental.pallas import tpu as pltpu
from jax.sharding import PartitionSpec as P

BQ = 256
WK = 4
HB = 4
HALO = HB * BQ
PARAMS = pltpu.CompilerParams(vmem_limit_bytes=32 * 1024 * 1024)
ANY = pl.BlockSpec(memory_space=pl.ANY)
HBM = pl.BlockSpec(memory_space=pltpu.HBM)
VMEM = pl.BlockSpec(memory_space=pltpu.VMEM)
SMEM = pl.BlockSpec(memory_space=pltpu.SMEM)


def pin(*arrays):
    return [pltpu.with_memory_space_constraint(a, pltpu.HBM) for a in arrays]


def moves(size):
    return pl.CostEstimate(flops=0, bytes_accessed=size, transcendentals=0)


def pack_kernel(*refs, count, chunks):
    arrays, out = refs[:count], refs[count]
    held, staged, sems, out_sems = refs[-4:]
    devices, columns = out.shape[0], held.shape[2]
    hd, heads, step = columns // devices, devices // chunks, columns // chunks
    copies = {}
    for c in range(chunks):
        lanes = pl.ds(c * step, step)
        for a, array in enumerate(arrays):
            copies[c, a] = pltpu.make_async_copy(
                array.at[:, lanes], held.at[a, :, lanes], sems.at[c, a]
            )
            copies[c, a].start()
    sends = []
    for c in range(chunks):
        for a in range(count):
            copies[c, a].wait()
        for h in range(c * heads, (c + 1) * heads):
            for a in range(count):
                staged[h, :, a * hd : (a + 1) * hd] = held[a, :, h * hd : (h + 1) * hd]
        part = pl.ds(c * heads, heads)
        sends.append(pltpu.make_async_copy(staged.at[part], out.at[part], out_sems.at[c]))
        sends[-1].start()
    for send in sends:
        send.wait()


def to_heads(arrays, devices, chunks=4):
    tokens, columns = arrays[0].shape
    count, hd = len(arrays), columns // devices
    shape = (devices, tokens, count * hd)
    return pl.pallas_call(
        functools.partial(pack_kernel, count=count, chunks=chunks),
        in_specs=[HBM] * count,
        out_specs=HBM,
        out_shape=pltpu.HBM(shape, jnp.bfloat16),
        scratch_shapes=[
            pltpu.VMEM((count, tokens, columns), jnp.bfloat16),
            pltpu.VMEM(shape, jnp.bfloat16),
            pltpu.SemaphoreType.DMA((chunks, count)),
            pltpu.SemaphoreType.DMA((chunks,)),
        ],
        compiler_params=PARAMS,
        cost_estimate=moves(4 * count * tokens * columns),
    )(*pin(*arrays))


def unpack_kernel(me, *refs, order):
    pieces, arrays = refs[: len(order)], refs[len(order) :]
    hd = pieces[0].shape[1] // len(arrays)
    for k, piece in zip(order, pieces):
        columns = pl.ds(pl.multiple_of((me[0] ^ k) * hd, hd), hd)
        for a, array in enumerate(arrays):
            array[:, columns] = piece[:, a * hd : (a + 1) * hd]


def from_heads(me, pieces, count):
    tokens, width = pieces[0].shape
    columns = len(pieces) * width // count
    return pl.pallas_call(
        functools.partial(unpack_kernel, order=list(pieces)),
        in_specs=[SMEM] + [VMEM] * len(pieces),
        out_specs=[VMEM] * count,
        out_shape=[jax.ShapeDtypeStruct((tokens, columns), jnp.bfloat16)] * count,
        compiler_params=PARAMS,
        cost_estimate=moves(4 * len(pieces) * tokens * width),
    )(me, *pieces.values())


def exchange(pieces):
    got = lax.all_to_all(pieces, "heads", split_axis=0, concat_axis=0, tiled=True)
    return got.reshape(-1, got.shape[2])


def attend_kernel(me, table, q_ref, *refs, sources, later, tokens, first, hd):
    parts, outs = refs[:sources], refs[sources + later : -3]
    kv, held, sems = refs[-3:]
    count, per = held.shape[0], BQ // tokens
    chip, core = me[0] // per, me[0] % per
    blocks = [chip ^ (first + i) for i in range(count)]
    copies, row = [], 0
    for i, ref in enumerate(parts):
        rows = ref.shape[0]
        copies.append(pltpu.make_async_copy(ref, kv.at[pl.ds(row, rows)], sems.at[i]))
        row += rows
    for copy in copies:
        copy.start()
    for copy in copies:
        copy.wait()

    scale = hd ** (-0.5)
    factor = scale * math.log2(math.e)
    trans = (((1,), (1,)), ((), ()))

    def products(block):
        both = q_ref[pl.ds(pl.multiple_of(block * BQ, BQ), BQ)]
        query = both[:, :hd]
        starts = [pl.multiple_of(table[block * WK + w] * BQ, BQ) for w in range(WK)]
        scores, tans = [], []
        for start in starts:
            keys = kv[pl.ds(start, BQ), : 2 * hd]
            scores.append(
                lax.dot_general(query, keys[:, hd:], trans, preferred_element_type=jnp.float32)
            )
            tans.append(lax.dot_general(both, keys, trans, preferred_element_type=jnp.float32))
        return starts, scores, tans

    def finish(i, starts, scores, tans):
        top = functools.reduce(jnp.maximum, scores)
        top = jnp.max(top, axis=1, keepdims=True) * factor
        probs = [jnp.exp2(s * factor - top) for s in scores]
        weighted = [p * t for p, t in zip(probs, tans)]
        total = jnp.sum(functools.reduce(jnp.add, probs), axis=1, keepdims=True)
        mean = jnp.sum(functools.reduce(jnp.add, weighted), axis=1, keepdims=True)
        main, side = 0.0, 0.0
        for start, p, w in zip(starts, probs, weighted):
            vals = kv[pl.ds(start, BQ), 2 * hd :]
            main += jnp.dot(p.astype(jnp.bfloat16), vals, preferred_element_type=jnp.float32)
            side += jnp.dot(
                w.astype(jnp.bfloat16), vals[:, :hd], preferred_element_type=jnp.float32
            )
        inverse = 1.0 / total
        out = main[:, :hd] * inverse
        tan = (main[:, hd:] + scale * side) * inverse - (scale * mean * inverse) * out
        held[i, :, :hd] = out.astype(jnp.bfloat16)
        held[i, :, hd:] = tan.astype(jnp.bfloat16)
        for p in range(per):
            start = pl.multiple_of((core ^ p) * tokens, tokens)
            outs[i * per + p][...] = held[i, pl.ds(start, tokens)]

    ahead = products(blocks[0])
    for i in range(count):
        current = ahead
        if i + 1 < count:
            ahead = products(blocks[i + 1])
        finish(i, *current)


def attend(me, table, q_pair, parts, later, tokens, first, count):
    rows, width = q_pair.shape
    hd = width // 2
    total = sum(a.shape[0] for a in parts)
    elements = count * BQ * WK * BQ
    pieces = count * BQ // tokens
    return pl.pallas_call(
        functools.partial(
            attend_kernel, sources=len(parts), later=len(later), tokens=tokens, first=first, hd=hd
        ),
        in_specs=[SMEM, SMEM, VMEM] + [ANY] * (len(parts) + len(later)),
        out_specs=[VMEM] * pieces,
        out_shape=[jax.ShapeDtypeStruct((tokens, width), jnp.bfloat16)] * pieces,
        scratch_shapes=[
            pltpu.VMEM((total, 4 * hd), jnp.bfloat16),
            pltpu.VMEM((count, BQ, width), jnp.bfloat16),
            pltpu.SemaphoreType.DMA((len(parts),)),
        ],
        compiler_params=PARAMS,
        cost_estimate=pl.CostEstimate(
            flops=12 * elements * hd,
            bytes_accessed=2 * (total * 4 * hd + 2 * rows * width),
            transcendentals=elements,
        ),
    )(me, table, q_pair, *parts, *later)


def slots(neighbors, frame, blocks):
    local = neighbors - frame * blocks
    even = frame % 2 == 0
    before = blocks + jnp.where(even, HB, 0) + local + HB
    after = blocks + jnp.where(even, 0, HB) + local - blocks
    return jnp.where(local < 0, before, jnp.where(local >= blocks, after, local)).reshape(-1)


def per_device(query, keys, values, query_tan, keys_tan, values_tan, neighbors):
    devices, frames = lax.axis_size("heads"), lax.axis_size("frames")
    frame = lax.axis_index("frames")
    tokens = query.shape[0]
    kv = exchange(to_heads([keys_tan, keys, values, values_tan], devices))
    rows = kv.shape[0]

    parts = [kv]
    for first in (0, 1):
        pairs = [(i, i + 1) for i in range(first, frames - 1, 2)]
        if pairs:
            start = jnp.where(frame % 2 == first, rows - HALO, 0)
            edge = lax.dynamic_slice_in_dim(kv, start, HALO, axis=0)
            parts.append(lax.ppermute(edge, "frames", pairs + [(j, i) for i, j in pairs]))

    q_pair = exchange(to_heads([query, query_tan], devices))
    table = slots(neighbors, frame, neighbors.shape[0])
    me = lax.axis_index("heads").reshape(1).astype(jnp.int32)
    half, middle = devices // 2, neighbors.shape[0] // 2
    back, later = {}, []
    for slot, first in ((half, middle), (0, 0)):
        pieces = attend(me, table, q_pair, parts, later, tokens, first, middle)
        for k, piece in enumerate(pieces, slot):
            pairs = [(d, d ^ k) for d in range(devices)]
            back[k] = lax.ppermute(piece, "heads", pairs) if k else piece
        later = [back[half], back[half + 1]]
    return from_heads(me, back, 2)


def solution(mesh):
    own = P(("frames", "heads"), None)
    return jax.shard_map(
        per_device,
        mesh=mesh,
        in_specs=(own,) * 6 + (P("frames", None),),
        out_specs=(own, own),
        check_vma=False,
    )
```

```python
import functools
import math

import jax
import jax.numpy as jnp
from jax import lax
from jax.experimental import pallas as pl
from jax.experimental.pallas import tpu as pltpu
from jax.sharding import PartitionSpec as P

BQ = 256
WK = 4
HB = 4
PAIR = 2
PARAMS = pltpu.CompilerParams(vmem_limit_bytes=40 * 1024 * 1024)
ANY = pl.BlockSpec(memory_space=pl.ANY)
HBM = pl.BlockSpec(memory_space=pltpu.HBM)
VMEM = pl.BlockSpec(memory_space=pltpu.VMEM)
SMEM = pl.BlockSpec(memory_space=pltpu.SMEM)


def pin(*arrays):
    return [pltpu.with_memory_space_constraint(a, pltpu.HBM) for a in arrays]


def moves(size):
    return pl.CostEstimate(flops=0, bytes_accessed=size, transcendentals=0)


def pack_kernel(*refs, count, chunks):
    arrays, out = refs[:count], refs[count]
    held, staged, sems, out_sems = refs[-4:]
    chips, columns = out.shape[0], held.shape[2]
    hd, some, step = columns // chips // PAIR, chips // chunks, columns // chunks
    copies = {}
    for c in range(chunks):
        lanes = pl.ds(c * step, step)
        for a, array in enumerate(arrays):
            copies[c, a] = pltpu.make_async_copy(
                array.at[:, lanes], held.at[a, :, lanes], sems.at[c, a]
            )
            copies[c, a].start()
    sends = []
    for c in range(chunks):
        for a in range(count):
            copies[c, a].wait()
        for chip in range(c * some, (c + 1) * some):
            for h in range(PAIR):
                source = (chip * PAIR + h) * hd
                for a in range(count):
                    target = (h * count + a) * hd
                    staged[chip, :, target : target + hd] = held[a, :, source : source + hd]
        part = pl.ds(c * some, some)
        sends.append(pltpu.make_async_copy(staged.at[part], out.at[part], out_sems.at[c]))
        sends[-1].start()
    for send in sends:
        send.wait()


def to_chips(arrays, devices, chunks=4):
    tokens, columns = arrays[0].shape
    count, chips = len(arrays), devices // PAIR
    shape = (chips, tokens, count * columns // chips)
    return pl.pallas_call(
        functools.partial(pack_kernel, count=count, chunks=chunks),
        in_specs=[HBM] * count,
        out_specs=HBM,
        out_shape=pltpu.HBM(shape, jnp.bfloat16),
        scratch_shapes=[
            pltpu.VMEM((count, tokens, columns), jnp.bfloat16),
            pltpu.VMEM(shape, jnp.bfloat16),
            pltpu.SemaphoreType.DMA((chunks, count)),
            pltpu.SemaphoreType.DMA((chunks,)),
        ],
        compiler_params=PARAMS,
        cost_estimate=moves(4 * count * tokens * columns),
    )(*pin(*arrays))


def exchange(pieces, devices):
    groups = [list(range(core, devices, PAIR)) for core in range(PAIR)]
    return lax.all_to_all(
        pieces, "heads", split_axis=0, concat_axis=0, axis_index_groups=groups, tiled=True
    )


def unpack_kernel(chip, *refs, order):
    pieces, arrays = refs[: len(order)], refs[len(order) :]
    hd = pieces[0].shape[1] // len(arrays) // PAIR
    for k, piece in zip(order, pieces):
        for h in range(PAIR):
            columns = pl.ds(pl.multiple_of(((chip[0] ^ k) * PAIR + h) * hd, hd), hd)
            for a, array in enumerate(arrays):
                source = (h * len(arrays) + a) * hd
                array[:, columns] = piece[:, source : source + hd]


def unpack(chip, pieces, count):
    tokens, width = pieces[0].shape
    columns = len(pieces) * width // count
    return pl.pallas_call(
        functools.partial(unpack_kernel, order=list(pieces)),
        in_specs=[SMEM] + [VMEM] * len(pieces),
        out_specs=[VMEM] * count,
        out_shape=[jax.ShapeDtypeStruct((tokens, columns), jnp.bfloat16)] * count,
        compiler_params=PARAMS,
        cost_estimate=moves(4 * len(pieces) * tokens * width),
    )(chip, *pieces.values())


def attend_kernel(chip, table, q_ref, *refs, sources, later, first, hd):
    parts, outs = refs[: PAIR * sources], refs[PAIR * sources + later : -2]
    kv, sems = refs[-2:]
    tokens = q_ref.shape[1]
    copies = []
    for core in range(PAIR):
        row = 0
        for i in range(sources):
            ref = parts[core * sources + i]
            target = kv.at[pl.ds(row, ref.shape[0]), core]
            copies.append(pltpu.make_async_copy(ref, target, sems.at[core * sources + i]))
            row += ref.shape[0]
    for copy in copies:
        copy.start()
    for copy in copies:
        copy.wait()

    scale = hd ** (-0.5)
    factor = scale * math.log2(math.e)
    trans = (((1,), (1,)), ((), ()))

    def products(i, h):
        block = chip[0] ^ (first + i)
        both = q_ref[block, :, 2 * h * hd : 2 * (h + 1) * hd]
        query = both[:, :hd]
        left = jnp.concatenate([jnp.zeros_like(query), query], axis=1)
        left = jnp.concatenate([left, both], axis=0)
        window = [table[block * WK + w] for w in range(WK)]
        low = 4 * h * hd
        scores, tans = [], []
        for index in window:
            keys = kv[index, :, :, low : low + 2 * hd].reshape(BQ, 2 * hd)
            product = lax.dot_general(left, keys, trans, preferred_element_type=jnp.float32)
            scores.append(product[:tokens])
            tans.append(product[tokens:])
        return window, scores, tans

    def finish(i, h, window, scores, tans):
        top = functools.reduce(jnp.maximum, scores)
        top = jnp.max(top, axis=1, keepdims=True) * factor
        probs = [jnp.exp2(s * factor - top) for s in scores]
        weighted = [p * t for p, t in zip(probs, tans)]
        total = jnp.sum(functools.reduce(jnp.add, probs), axis=1, keepdims=True)
        mean = jnp.sum(functools.reduce(jnp.add, weighted), axis=1, keepdims=True)
        low = (4 * h + 2) * hd
        mixed = jnp.zeros((2 * tokens, 2 * hd), jnp.float32)
        for index, p, w in zip(window, probs, weighted):
            vals = kv[index, :, :, low : low + 2 * hd].reshape(BQ, 2 * hd)
            right = jnp.concatenate([p.astype(jnp.bfloat16), w.astype(jnp.bfloat16)], axis=0)
            mixed += jnp.dot(right, vals, preferred_element_type=jnp.float32)
        inverse = 1.0 / total
        out = mixed[:tokens, :hd] * inverse
        tan = (mixed[:tokens, hd:] + scale * mixed[tokens:, :hd]) * inverse
        tan = tan - (scale * mean * inverse) * out
        outs[i][:, 2 * h * hd : (2 * h + 1) * hd] = out.astype(jnp.bfloat16)
        outs[i][:, (2 * h + 1) * hd : 2 * (h + 1) * hd] = tan.astype(jnp.bfloat16)

    units = [(i, h) for i in range(len(outs)) for h in range(PAIR)]
    ahead = products(*units[0])
    for unit, following in zip(units, units[1:] + [None]):
        current = ahead
        if following is not None:
            ahead = products(*following)
        finish(*unit, *current)


def attend(chip, table, queries, mine, other, later, first, count):
    _, tokens, width = queries.shape
    hd, sources = width // (2 * PAIR), len(mine)
    total = sum(a.shape[0] for a in mine)
    elements = count * BQ * WK * BQ
    return pl.pallas_call(
        functools.partial(
            attend_kernel, sources=sources, later=len(later), first=first, hd=hd
        ),
        in_specs=[SMEM, SMEM, VMEM] + [ANY] * (PAIR * sources + len(later)),
        out_specs=[VMEM] * count,
        out_shape=[jax.ShapeDtypeStruct((tokens, width), jnp.bfloat16)] * count,
        scratch_shapes=[
            pltpu.VMEM((total, PAIR, tokens, 2 * width), jnp.bfloat16),
            pltpu.SemaphoreType.DMA((PAIR * sources,)),
        ],
        compiler_params=PARAMS,
        cost_estimate=pl.CostEstimate(
            flops=12 * elements * hd,
            bytes_accessed=8 * total * tokens * width,
            transcendentals=elements,
        ),
    )(chip, table, queries, *mine, *other, *later)


def slots(neighbors, frame, blocks):
    local = neighbors - frame * blocks
    even = frame % 2 == 0
    before = blocks + jnp.where(even, HB, 0) + local + HB
    after = blocks + jnp.where(even, 0, HB) + local - blocks
    return jnp.where(local < 0, before, jnp.where(local >= blocks, after, local)).reshape(-1)


def per_device(query, keys, values, query_tan, keys_tan, values_tan, neighbors):
    devices, frames = lax.axis_size("heads"), lax.axis_size("frames")
    frame = lax.axis_index("frames")
    chip = (lax.axis_index("heads") // PAIR).reshape(1).astype(jnp.int32)
    blocks = neighbors.shape[0]
    swap = [(d, d ^ 1) for d in range(devices)]
    kv = exchange(to_chips([keys_tan, keys, values, values_tan], devices), devices)

    mine = [kv]
    for first in (0, 1):
        pairs = [(i, i + 1) for i in range(first, frames - 1, 2)]
        if pairs:
            start = jnp.where(frame % 2 == first, blocks - HB, 0)
            edge = lax.dynamic_slice_in_dim(kv, start, HB, axis=0)
            mine.append(lax.ppermute(edge, "frames", pairs + [(j, i) for i, j in pairs]))
    other = [lax.ppermute(a, "heads", swap) for a in mine]

    queries = exchange(to_chips([query, query_tan], devices), devices)
    table = slots(neighbors, frame, blocks)
    half = blocks // 2
    back, later = {}, []
    for first in (half, 0):
        pieces = attend(chip, table, queries, mine, other, later, first, half)
        for k, piece in enumerate(pieces, first):
            pairs = [(d, d ^ (k * PAIR)) for d in range(devices)]
            back[k] = lax.ppermute(piece, "heads", pairs) if k else piece
        later = [back[half]]
    return unpack(chip, back, 2)


def solution(mesh):
    own = P(("frames", "heads"), None)
    return jax.shard_map(
        per_device,
        mesh=mesh,
        in_specs=(own,) * 6 + (P("frames", None),),
        out_specs=(own, own),
        check_vma=False,
    )
```

```python
import functools
import math

import jax
import jax.numpy as jnp
from jax import lax
from jax.experimental import pallas as pl
from jax.experimental.pallas import tpu as pltpu
from jax.sharding import PartitionSpec as P

BQ = 256
WK = 4
HB = 4
PAIR = 2
LEAD = 16
PARAMS = pltpu.CompilerParams(vmem_limit_bytes=40 * 1024 * 1024)
ANY = pl.BlockSpec(memory_space=pl.ANY)
HBM = pl.BlockSpec(memory_space=pltpu.HBM)
VMEM = pl.BlockSpec(memory_space=pltpu.VMEM)
SMEM = pl.BlockSpec(memory_space=pltpu.SMEM)


def pin(*arrays):
    return [pltpu.with_memory_space_constraint(a, pltpu.HBM) for a in arrays]


def moves(size):
    return pl.CostEstimate(flops=0, bytes_accessed=size, transcendentals=0)


def pack_kernel(before, *refs, count, chunks):
    arrays, out, zero = refs[:count], refs[count], refs[count + 1]
    held, staged, sems, out_sems = refs[-4:]
    zero[0] = before[0]
    chips, columns = out.shape[0], held.shape[2]
    hd, some, step = columns // chips // PAIR, chips // chunks, columns // chunks
    copies = {}
    for c in range(chunks):
        lanes = pl.ds(c * step, step)
        for a, array in enumerate(arrays):
            copies[c, a] = pltpu.make_async_copy(
                array.at[:, lanes], held.at[a, :, lanes], sems.at[c, a]
            )
            copies[c, a].start()
    sends = []
    for c in range(chunks):
        for a in range(count):
            copies[c, a].wait()
        for chip in range(c * some, (c + 1) * some):
            for h in range(PAIR):
                source = (chip * PAIR + h) * hd
                for a in range(count):
                    target = (h * count + a) * hd
                    staged[chip, :, target : target + hd] = held[a, :, source : source + hd]
        part = pl.ds(c * some, some)
        sends.append(pltpu.make_async_copy(staged.at[part], out.at[part], out_sems.at[c]))
        sends[-1].start()
    for send in sends:
        send.wait()


def to_chips(before, arrays, devices, chunks=4):
    tokens, columns = arrays[0].shape
    count, chips = len(arrays), devices // PAIR
    shape = (chips, tokens, count * columns // chips)
    return pl.pallas_call(
        functools.partial(pack_kernel, count=count, chunks=chunks),
        in_specs=[SMEM] + [HBM] * count,
        out_specs=[HBM, SMEM],
        out_shape=[pltpu.HBM(shape, jnp.bfloat16), jax.ShapeDtypeStruct((1,), jnp.int32)],
        scratch_shapes=[
            pltpu.VMEM((count, tokens, columns), jnp.bfloat16),
            pltpu.VMEM(shape, jnp.bfloat16),
            pltpu.SemaphoreType.DMA((chunks, count)),
            pltpu.SemaphoreType.DMA((chunks,)),
        ],
        compiler_params=PARAMS,
        cost_estimate=moves(4 * count * tokens * columns),
    )(before, *pin(*arrays))


def exchange(pieces, devices):
    groups = [list(range(core, devices, PAIR)) for core in range(PAIR)]
    return lax.all_to_all(
        pieces, "heads", split_axis=0, concat_axis=0, axis_index_groups=groups, tiled=True
    )


def unpack_kernel(chip, *refs, places):
    pieces, arrays = refs[: len(places)], refs[len(places) :]
    hd = pieces[0].shape[1] // len(arrays) // PAIR
    for (k, row), piece in zip(places, pieces):
        rows = slice(row, row + piece.shape[0])
        for h in range(PAIR):
            columns = pl.ds(pl.multiple_of(((chip[0] ^ k) * PAIR + h) * hd, hd), hd)
            for a, array in enumerate(arrays):
                source = (h * len(arrays) + a) * hd
                array[rows, columns] = piece[:, source : source + hd]


def unpack(chip, pieces, tokens, columns, count):
    return pl.pallas_call(
        functools.partial(unpack_kernel, places=list(pieces)),
        in_specs=[SMEM] + [VMEM] * len(pieces),
        out_specs=[VMEM] * count,
        out_shape=[jax.ShapeDtypeStruct((tokens, columns), jnp.bfloat16)] * count,
        compiler_params=PARAMS,
        cost_estimate=moves(4 * count * tokens * columns),
    )(chip, *pieces.values())


def attend_kernel(chip, table, q_ref, *refs, sources, later, places, hd):
    parts, outs = refs[: PAIR * sources], refs[PAIR * sources + later : -2]
    kv, sems = refs[-2:]
    tokens = q_ref.shape[1]
    copies = []
    for core in range(PAIR):
        row = 0
        for i in range(sources):
            ref = parts[core * sources + i]
            target = kv.at[pl.ds(row, ref.shape[0]), core]
            copies.append(pltpu.make_async_copy(ref, target, sems.at[core * sources + i]))
            row += ref.shape[0]
    for copy in copies:
        copy.start()
    for copy in copies:
        copy.wait()

    scale = hd ** (-0.5)
    factor = scale * math.log2(math.e)
    trans = (((1,), (1,)), ((), ()))

    def products(k, h):
        block = chip[0] ^ k
        both = q_ref[block, :, 2 * h * hd : 2 * (h + 1) * hd]
        query = both[:, :hd]
        left = jnp.concatenate([jnp.zeros_like(query), query], axis=1)
        left = jnp.concatenate([left, both], axis=0)
        window = [table[block * WK + w] for w in range(WK)]
        low = 4 * h * hd
        scores, tans = [], []
        for index in window:
            keys = kv[index, :, :, low : low + 2 * hd].reshape(BQ, 2 * hd)
            product = lax.dot_general(left, keys, trans, preferred_element_type=jnp.float32)
            scores.append(product[:tokens])
            tans.append(product[tokens:])
        return window, scores, tans

    def finish(k, h, window, scores, tans):
        top = functools.reduce(jnp.maximum, scores)
        top = jnp.max(top, axis=1, keepdims=True) * factor
        probs = [jnp.exp2(s * factor - top) for s in scores]
        weighted = [p * t for p, t in zip(probs, tans)]
        total = jnp.sum(functools.reduce(jnp.add, probs), axis=1, keepdims=True)
        mean = jnp.sum(functools.reduce(jnp.add, weighted), axis=1, keepdims=True)
        low = (4 * h + 2) * hd
        mixed = jnp.zeros((2 * tokens, 2 * hd), jnp.float32)
        for index, p, w in zip(window, probs, weighted):
            vals = kv[index, :, :, low : low + 2 * hd].reshape(BQ, 2 * hd)
            right = jnp.concatenate([p.astype(jnp.bfloat16), w.astype(jnp.bfloat16)], axis=0)
            mixed += jnp.dot(right, vals, preferred_element_type=jnp.float32)
        inverse = 1.0 / total
        out = mixed[:tokens, :hd] * inverse
        tan = (mixed[:tokens, hd:] + scale * mixed[tokens:, :hd]) * inverse
        tan = tan - (scale * mean * inverse) * out
        for (slot, row), ref in zip(places, outs):
            if slot == k:
                rows = slice(row, row + ref.shape[0])
                ref[:, 2 * h * hd : (2 * h + 1) * hd] = out[rows].astype(jnp.bfloat16)
                ref[:, (2 * h + 1) * hd : 2 * (h + 1) * hd] = tan[rows].astype(jnp.bfloat16)

    units = [(k, h) for k in dict(places) for h in range(PAIR)]
    ahead = products(*units[0])
    for unit, following in zip(units, units[1:] + [None]):
        current = ahead
        if following is not None:
            ahead = products(*following)
        finish(*unit, *current)


def attend(chip, table, queries, mine, other, later, places):
    _, tokens, width = queries.shape
    hd, sources = width // (2 * PAIR), len(mine)
    total = sum(a.shape[0] for a in mine)
    elements = len(dict(places)) * BQ * WK * BQ
    ends = [following[1] or tokens for following in places[1:]] + [tokens]
    sizes = [end - row for (_, row), end in zip(places, ends)]
    return pl.pallas_call(
        functools.partial(
            attend_kernel, sources=sources, later=len(later), places=places, hd=hd
        ),
        in_specs=[SMEM, SMEM, VMEM] + [ANY] * (PAIR * sources + len(later)),
        out_specs=[VMEM] * len(places),
        out_shape=[jax.ShapeDtypeStruct((size, width), jnp.bfloat16) for size in sizes],
        scratch_shapes=[
            pltpu.VMEM((total, PAIR, tokens, 2 * width), jnp.bfloat16),
            pltpu.SemaphoreType.DMA((PAIR * sources,)),
        ],
        compiler_params=PARAMS,
        cost_estimate=pl.CostEstimate(
            flops=12 * elements * hd,
            bytes_accessed=8 * total * tokens * width,
            transcendentals=elements,
        ),
    )(chip, table, queries, *mine, *other, *later)


def slots(neighbors, frame, blocks):
    local = neighbors - frame * blocks
    even = frame % 2 == 0
    before = blocks + jnp.where(even, HB, 0) + local + HB
    after = blocks + jnp.where(even, 0, HB) + local - blocks
    return jnp.where(local < 0, before, jnp.where(local >= blocks, after, local)).reshape(-1)


def per_device(query, keys, values, query_tan, keys_tan, values_tan, neighbors):
    devices, frames = lax.axis_size("heads"), lax.axis_size("frames")
    frame = lax.axis_index("frames")
    chip = (lax.axis_index("heads") // PAIR).reshape(1).astype(jnp.int32)
    blocks = neighbors.shape[0]
    swap = [(d, d ^ 1) for d in range(devices)]
    zero = jnp.zeros((1,), jnp.int32)
    kv_sent, zero = to_chips(zero, [keys_tan, keys, values, values_tan], devices)
    q_sent, zero = to_chips(zero, [query, query_tan], devices)
    kv = exchange(kv_sent, devices)

    mine = [kv]
    for first in (0, 1):
        pairs = [(i, i + 1) for i in range(first, frames - 1, 2)]
        if pairs:
            start = jnp.where(frame % 2 == first, blocks - HB, 0) + zero[0]
            edge = lax.dynamic_slice_in_dim(kv, start, HB, axis=0)
            mine.append(lax.ppermute(edge, "frames", pairs + [(j, i) for i, j in pairs]))
    other = [lax.ppermute(a, "heads", swap) for a in mine]

    queries = exchange(q_sent, devices)
    table = slots(neighbors, frame, blocks)
    half = blocks // 2
    far, near = [(k, 0) for k in range(half, blocks)], [(k, 0) for k in range(half)]
    far.insert(1, (half, LEAD))
    back, later = {}, []
    for places in (far, near):
        pieces = attend(chip, table, queries, mine, other, later, places)
        for place, piece in zip(places, pieces):
            pairs = [(d, d ^ (place[0] * PAIR)) for d in range(devices)]
            back[place] = lax.ppermute(piece, "heads", pairs) if place[0] else piece
        later = [back[far[0]]]
    return unpack(chip, back, *query.shape, 2)


def solution(mesh):
    own = P(("frames", "heads"), None)
    return jax.shard_map(
        per_device,
        mesh=mesh,
        in_specs=(own,) * 6 + (P("frames", None),),
        out_specs=(own, own),
        check_vma=False,
    )
```

```python
import functools
import math

import jax
import jax.numpy as jnp
from jax import lax
from jax.experimental import pallas as pl
from jax.experimental.pallas import tpu as pltpu
from jax.sharding import PartitionSpec as P

BQ = 256
WK = 4
HB = 4
PAIR = 2
PARAMS = pltpu.CompilerParams(vmem_limit_bytes=40 * 1024 * 1024)
ANY = pl.BlockSpec(memory_space=pl.ANY)
HBM = pl.BlockSpec(memory_space=pltpu.HBM)
VMEM = pl.BlockSpec(memory_space=pltpu.VMEM)
SMEM = pl.BlockSpec(memory_space=pltpu.SMEM)


def pin(*arrays):
    return [pltpu.with_memory_space_constraint(a, pltpu.HBM) for a in arrays]


def moves(size):
    return pl.CostEstimate(flops=0, bytes_accessed=size, transcendentals=0)


def pack_kernel(*refs, count, before, chunks):
    arrays, out = refs[:count], refs[count + before]
    held, staged, sems, out_sems = refs[-4:]
    if before:
        refs[count + before + 1][0] = 0
    chips, columns = out.shape[0], held.shape[2]
    hd, some, step = columns // chips // PAIR, chips // chunks, columns // chunks
    copies = {}
    for c in range(chunks):
        lanes = pl.ds(c * step, step)
        for a, array in enumerate(arrays):
            copies[c, a] = pltpu.make_async_copy(
                array.at[:, lanes], held.at[a, :, lanes], sems.at[c, a]
            )
            copies[c, a].start()
    sends = []
    for c in range(chunks):
        for a in range(count):
            copies[c, a].wait()
        for chip in range(c * some, (c + 1) * some):
            for h in range(PAIR):
                source = (chip * PAIR + h) * hd
                for a in range(count):
                    target = (h * count + a) * hd
                    staged[chip, :, target : target + hd] = held[a, :, source : source + hd]
        part = pl.ds(c * some, some)
        sends.append(pltpu.make_async_copy(staged.at[part], out.at[part], out_sems.at[c]))
        sends[-1].start()
    for send in sends:
        send.wait()


def to_chips(arrays, devices, before=(), chunks=4):
    tokens, columns = arrays[0].shape
    count, chips = len(arrays), devices // PAIR
    shape = (chips, tokens, count * columns // chips)
    more = min(len(before), 1)
    return pl.pallas_call(
        functools.partial(pack_kernel, count=count, before=len(before), chunks=chunks),
        in_specs=[HBM] * (count + len(before)),
        out_specs=[HBM] + [SMEM] * more,
        out_shape=[pltpu.HBM(shape, jnp.bfloat16)]
        + [jax.ShapeDtypeStruct((1,), jnp.int32)] * more,
        scratch_shapes=[
            pltpu.VMEM((count, tokens, columns), jnp.bfloat16),
            pltpu.VMEM(shape, jnp.bfloat16),
            pltpu.SemaphoreType.DMA((chunks, count)),
            pltpu.SemaphoreType.DMA((chunks,)),
        ],
        compiler_params=PARAMS,
        cost_estimate=moves(4 * count * tokens * columns),
    )(*pin(*arrays, *before))


def exchange(pieces, devices):
    groups = [list(range(core, devices, PAIR)) for core in range(PAIR)]
    return lax.all_to_all(
        pieces, "heads", split_axis=0, concat_axis=0, axis_index_groups=groups, tiled=True
    )


def unpack_kernel(chip, *refs, order):
    pieces, arrays = refs[: len(order)], refs[len(order) :]
    hd = pieces[0].shape[1] // len(arrays) // PAIR
    for k, piece in zip(order, pieces):
        for h in range(PAIR):
            columns = pl.ds(pl.multiple_of(((chip[0] ^ k) * PAIR + h) * hd, hd), hd)
            for a, array in enumerate(arrays):
                source = (h * len(arrays) + a) * hd
                array[:, columns] = piece[:, source : source + hd]


def unpack(chip, pieces, count):
    tokens, width = pieces[0].shape
    columns = len(pieces) * width // count
    return pl.pallas_call(
        functools.partial(unpack_kernel, order=list(pieces)),
        in_specs=[SMEM] + [VMEM] * len(pieces),
        out_specs=[VMEM] * count,
        out_shape=[jax.ShapeDtypeStruct((tokens, columns), jnp.bfloat16)] * count,
        compiler_params=PARAMS,
        cost_estimate=moves(4 * len(pieces) * tokens * width),
    )(chip, *pieces.values())


def attend_kernel(chip, table, q_ref, *refs, sources, later, slots, hd):
    parts, outs = refs[: PAIR * sources], refs[PAIR * sources + later : -2]
    kv, sems = refs[-2:]
    tokens = q_ref.shape[1]
    groups = 2 * PAIR
    copies = []
    for g in range(groups):
        lanes = pl.ds(g * 2 * hd, 2 * hd)
        for core in range(PAIR):
            row = 0
            for i in range(sources):
                ref, n = parts[core * sources + i], core * sources + i
                rows = pl.ds(row, ref.shape[0])
                copies.append(
                    pltpu.make_async_copy(
                        ref.at[:, :, lanes], kv.at[rows, core, :, lanes], sems.at[g, n]
                    )
                )
                row += ref.shape[0]
    for copy in copies:
        copy.start()

    def arrive(group):
        size = len(copies) // groups
        for copy in copies[group * size : (group + 1) * size]:
            copy.wait()

    scale = hd ** (-0.5)
    factor = scale * math.log2(math.e)
    trans = (((1,), (1,)), ((), ()))

    def products(k, h):
        block = chip[0] ^ k
        both = q_ref[block, :, 2 * h * hd : 2 * (h + 1) * hd]
        query = both[:, :hd]
        left = jnp.concatenate([jnp.zeros_like(query), query], axis=1)
        left = jnp.concatenate([left, both], axis=0)
        window = [table[block * WK + w] for w in range(WK)]
        low = 4 * h * hd
        scores, tans = [], []
        for index in window:
            keys = kv[index, :, :, low : low + 2 * hd].reshape(BQ, 2 * hd)
            product = lax.dot_general(left, keys, trans, preferred_element_type=jnp.float32)
            scores.append(product[:tokens])
            tans.append(product[tokens:])
        return window, scores, tans

    def finish(k, h, window, scores, tans):
        top = functools.reduce(jnp.maximum, scores)
        top = jnp.max(top, axis=1, keepdims=True) * factor
        probs = [jnp.exp2(s * factor - top) for s in scores]
        weighted = [p * t for p, t in zip(probs, tans)]
        total = jnp.sum(functools.reduce(jnp.add, probs), axis=1, keepdims=True)
        mean = jnp.sum(functools.reduce(jnp.add, weighted), axis=1, keepdims=True)
        low = (4 * h + 2) * hd
        mixed = jnp.zeros((2 * tokens, 2 * hd), jnp.float32)
        for index, p, w in zip(window, probs, weighted):
            vals = kv[index, :, :, low : low + 2 * hd].reshape(BQ, 2 * hd)
            right = jnp.concatenate([p.astype(jnp.bfloat16), w.astype(jnp.bfloat16)], axis=0)
            mixed += jnp.dot(right, vals, preferred_element_type=jnp.float32)
        inverse = 1.0 / total
        out = mixed[:tokens, :hd] * inverse
        tan = (mixed[:tokens, hd:] + scale * mixed[tokens:, :hd]) * inverse
        tan = tan - (scale * mean * inverse) * out
        ref = outs[slots.index(k)]
        ref[:, 2 * h * hd : (2 * h + 1) * hd] = out.astype(jnp.bfloat16)
        ref[:, (2 * h + 1) * hd : 2 * (h + 1) * hd] = tan.astype(jnp.bfloat16)

    units = [(k, h) for h in range(PAIR) for k in slots]
    arrive(0)
    ahead = products(*units[0])
    arrive(1)
    for unit, following in zip(units, units[1:] + [None]):
        current = ahead
        if following is not None:
            if following[1] > unit[1]:
                arrive(2)
                arrive(3)
            ahead = products(*following)
        finish(*unit, *current)


def attend(chip, table, queries, mine, other, later, slots):
    _, tokens, width = queries.shape
    hd, sources = width // (2 * PAIR), len(mine)
    total = sum(a.shape[0] for a in mine)
    elements = len(slots) * BQ * WK * BQ
    return pl.pallas_call(
        functools.partial(
            attend_kernel, sources=sources, later=len(later), slots=slots, hd=hd
        ),
        in_specs=[SMEM, SMEM, VMEM] + [ANY] * (PAIR * sources + len(later)),
        out_specs=[VMEM] * len(slots),
        out_shape=[jax.ShapeDtypeStruct((tokens, width), jnp.bfloat16)] * len(slots),
        scratch_shapes=[
            pltpu.VMEM((total, PAIR, tokens, 2 * width), jnp.bfloat16),
            pltpu.SemaphoreType.DMA((2 * PAIR, PAIR * sources)),
        ],
        compiler_params=PARAMS,
        cost_estimate=pl.CostEstimate(
            flops=12 * elements * hd,
            bytes_accessed=8 * total * tokens * width,
            transcendentals=elements,
        ),
    )(chip, table, queries, *mine, *other, *later)


def places(neighbors, frame, blocks):
    local = neighbors - frame * blocks
    even = frame % 2 == 0
    before = blocks + jnp.where(even, HB, 0) + local + HB
    after = blocks + jnp.where(even, 0, HB) + local - blocks
    return jnp.where(local < 0, before, jnp.where(local >= blocks, after, local)).reshape(-1)


def per_device(query, keys, values, query_tan, keys_tan, values_tan, neighbors):
    devices, frames = lax.axis_size("heads"), lax.axis_size("frames")
    frame = lax.axis_index("frames")
    chip = (lax.axis_index("heads") // PAIR).reshape(1).astype(jnp.int32)
    blocks = neighbors.shape[0]
    swap = [(d, d ^ 1) for d in range(devices)]
    (kv_sent,) = to_chips([keys_tan, keys, values, values_tan], devices)
    q_sent, zero = to_chips([query, query_tan], devices, [kv_sent])
    kv = exchange(kv_sent, devices)

    mine = [kv]
    for first in (0, 1):
        pairs = [(i, i + 1) for i in range(first, frames - 1, 2)]
        if pairs:
            start = jnp.where(frame % 2 == first, blocks - HB, 0) + zero[0]
            edge = lax.dynamic_slice_in_dim(kv, start, HB, axis=0)
            mine.append(lax.ppermute(edge, "frames", pairs + [(j, i) for i, j in pairs]))
    other = [lax.ppermute(a, "heads", swap) for a in mine]

    queries = exchange(q_sent, devices)
    table = places(neighbors, frame, blocks)
    half = blocks // 2
    back, later = {}, []
    for part in ([1, *range(half, blocks)], [*range(2, half), 0]):
        pieces = attend(chip, table, queries, mine, other, later, part)
        for k, piece in zip(part, pieces):
            pairs = [(d, d ^ (k * PAIR)) for d in range(devices)]
            back[k] = lax.ppermute(piece, "heads", pairs) if k else piece
        later = [back[1]]
    return unpack(chip, back, 2)


def solution(mesh):
    own = P(("frames", "heads"), None)
    return jax.shard_map(
        per_device,
        mesh=mesh,
        in_specs=(own,) * 6 + (P("frames", None),),
        out_specs=(own, own),
        check_vma=False,
    )
```

```python
import functools
import math

import jax
import jax.numpy as jnp
from jax import lax
from jax.experimental import pallas as pl
from jax.experimental.pallas import tpu as pltpu
from jax.sharding import PartitionSpec as P

BQ = 256
WK = 4
HB = 4
PAIR = 2
LEAD = 16
PARAMS = pltpu.CompilerParams(vmem_limit_bytes=40 * 1024 * 1024)
ANY = pl.BlockSpec(memory_space=pl.ANY)
HBM = pl.BlockSpec(memory_space=pltpu.HBM)
VMEM = pl.BlockSpec(memory_space=pltpu.VMEM)
SMEM = pl.BlockSpec(memory_space=pltpu.SMEM)


def pin(*arrays):
    return [pltpu.with_memory_space_constraint(a, pltpu.HBM) for a in arrays]


def moves(size):
    return pl.CostEstimate(flops=0, bytes_accessed=size, transcendentals=0)


def pack_kernel(*refs, count, before, chunks):
    arrays, out = refs[:count], refs[count + before]
    held, staged, sems, out_sems = refs[-4:]
    if before:
        refs[count + before + 1][0] = 0
    chips, columns = out.shape[0], held.shape[2]
    hd, some, step = columns // chips // PAIR, chips // chunks, columns // chunks
    copies = {}
    for c in range(chunks):
        lanes = pl.ds(c * step, step)
        for a, array in enumerate(arrays):
            copies[c, a] = pltpu.make_async_copy(
                array.at[:, lanes], held.at[a, :, lanes], sems.at[c, a]
            )
            copies[c, a].start()
    sends = []
    for c in range(chunks):
        for a in range(count):
            copies[c, a].wait()
        for chip in range(c * some, (c + 1) * some):
            for h in range(PAIR):
                source = (chip * PAIR + h) * hd
                for a in range(count):
                    target = (h * count + a) * hd
                    staged[chip, :, target : target + hd] = held[a, :, source : source + hd]
        part = pl.ds(c * some, some)
        sends.append(pltpu.make_async_copy(staged.at[part], out.at[part], out_sems.at[c]))
        sends[-1].start()
    for send in sends:
        send.wait()


def to_chips(arrays, devices, before=(), chunks=4):
    tokens, columns = arrays[0].shape
    count, chips = len(arrays), devices // PAIR
    shape = (chips, tokens, count * columns // chips)
    more = min(len(before), 1)
    return pl.pallas_call(
        functools.partial(pack_kernel, count=count, before=len(before), chunks=chunks),
        in_specs=[HBM] * (count + len(before)),
        out_specs=[HBM] + [SMEM] * more,
        out_shape=[pltpu.HBM(shape, jnp.bfloat16)]
        + [jax.ShapeDtypeStruct((1,), jnp.int32)] * more,
        scratch_shapes=[
            pltpu.VMEM((count, tokens, columns), jnp.bfloat16),
            pltpu.VMEM(shape, jnp.bfloat16),
            pltpu.SemaphoreType.DMA((chunks, count)),
            pltpu.SemaphoreType.DMA((chunks,)),
        ],
        compiler_params=PARAMS,
        cost_estimate=moves(4 * count * tokens * columns),
    )(*pin(*arrays, *before))


def exchange(pieces, devices):
    groups = [list(range(core, devices, PAIR)) for core in range(PAIR)]
    return lax.all_to_all(
        pieces, "heads", split_axis=0, concat_axis=0, axis_index_groups=groups, tiled=True
    )


def unpack_kernel(chip, *refs, places):
    pieces, arrays = refs[: len(places)], refs[len(places) :]
    hd = pieces[0].shape[1] // len(arrays) // PAIR
    for (k, row), piece in zip(places, pieces):
        rows = slice(row, row + piece.shape[0])
        for h in range(PAIR):
            columns = pl.ds(pl.multiple_of(((chip[0] ^ k) * PAIR + h) * hd, hd), hd)
            for a, array in enumerate(arrays):
                source = (h * len(arrays) + a) * hd
                array[rows, columns] = piece[:, source : source + hd]


def unpack(chip, pieces, tokens, columns, count):
    return pl.pallas_call(
        functools.partial(unpack_kernel, places=list(pieces)),
        in_specs=[SMEM] + [VMEM] * len(pieces),
        out_specs=[VMEM] * count,
        out_shape=[jax.ShapeDtypeStruct((tokens, columns), jnp.bfloat16)] * count,
        compiler_params=PARAMS,
        cost_estimate=moves(4 * count * tokens * columns),
    )(chip, *pieces.values())


def attend_kernel(chip, table, q_ref, *refs, sources, later, places, hd):
    parts, outs = refs[: PAIR * sources], refs[PAIR * sources + later : -2]
    kv, sems = refs[-2:]
    tokens = q_ref.shape[1]
    groups = 2 * PAIR
    copies = []
    for g in range(groups):
        lanes = pl.ds(g * 2 * hd, 2 * hd)
        for core in range(PAIR):
            row = 0
            for i in range(sources):
                ref, n = parts[core * sources + i], core * sources + i
                rows = pl.ds(row, ref.shape[0])
                copies.append(
                    pltpu.make_async_copy(
                        ref.at[:, :, lanes], kv.at[rows, core, :, lanes], sems.at[g, n]
                    )
                )
                row += ref.shape[0]
    for copy in copies:
        copy.start()

    def arrive(group):
        size = len(copies) // groups
        for copy in copies[group * size : (group + 1) * size]:
            copy.wait()

    scale = hd ** (-0.5)
    factor = scale * math.log2(math.e)
    trans = (((1,), (1,)), ((), ()))

    def products(k, h):
        block = chip[0] ^ k
        both = q_ref[block, :, 2 * h * hd : 2 * (h + 1) * hd]
        query = both[:, :hd]
        left = jnp.concatenate([jnp.zeros_like(query), query], axis=1)
        left = jnp.concatenate([left, both], axis=0)
        window = [table[block * WK + w] for w in range(WK)]
        low = 4 * h * hd
        scores, tans = [], []
        for index in window:
            keys = kv[index, :, :, low : low + 2 * hd].reshape(BQ, 2 * hd)
            product = lax.dot_general(left, keys, trans, preferred_element_type=jnp.float32)
            scores.append(product[:tokens])
            tans.append(product[tokens:])
        return window, scores, tans

    def finish(k, h, window, scores, tans):
        top = functools.reduce(jnp.maximum, scores)
        top = jnp.max(top, axis=1, keepdims=True) * factor
        probs = [jnp.exp2(s * factor - top) for s in scores]
        weighted = [p * t for p, t in zip(probs, tans)]
        total = jnp.sum(functools.reduce(jnp.add, probs), axis=1, keepdims=True)
        mean = jnp.sum(functools.reduce(jnp.add, weighted), axis=1, keepdims=True)
        low = (4 * h + 2) * hd
        mixed = jnp.zeros((2 * tokens, 2 * hd), jnp.float32)
        for index, p, w in zip(window, probs, weighted):
            vals = kv[index, :, :, low : low + 2 * hd].reshape(BQ, 2 * hd)
            right = jnp.concatenate([p.astype(jnp.bfloat16), w.astype(jnp.bfloat16)], axis=0)
            mixed += jnp.dot(right, vals, preferred_element_type=jnp.float32)
        inverse = 1.0 / total
        out = mixed[:tokens, :hd] * inverse
        tan = (mixed[:tokens, hd:] + scale * mixed[tokens:, :hd]) * inverse
        tan = tan - (scale * mean * inverse) * out
        for (slot, row), ref in zip(places, outs):
            if slot == k:
                rows = slice(row, row + ref.shape[0])
                ref[:, 2 * h * hd : (2 * h + 1) * hd] = out[rows].astype(jnp.bfloat16)
                ref[:, (2 * h + 1) * hd : 2 * (h + 1) * hd] = tan[rows].astype(jnp.bfloat16)

    units = [(k, h) for h in range(PAIR) for k in dict(places)]
    arrive(0)
    ahead = products(*units[0])
    arrive(1)
    for unit, following in zip(units, units[1:] + [None]):
        current = ahead
        if following is not None:
            if following[1] > unit[1]:
                arrive(2)
                arrive(3)
            ahead = products(*following)
        finish(*unit, *current)


def attend(chip, table, queries, mine, other, later, places):
    _, tokens, width = queries.shape
    hd, sources = width // (2 * PAIR), len(mine)
    total = sum(a.shape[0] for a in mine)
    elements = len(dict(places)) * BQ * WK * BQ
    ends = [following[1] or tokens for following in places[1:]] + [tokens]
    sizes = [end - row for (_, row), end in zip(places, ends)]
    return pl.pallas_call(
        functools.partial(
            attend_kernel, sources=sources, later=len(later), places=places, hd=hd
        ),
        in_specs=[SMEM, SMEM, VMEM] + [ANY] * (PAIR * sources + len(later)),
        out_specs=[VMEM] * len(places),
        out_shape=[jax.ShapeDtypeStruct((size, width), jnp.bfloat16) for size in sizes],
        scratch_shapes=[
            pltpu.VMEM((total, PAIR, tokens, 2 * width), jnp.bfloat16),
            pltpu.SemaphoreType.DMA((2 * PAIR, PAIR * sources)),
        ],
        compiler_params=PARAMS,
        cost_estimate=pl.CostEstimate(
            flops=12 * elements * hd,
            bytes_accessed=8 * total * tokens * width,
            transcendentals=elements,
        ),
    )(chip, table, queries, *mine, *other, *later)


def locate(neighbors, frame, blocks):
    local = neighbors - frame * blocks
    even = frame % 2 == 0
    before = blocks + jnp.where(even, HB, 0) + local + HB
    after = blocks + jnp.where(even, 0, HB) + local - blocks
    return jnp.where(local < 0, before, jnp.where(local >= blocks, after, local)).reshape(-1)


def per_device(query, keys, values, query_tan, keys_tan, values_tan, neighbors):
    devices, frames = lax.axis_size("heads"), lax.axis_size("frames")
    frame = lax.axis_index("frames")
    chip = (lax.axis_index("heads") // PAIR).reshape(1).astype(jnp.int32)
    blocks = neighbors.shape[0]
    swap = [(d, d ^ 1) for d in range(devices)]
    (kv_sent,) = to_chips([keys_tan, keys, values, values_tan], devices)
    q_sent, zero = to_chips([query, query_tan], devices, [kv_sent])
    kv = exchange(kv_sent, devices)

    mine = [kv]
    for first in (0, 1):
        pairs = [(i, i + 1) for i in range(first, frames - 1, 2)]
        if pairs:
            start = jnp.where(frame % 2 == first, blocks - HB, 0) + zero[0]
            edge = lax.dynamic_slice_in_dim(kv, start, HB, axis=0)
            mine.append(lax.ppermute(edge, "frames", pairs + [(j, i) for i, j in pairs]))
    other = [lax.ppermute(a, "heads", swap) for a in mine]

    queries = exchange(q_sent, devices)
    table = locate(neighbors, frame, blocks)
    half, middle = blocks // 2, blocks // 2 + blocks // 4
    calls = [
        [(half, 0), (half, LEAD), *((k, 0) for k in range(half + 1, middle))],
        [(k, 0) for k in (*range(middle, blocks), *range(1, half), 0)],
    ]
    back, later = {}, []
    for places in calls:
        pieces = attend(chip, table, queries, mine, other, later, places)
        for place, piece in zip(places, pieces):
            pairs = [(d, d ^ (place[0] * PAIR)) for d in range(devices)]
            back[place] = lax.ppermute(piece, "heads", pairs) if place[0] else piece
        later = [back[places[0]]]
    return unpack(chip, back, *query.shape, 2)


def solution(mesh):
    own = P(("frames", "heads"), None)
    return jax.shard_map(
        per_device,
        mesh=mesh,
        in_specs=(own,) * 6 + (P("frames", None),),
        out_specs=(own, own),
        check_vma=False,
    )
```

```python
import functools
import math

import jax
import jax.numpy as jnp
from jax import lax
from jax.experimental import pallas as pl
from jax.experimental.pallas import tpu as pltpu
from jax.sharding import PartitionSpec as P

BQ = 256
WK = 4
HB = 4
PAIR = 2
LEAD = 16
PARAMS = pltpu.CompilerParams(vmem_limit_bytes=32 * 1024 * 1024)
ANY = pl.BlockSpec(memory_space=pl.ANY)
HBM = pl.BlockSpec(memory_space=pltpu.HBM)
VMEM = pl.BlockSpec(memory_space=pltpu.VMEM)
SMEM = pl.BlockSpec(memory_space=pltpu.SMEM)


def pin(*arrays):
    return [pltpu.with_memory_space_constraint(a, pltpu.HBM) for a in arrays]


def moves(size):
    return pl.CostEstimate(flops=0, bytes_accessed=size, transcendentals=0)


def pack_kernel(*refs, count, before, chunks):
    arrays, out = refs[:count], refs[count + before]
    held, staged, sems, out_sems = refs[-4:]
    if before:
        refs[count + before + 1][0] = 0
    chips, columns = out.shape[0], held.shape[2]
    hd, some, step = columns // chips // PAIR, chips // chunks, columns // chunks
    copies = {}
    for c in range(chunks):
        lanes = pl.ds(c * step, step)
        for a, array in enumerate(arrays):
            copies[c, a] = pltpu.make_async_copy(
                array.at[:, lanes], held.at[a, :, lanes], sems.at[c, a]
            )
            copies[c, a].start()
    sends = []
    for c in range(chunks):
        for a in range(count):
            copies[c, a].wait()
        for chip in range(c * some, (c + 1) * some):
            for h in range(PAIR):
                source = (chip * PAIR + h) * hd
                for a in range(count):
                    target = (h * count + a) * hd
                    staged[chip, :, target : target + hd] = held[a, :, source : source + hd]
        part = pl.ds(c * some, some)
        sends.append(pltpu.make_async_copy(staged.at[part], out.at[part], out_sems.at[c]))
        sends[-1].start()
    for send in sends:
        send.wait()


def to_chips(arrays, devices, before=(), chunks=4):
    tokens, columns = arrays[0].shape
    count, chips = len(arrays), devices // PAIR
    shape = (chips, tokens, count * columns // chips)
    more = min(len(before), 1)
    return pl.pallas_call(
        functools.partial(pack_kernel, count=count, before=len(before), chunks=chunks),
        in_specs=[HBM] * (count + len(before)),
        out_specs=[HBM] + [SMEM] * more,
        out_shape=[pltpu.HBM(shape, jnp.bfloat16)]
        + [jax.ShapeDtypeStruct((1,), jnp.int32)] * more,
        scratch_shapes=[
            pltpu.VMEM((count, tokens, columns), jnp.bfloat16),
            pltpu.VMEM(shape, jnp.bfloat16),
            pltpu.SemaphoreType.DMA((chunks, count)),
            pltpu.SemaphoreType.DMA((chunks,)),
        ],
        compiler_params=PARAMS,
        cost_estimate=moves(4 * count * tokens * columns),
    )(*pin(*arrays, *before))


def exchange(pieces, devices):
    groups = [list(range(core, devices, PAIR)) for core in range(PAIR)]
    return lax.all_to_all(
        pieces, "heads", split_axis=0, concat_axis=0, axis_index_groups=groups, tiled=True
    )


def unpack_kernel(chip, *refs, order):
    pieces, arrays = refs[: len(order)], refs[len(order) :]
    hd = pieces[0].shape[1] // len(arrays) // PAIR
    for k, piece in zip(order, pieces):
        for h in range(PAIR):
            columns = pl.ds(pl.multiple_of(((chip[0] ^ k) * PAIR + h) * hd, hd), hd)
            for a, array in enumerate(arrays):
                source = (h * len(arrays) + a) * hd
                array[:, columns] = piece[:, source : source + hd]


def unpack(chip, pieces, count):
    tokens, width = pieces[0].shape
    columns = len(pieces) * width // count
    return pl.pallas_call(
        functools.partial(unpack_kernel, order=list(pieces)),
        in_specs=[SMEM] + [VMEM] * len(pieces),
        out_specs=[VMEM] * count,
        out_shape=[jax.ShapeDtypeStruct((tokens, columns), jnp.bfloat16)] * count,
        compiler_params=PARAMS,
        cost_estimate=moves(4 * len(pieces) * tokens * width),
    )(chip, *pieces.values())


def join_kernel(*refs, sources):
    parts, kv, sems = refs[: PAIR * sources], refs[-2], refs[-1]
    copies = []
    for core in range(PAIR):
        row = 0
        for i in range(sources):
            n = core * sources + i
            target = kv.at[pl.ds(row, parts[n].shape[0]), core]
            copies.append(pltpu.make_async_copy(parts[n], target, sems.at[n]))
            row += parts[n].shape[0]
    for copy in copies:
        copy.start()
    for copy in copies:
        copy.wait()


def join(mine, other):
    _, tokens, width = mine[0].shape
    shape = (sum(a.shape[0] for a in mine), PAIR, tokens, width)
    return pl.pallas_call(
        functools.partial(join_kernel, sources=len(mine)),
        in_specs=[ANY] * (PAIR * len(mine)),
        out_specs=VMEM,
        out_shape=jax.ShapeDtypeStruct(shape, jnp.bfloat16),
        scratch_shapes=[pltpu.SemaphoreType.DMA((PAIR * len(mine),))],
        compiler_params=PARAMS,
        cost_estimate=moves(8 * shape[0] * PAIR * tokens * width),
    )(*mine, *other)


def attend_kernel(chip, table, q_ref, kv, *refs, later, places, token, hd):
    outs = refs[later:]
    tokens = q_ref.shape[1]
    scale = hd ** (-0.5)
    factor = scale * math.log2(math.e)
    trans = (((1,), (1,)), ((), ()))

    def products(k, h):
        block = chip[0] ^ k
        both = q_ref[block, :, 2 * h * hd : 2 * (h + 1) * hd]
        query = both[:, :hd]
        left = jnp.concatenate([jnp.zeros_like(query), query], axis=1)
        left = jnp.concatenate([left, both], axis=0)
        window = [table[block * WK + w] for w in range(WK)]
        low = 4 * h * hd
        scores, tans = [], []
        for index in window:
            keys = kv[index, :, :, low : low + 2 * hd].reshape(BQ, 2 * hd)
            product = lax.dot_general(left, keys, trans, preferred_element_type=jnp.float32)
            scores.append(product[:tokens])
            tans.append(product[tokens:])
        return window, scores, tans

    def finish(k, h, window, scores, tans):
        top = functools.reduce(jnp.maximum, scores)
        top = jnp.max(top, axis=1, keepdims=True) * factor
        probs = [jnp.exp2(s * factor - top) for s in scores]
        weighted = [p * t for p, t in zip(probs, tans)]
        total = jnp.sum(functools.reduce(jnp.add, probs), axis=1, keepdims=True)
        mean = jnp.sum(functools.reduce(jnp.add, weighted), axis=1, keepdims=True)
        low = (4 * h + 2) * hd
        mixed = jnp.zeros((2 * tokens, 2 * hd), jnp.float32)
        for index, p, w in zip(window, probs, weighted):
            vals = kv[index, :, :, low : low + 2 * hd].reshape(BQ, 2 * hd)
            right = jnp.concatenate([p.astype(jnp.bfloat16), w.astype(jnp.bfloat16)], axis=0)
            mixed += jnp.dot(right, vals, preferred_element_type=jnp.float32)
        inverse = 1.0 / total
        out = mixed[:tokens, :hd] * inverse
        tan = (mixed[:tokens, hd:] + scale * mixed[tokens:, :hd]) * inverse
        tan = tan - (scale * mean * inverse) * out
        ref = outs[places.index(k)]
        ref[:, 2 * h * hd : (2 * h + 1) * hd] = out.astype(jnp.bfloat16)
        ref[:, (2 * h + 1) * hd : 2 * (h + 1) * hd] = tan.astype(jnp.bfloat16)

    units = [(k, h) for k in places for h in range(PAIR)]
    ahead = products(*units[0])
    for unit, following in zip(units, units[1:] + [None]):
        current = ahead
        if following is not None:
            ahead = products(*following)
        finish(*unit, *current)
    if token:
        outs[-1][...] = outs[0][:LEAD]


def attend(chip, table, queries, kv, later, places, token):
    _, tokens, width = queries.shape
    hd = width // (2 * PAIR)
    elements = len(places) * BQ * WK * BQ
    sizes = [tokens] * len(places) + [LEAD] * token
    return pl.pallas_call(
        functools.partial(
            attend_kernel, later=len(later), places=places, token=token, hd=hd
        ),
        in_specs=[SMEM, SMEM, VMEM, VMEM] + [ANY] * len(later),
        out_specs=[VMEM] * len(sizes),
        out_shape=[jax.ShapeDtypeStruct((size, width), jnp.bfloat16) for size in sizes],
        compiler_params=PARAMS,
        cost_estimate=pl.CostEstimate(
            flops=12 * elements * hd,
            bytes_accessed=2 * kv.size,
            transcendentals=elements,
        ),
    )(chip, table, queries, kv, *later)


def locate(neighbors, frame, blocks):
    local = neighbors - frame * blocks
    even = frame % 2 == 0
    before = blocks + jnp.where(even, HB, 0) + local + HB
    after = blocks + jnp.where(even, 0, HB) + local - blocks
    return jnp.where(local < 0, before, jnp.where(local >= blocks, after, local)).reshape(-1)


def per_device(query, keys, values, query_tan, keys_tan, values_tan, neighbors):
    devices, frames = lax.axis_size("heads"), lax.axis_size("frames")
    frame = lax.axis_index("frames")
    chip = (lax.axis_index("heads") // PAIR).reshape(1).astype(jnp.int32)
    blocks = neighbors.shape[0]
    swap = [(d, d ^ 1) for d in range(devices)]
    (kv_sent,) = to_chips([keys_tan, keys, values, values_tan], devices)
    q_sent, zero = to_chips([query, query_tan], devices, [kv_sent])
    kv = exchange(kv_sent, devices)

    mine = [kv]
    for first in (0, 1):
        pairs = [(i, i + 1) for i in range(first, frames - 1, 2)]
        if pairs:
            start = jnp.where(frame % 2 == first, blocks - HB, 0) + zero[0]
            edge = lax.dynamic_slice_in_dim(kv, start, HB, axis=0)
            mine.append(lax.ppermute(edge, "frames", pairs + [(j, i) for i, j in pairs]))
    other = [lax.ppermute(a, "heads", swap) for a in mine]

    queries = exchange(q_sent, devices)
    table = locate(neighbors, frame, blocks)
    half, middle = blocks // 2, blocks // 2 + blocks // 4
    kv = join(mine, other)
    back, later = {}, []
    for part in (range(half, middle), [*range(middle, blocks), *range(1, half), 0]):
        pieces = attend(chip, table, queries, kv, later, list(part), not later)
        for k, piece in zip(part, pieces):
            pairs = [(d, d ^ (k * PAIR)) for d in range(devices)]
            back[k] = lax.ppermute(piece, "heads", pairs) if k else piece
        later = [lax.ppermute(pieces[-1], "heads", swap)] if not later else later
    return unpack(chip, back, 2)


def solution(mesh):
    own = P(("frames", "heads"), None)
    return jax.shard_map(
        per_device,
        mesh=mesh,
        in_specs=(own,) * 6 + (P("frames", None),),
        out_specs=(own, own),
        check_vma=False,
    )
```

```python
import functools
import math

import jax
import jax.numpy as jnp
from jax import lax
from jax.experimental import pallas as pl
from jax.experimental.pallas import tpu as pltpu
from jax.sharding import PartitionSpec as P

BQ = 256
WK = 4
HB = 4
PAIR = 2
PARAMS = pltpu.CompilerParams(vmem_limit_bytes=32 * 1024 * 1024)
ANY = pl.BlockSpec(memory_space=pl.ANY)
HBM = pl.BlockSpec(memory_space=pltpu.HBM)
VMEM = pl.BlockSpec(memory_space=pltpu.VMEM)
SMEM = pl.BlockSpec(memory_space=pltpu.SMEM)


def pin(*arrays):
    return [pltpu.with_memory_space_constraint(a, pltpu.HBM) for a in arrays]


def moves(size):
    return pl.CostEstimate(flops=0, bytes_accessed=size, transcendentals=0)


def pack_kernel(*refs, count, before, chunks):
    arrays, out = refs[:count], refs[count + before]
    held, staged, sems, out_sems = refs[-4:]
    if before:
        refs[count + before + 1][0] = 0
    chips, columns = out.shape[0], held.shape[2]
    hd, some, step = columns // chips // PAIR, chips // chunks, columns // chunks
    copies = {}
    for c in range(chunks):
        lanes = pl.ds(c * step, step)
        for a, array in enumerate(arrays):
            copies[c, a] = pltpu.make_async_copy(
                array.at[:, lanes], held.at[a, :, lanes], sems.at[c, a]
            )
            copies[c, a].start()
    sends = []
    for c in range(chunks):
        for a in range(count):
            copies[c, a].wait()
        for chip in range(c * some, (c + 1) * some):
            for h in range(PAIR):
                source = (chip * PAIR + h) * hd
                for a in range(count):
                    target = (h * count + a) * hd
                    staged[chip, :, target : target + hd] = held[a, :, source : source + hd]
        part = pl.ds(c * some, some)
        sends.append(pltpu.make_async_copy(staged.at[part], out.at[part], out_sems.at[c]))
        sends[-1].start()
    for send in sends:
        send.wait()


def to_chips(arrays, devices, before=(), chunks=4):
    tokens, columns = arrays[0].shape
    count, chips = len(arrays), devices // PAIR
    shape = (chips, tokens, count * columns // chips)
    more = min(len(before), 1)
    return pl.pallas_call(
        functools.partial(pack_kernel, count=count, before=len(before), chunks=chunks),
        in_specs=[HBM] * (count + len(before)),
        out_specs=[HBM] + [SMEM] * more,
        out_shape=[pltpu.HBM(shape, jnp.bfloat16)]
        + [jax.ShapeDtypeStruct((1,), jnp.int32)] * more,
        scratch_shapes=[
            pltpu.VMEM((count, tokens, columns), jnp.bfloat16),
            pltpu.VMEM(shape, jnp.bfloat16),
            pltpu.SemaphoreType.DMA((chunks, count)),
            pltpu.SemaphoreType.DMA((chunks,)),
        ],
        compiler_params=PARAMS,
        cost_estimate=moves(4 * count * tokens * columns),
    )(*pin(*arrays, *before))


def exchange(pieces, devices):
    groups = [list(range(core, devices, PAIR)) for core in range(PAIR)]
    return lax.all_to_all(
        pieces, "heads", split_axis=0, concat_axis=0, axis_index_groups=groups, tiled=True
    )


def unpack_kernel(chip, *refs, order):
    pieces, arrays = refs[: len(order)], refs[len(order) :]
    hd = pieces[0].shape[1] // len(arrays) // PAIR
    for k, piece in zip(order, pieces):
        for h in range(PAIR):
            columns = pl.ds(pl.multiple_of(((chip[0] ^ k) * PAIR + h) * hd, hd), hd)
            for a, array in enumerate(arrays):
                source = (h * len(arrays) + a) * hd
                array[:, columns] = piece[:, source : source + hd]


def unpack(chip, pieces, count):
    tokens, width = pieces[0].shape
    columns = len(pieces) * width // count
    return pl.pallas_call(
        functools.partial(unpack_kernel, order=list(pieces)),
        in_specs=[SMEM] + [VMEM] * len(pieces),
        out_specs=[VMEM] * count,
        out_shape=[jax.ShapeDtypeStruct((tokens, columns), jnp.bfloat16)] * count,
        compiler_params=PARAMS,
        cost_estimate=moves(4 * len(pieces) * tokens * width),
    )(chip, *pieces.values())


def attend_kernel(chip, table, q_ref, *refs, sources, later, places, hd):
    tokens = q_ref.shape[1]
    if sources:
        parts, sems, kv = refs[: PAIR * sources], refs[-1], refs[-2]
        outs = refs[PAIR * sources + later : -2]
    else:
        kv, outs = refs[0], refs[1 + later :]
    groups = []
    for g in range(2 * PAIR if sources else 0):
        lanes, copies = pl.ds(g * 2 * hd, 2 * hd), []
        for n, ref in enumerate(parts):
            core, row = n // sources, 0 if n % sources == 0 else parts[0].shape[0]
            row += max(n % sources - 1, 0) * HB
            target = kv.at[pl.ds(row, ref.shape[0]), core, :, lanes]
            copies.append(pltpu.make_async_copy(ref.at[:, :, lanes], target, sems.at[g, n]))
        groups.append(copies)

    def start(*group):
        for g in group:
            for copy in groups[g] if sources else []:
                copy.start()

    def wait(*group):
        for g in group:
            for copy in groups[g] if sources else []:
                copy.wait()

    scale = hd ** (-0.5)
    factor = scale * math.log2(math.e)
    trans = (((1,), (1,)), ((), ()))

    def products(k, h):
        block = chip[0] ^ k
        both = q_ref[block, :, 2 * h * hd : 2 * (h + 1) * hd]
        query = both[:, :hd]
        left = jnp.concatenate([jnp.zeros_like(query), query], axis=1)
        left = jnp.concatenate([left, both], axis=0)
        window = [table[block * WK + w] for w in range(WK)]
        low = 4 * h * hd
        scores, tans = [], []
        for index in window:
            keys = kv[index, :, :, low : low + 2 * hd].reshape(BQ, 2 * hd)
            product = lax.dot_general(left, keys, trans, preferred_element_type=jnp.float32)
            scores.append(product[:tokens])
            tans.append(product[tokens:])
        return window, scores, tans

    def finish(k, h, window, scores, tans):
        top = functools.reduce(jnp.maximum, scores)
        top = jnp.max(top, axis=1, keepdims=True) * factor
        probs = [jnp.exp2(s * factor - top) for s in scores]
        weighted = [p * t for p, t in zip(probs, tans)]
        total = jnp.sum(functools.reduce(jnp.add, probs), axis=1, keepdims=True)
        mean = jnp.sum(functools.reduce(jnp.add, weighted), axis=1, keepdims=True)
        low = (4 * h + 2) * hd
        mixed = jnp.zeros((2 * tokens, 2 * hd), jnp.float32)
        for index, p, w in zip(window, probs, weighted):
            vals = kv[index, :, :, low : low + 2 * hd].reshape(BQ, 2 * hd)
            right = jnp.concatenate([p.astype(jnp.bfloat16), w.astype(jnp.bfloat16)], axis=0)
            mixed += jnp.dot(right, vals, preferred_element_type=jnp.float32)
        inverse = 1.0 / total
        out = mixed[:tokens, :hd] * inverse
        tan = (mixed[:tokens, hd:] + scale * mixed[tokens:, :hd]) * inverse
        tan = tan - (scale * mean * inverse) * out
        ref = outs[places.index(k)]
        ref[:, 2 * h * hd : (2 * h + 1) * hd] = out.astype(jnp.bfloat16)
        ref[:, (2 * h + 1) * hd : 2 * (h + 1) * hd] = tan.astype(jnp.bfloat16)

    units = [(k, h) for h in range(PAIR) for k in places]
    start(0)
    wait(0)
    start(1, 2, 3)
    ahead = products(*units[0])
    wait(1)
    for unit, following in zip(units, units[1:] + [None]):
        current = ahead
        if following is not None:
            if following[1] > unit[1]:
                wait(2, 3)
            ahead = products(*following)
        finish(*unit, *current)


def attend(chip, table, queries, sources, later, places):
    _, tokens, width = queries.shape
    hd, joins = width // (2 * PAIR), len(sources) > 1
    elements = len(places) * BQ * WK * BQ
    outs = [jax.ShapeDtypeStruct((tokens, width), jnp.bfloat16)] * len(places)
    scratch, total = [], 0
    if joins:
        total = sum(a.shape[0] for a in sources) // PAIR
        outs.append(jax.ShapeDtypeStruct((total, PAIR, tokens, 2 * width), jnp.bfloat16))
        scratch.append(pltpu.SemaphoreType.DMA((2 * PAIR, len(sources))))
    return pl.pallas_call(
        functools.partial(
            attend_kernel,
            sources=len(sources) // PAIR if joins else 0,
            later=len(later),
            places=places,
            hd=hd,
        ),
        in_specs=[SMEM, SMEM, VMEM]
        + [ANY if joins else VMEM] * len(sources)
        + [ANY] * len(later),
        out_specs=[VMEM] * len(outs),
        out_shape=outs,
        scratch_shapes=scratch,
        compiler_params=PARAMS,
        cost_estimate=pl.CostEstimate(
            flops=12 * elements * hd,
            bytes_accessed=8 * total * tokens * width,
            transcendentals=elements,
        ),
    )(chip, table, queries, *sources, *later)


def locate(neighbors, frame, blocks):
    local = neighbors - frame * blocks
    even = frame % 2 == 0
    before = blocks + jnp.where(even, HB, 0) + local + HB
    after = blocks + jnp.where(even, 0, HB) + local - blocks
    return jnp.where(local < 0, before, jnp.where(local >= blocks, after, local)).reshape(-1)


def per_device(query, keys, values, query_tan, keys_tan, values_tan, neighbors):
    devices, frames = lax.axis_size("heads"), lax.axis_size("frames")
    frame = lax.axis_index("frames")
    chip = (lax.axis_index("heads") // PAIR).reshape(1).astype(jnp.int32)
    blocks = neighbors.shape[0]
    swap = [(d, d ^ 1) for d in range(devices)]
    (kv_sent,) = to_chips([keys_tan, keys, values, values_tan], devices)
    q_sent, zero = to_chips([query, query_tan], devices, [kv_sent])
    kv = exchange(kv_sent, devices)

    mine = [kv]
    for first in (0, 1):
        pairs = [(i, i + 1) for i in range(first, frames - 1, 2)]
        if pairs:
            start = jnp.where(frame % 2 == first, blocks - HB, 0) + zero[0]
            edge = lax.dynamic_slice_in_dim(kv, start, HB, axis=0)
            mine.append(lax.ppermute(edge, "frames", pairs + [(j, i) for i, j in pairs]))
    other = [lax.ppermute(a, "heads", swap) for a in mine]

    queries = exchange(q_sent, devices)
    table = locate(neighbors, frame, blocks)
    half, middle = blocks // 2, blocks // 2 + blocks // 4
    back, later, sources = {}, [], mine + other
    for part in ([*range(half, middle), 1], [*range(middle, blocks), *range(2, half), 0]):
        pieces = attend(chip, table, queries, sources, later, part)
        for k, piece in zip(part, pieces):
            pairs = [(d, d ^ (k * PAIR)) for d in range(devices)]
            back[k] = lax.ppermute(piece, "heads", pairs) if k else piece
        later, sources = [back[1]], pieces[len(part) :]
    return unpack(chip, back, 2)


def solution(mesh):
    own = P(("frames", "heads"), None)
    return jax.shard_map(
        per_device,
        mesh=mesh,
        in_specs=(own,) * 6 + (P("frames", None),),
        out_specs=(own, own),
        check_vma=False,
    )
```

```python
import functools
import math

import jax
import jax.numpy as jnp
from jax import lax
from jax.experimental import pallas as pl
from jax.experimental.pallas import tpu as pltpu
from jax.sharding import PartitionSpec as P

BQ = 256
WK = 4
HB = 4
PAIR = 2
PARAMS = pltpu.CompilerParams(vmem_limit_bytes=32 * 1024 * 1024)
ANY = pl.BlockSpec(memory_space=pl.ANY)
HBM = pl.BlockSpec(memory_space=pltpu.HBM)
VMEM = pl.BlockSpec(memory_space=pltpu.VMEM)
SMEM = pl.BlockSpec(memory_space=pltpu.SMEM)


def pin(*arrays):
    return [pltpu.with_memory_space_constraint(a, pltpu.HBM) for a in arrays]


def moves(size):
    return pl.CostEstimate(flops=0, bytes_accessed=size, transcendentals=0)


def pack_kernel(*refs, count, before, chunks):
    arrays, out = refs[:count], refs[count + before]
    held, staged, sems, out_sems = refs[-4:]
    if before:
        refs[count + before + 1][0] = 0
    chips, columns = out.shape[0], held.shape[2]
    hd, some, step = columns // chips // PAIR, chips // chunks, columns // chunks
    copies = {}
    for c in range(chunks):
        lanes = pl.ds(c * step, step)
        for a, array in enumerate(arrays):
            copies[c, a] = pltpu.make_async_copy(
                array.at[:, lanes], held.at[a, :, lanes], sems.at[c, a]
            )
            copies[c, a].start()
    sends = []
    for c in range(chunks):
        for a in range(count):
            copies[c, a].wait()
        for chip in range(c * some, (c + 1) * some):
            for h in range(PAIR):
                source = (chip * PAIR + h) * hd
                for a in range(count):
                    group, target = h * (count // 2) + a // 2, a % 2 * hd
                    staged[chip, group, :, target : target + hd] = held[
                        a, :, source : source + hd
                    ]
        part = pl.ds(c * some, some)
        sends.append(pltpu.make_async_copy(staged.at[part], out.at[part], out_sems.at[c]))
        sends[-1].start()
    for send in sends:
        send.wait()


def to_chips(arrays, devices, before=(), chunks=4):
    tokens, columns = arrays[0].shape
    count, chips, hd = len(arrays), devices // PAIR, columns // devices
    shape = (chips, PAIR * count // 2, tokens, 2 * hd)
    more = min(len(before), 1)
    return pl.pallas_call(
        functools.partial(pack_kernel, count=count, before=len(before), chunks=chunks),
        in_specs=[HBM] * (count + len(before)),
        out_specs=[HBM] + [SMEM] * more,
        out_shape=[pltpu.HBM(shape, jnp.bfloat16)]
        + [jax.ShapeDtypeStruct((1,), jnp.int32)] * more,
        scratch_shapes=[
            pltpu.VMEM((count, tokens, columns), jnp.bfloat16),
            pltpu.VMEM(shape, jnp.bfloat16),
            pltpu.SemaphoreType.DMA((chunks, count)),
            pltpu.SemaphoreType.DMA((chunks,)),
        ],
        compiler_params=PARAMS,
        cost_estimate=moves(4 * count * tokens * columns),
    )(*pin(*arrays, *before))


def exchange(pieces, devices):
    groups = [list(range(core, devices, PAIR)) for core in range(PAIR)]
    return lax.all_to_all(
        pieces, "heads", split_axis=0, concat_axis=0, axis_index_groups=groups, tiled=True
    )


def unpack_kernel(chip, *refs, order):
    pieces, arrays = refs[: len(order)], refs[len(order) :]
    hd = pieces[0].shape[1] // len(arrays) // PAIR
    for k, piece in zip(order, pieces):
        for h in range(PAIR):
            columns = pl.ds(pl.multiple_of(((chip[0] ^ k) * PAIR + h) * hd, hd), hd)
            for a, array in enumerate(arrays):
                source = (h * len(arrays) + a) * hd
                array[:, columns] = piece[:, source : source + hd]


def unpack(chip, pieces, count):
    tokens, width = pieces[0].shape
    columns = len(pieces) * width // count
    return pl.pallas_call(
        functools.partial(unpack_kernel, order=list(pieces)),
        in_specs=[SMEM] + [VMEM] * len(pieces),
        out_specs=[VMEM] * count,
        out_shape=[jax.ShapeDtypeStruct((tokens, columns), jnp.bfloat16)] * count,
        compiler_params=PARAMS,
        cost_estimate=moves(4 * len(pieces) * tokens * width),
    )(chip, *pieces.values())


def attend_kernel(chip, table, q_ref, *refs, sources, later, places, hd):
    tokens = q_ref.shape[2]
    if sources:
        parts, sems, kv = refs[: PAIR * sources], refs[-1], refs[-2]
        outs = refs[PAIR * sources + later : -2]
    else:
        kv, outs = refs[0], refs[1 + later :]
    groups = []
    for g in range(2 * PAIR if sources else 0):
        copies = []
        for n, ref in enumerate(parts):
            core, row = n // sources, 0 if n % sources == 0 else parts[0].shape[0]
            row += max(n % sources - 1, 0) * HB
            target = kv.at[pl.ds(row, ref.shape[0]), core, g]
            copies.append(pltpu.make_async_copy(ref.at[:, g], target, sems.at[g, n]))
        groups.append(copies)

    def start(*group):
        for g in group:
            for copy in groups[g] if sources else []:
                copy.start()

    def wait(*group):
        for g in group:
            for copy in groups[g] if sources else []:
                copy.wait()

    scale = hd ** (-0.5)
    factor = scale * math.log2(math.e)
    trans = (((1,), (1,)), ((), ()))

    def products(k, h):
        block = chip[0] ^ k
        both = q_ref[block, h]
        query = both[:, :hd]
        left = jnp.concatenate([jnp.zeros_like(query), query], axis=1)
        left = jnp.concatenate([left, both], axis=0)
        window = [table[block * WK + w] for w in range(WK)]
        scores, tans = [], []
        for index in window:
            keys = kv[index, :, 2 * h].reshape(BQ, 2 * hd)
            product = lax.dot_general(left, keys, trans, preferred_element_type=jnp.float32)
            scores.append(product[:tokens])
            tans.append(product[tokens:])
        return window, scores, tans

    def finish(k, h, window, scores, tans):
        top = functools.reduce(jnp.maximum, scores)
        top = jnp.max(top, axis=1, keepdims=True) * factor
        probs = [jnp.exp2(s * factor - top) for s in scores]
        weighted = [p * t for p, t in zip(probs, tans)]
        total = jnp.sum(functools.reduce(jnp.add, probs), axis=1, keepdims=True)
        mean = jnp.sum(functools.reduce(jnp.add, weighted), axis=1, keepdims=True)
        mixed = jnp.zeros((2 * tokens, 2 * hd), jnp.float32)
        for index, p, w in zip(window, probs, weighted):
            vals = kv[index, :, 2 * h + 1].reshape(BQ, 2 * hd)
            right = jnp.concatenate([p.astype(jnp.bfloat16), w.astype(jnp.bfloat16)], axis=0)
            mixed += jnp.dot(right, vals, preferred_element_type=jnp.float32)
        inverse = 1.0 / total
        out = mixed[:tokens, :hd] * inverse
        tan = (mixed[:tokens, hd:] + scale * mixed[tokens:, :hd]) * inverse
        tan = tan - (scale * mean * inverse) * out
        ref = outs[places.index(k)]
        ref[:, 2 * h * hd : (2 * h + 1) * hd] = out.astype(jnp.bfloat16)
        ref[:, (2 * h + 1) * hd : 2 * (h + 1) * hd] = tan.astype(jnp.bfloat16)

    units = [(k, h) for h in range(PAIR) for k in places]
    start(0)
    wait(0)
    start(1, 2, 3)
    ahead = products(*units[0])
    wait(1)
    for unit, following in zip(units, units[1:] + [None]):
        current = ahead
        if following is not None:
            if following[1] > unit[1]:
                wait(2, 3)
            ahead = products(*following)
        finish(*unit, *current)


def attend(chip, table, queries, sources, later, places):
    _, _, tokens, pair = queries.shape
    hd, joins, width = pair // 2, len(sources) > 1, PAIR * pair
    elements = len(places) * BQ * WK * BQ
    outs = [jax.ShapeDtypeStruct((tokens, width), jnp.bfloat16)] * len(places)
    scratch, total = [], 0
    if joins:
        total = sum(a.shape[0] for a in sources) // PAIR
        outs.append(jax.ShapeDtypeStruct((total, PAIR, 2 * PAIR, tokens, pair), jnp.bfloat16))
        scratch.append(pltpu.SemaphoreType.DMA((2 * PAIR, len(sources))))
    return pl.pallas_call(
        functools.partial(
            attend_kernel,
            sources=len(sources) // PAIR if joins else 0,
            later=len(later),
            places=places,
            hd=hd,
        ),
        in_specs=[SMEM, SMEM, VMEM]
        + [ANY if joins else VMEM] * len(sources)
        + [ANY] * len(later),
        out_specs=[VMEM] * len(outs),
        out_shape=outs,
        scratch_shapes=scratch,
        compiler_params=PARAMS,
        cost_estimate=pl.CostEstimate(
            flops=12 * elements * hd,
            bytes_accessed=8 * total * tokens * width,
            transcendentals=elements,
        ),
    )(chip, table, queries, *sources, *later)


def locate(neighbors, frame, blocks):
    local = neighbors - frame * blocks
    even = frame % 2 == 0
    before = blocks + jnp.where(even, HB, 0) + local + HB
    after = blocks + jnp.where(even, 0, HB) + local - blocks
    return jnp.where(local < 0, before, jnp.where(local >= blocks, after, local)).reshape(-1)


def per_device(query, keys, values, query_tan, keys_tan, values_tan, neighbors):
    devices, frames = lax.axis_size("heads"), lax.axis_size("frames")
    frame = lax.axis_index("frames")
    chip = (lax.axis_index("heads") // PAIR).reshape(1).astype(jnp.int32)
    blocks = neighbors.shape[0]
    swap = [(d, d ^ 1) for d in range(devices)]
    (kv_sent,) = to_chips([keys_tan, keys, values, values_tan], devices)
    q_sent, zero = to_chips([query, query_tan], devices, [kv_sent])
    kv = exchange(kv_sent, devices)

    mine = [kv]
    for first in (0, 1):
        pairs = [(i, i + 1) for i in range(first, frames - 1, 2)]
        if pairs:
            start = jnp.where(frame % 2 == first, blocks - HB, 0) + zero[0]
            edge = lax.dynamic_slice_in_dim(kv, start, HB, axis=0)
            mine.append(lax.ppermute(edge, "frames", pairs + [(j, i) for i, j in pairs]))
    other = [lax.ppermute(a, "heads", swap) for a in mine]

    queries = exchange(q_sent, devices)
    table = locate(neighbors, frame, blocks)
    half, middle = blocks // 2, blocks // 2 + blocks // 4
    back, later, sources = {}, [], mine + other
    for part in ([*range(half, middle), 1], [*range(middle, blocks), *range(2, half), 0]):
        pieces = attend(chip, table, queries, sources, later, part)
        for k, piece in zip(part, pieces):
            pairs = [(d, d ^ (k * PAIR)) for d in range(devices)]
            back[k] = lax.ppermute(piece, "heads", pairs) if k else piece
        later, sources = [back[1]], pieces[len(part) :]
    return unpack(chip, back, 2)


def solution(mesh):
    own = P(("frames", "heads"), None)
    return jax.shard_map(
        per_device,
        mesh=mesh,
        in_specs=(own,) * 6 + (P("frames", None),),
        out_specs=(own, own),
        check_vma=False,
    )
```

```python
import functools
import math

import jax
import jax.numpy as jnp
from jax import lax
from jax.experimental import pallas as pl
from jax.experimental.pallas import tpu as pltpu
from jax.sharding import PartitionSpec as P

BQ = 256
WK = 4
HB = 4
PAIR = 2
PARAMS = pltpu.CompilerParams(vmem_limit_bytes=32 * 1024 * 1024)
ANY = pl.BlockSpec(memory_space=pl.ANY)
HBM = pl.BlockSpec(memory_space=pltpu.HBM)
VMEM = pl.BlockSpec(memory_space=pltpu.VMEM)
SMEM = pl.BlockSpec(memory_space=pltpu.SMEM)


def pin(*arrays):
    return [pltpu.with_memory_space_constraint(a, pltpu.HBM) for a in arrays]


def moves(size):
    return pl.CostEstimate(flops=0, bytes_accessed=size, transcendentals=0)


def pack_kernel(*refs, count, before, chunks):
    arrays, out = refs[:count], refs[count + before]
    held, staged, sems, out_sems = refs[-4:]
    if before:
        refs[count + before + 1][0] = 0
    chips, columns = out.shape[0], held.shape[2]
    hd, some, step = columns // chips // PAIR, chips // chunks, columns // chunks
    copies = {}
    for c in range(chunks):
        lanes = pl.ds(c * step, step)
        for a, array in enumerate(arrays):
            copies[c, a] = pltpu.make_async_copy(
                array.at[:, lanes], held.at[a, :, lanes], sems.at[c, a]
            )
            copies[c, a].start()
    sends = []
    for c in range(chunks):
        for a in range(count):
            copies[c, a].wait()
        for chip in range(c * some, (c + 1) * some):
            for h in range(PAIR):
                source = (chip * PAIR + h) * hd
                for a in range(count):
                    group, target = h * (count // 2) + a // 2, a % 2 * hd
                    staged[chip, group, :, target : target + hd] = held[
                        a, :, source : source + hd
                    ]
        part = pl.ds(c * some, some)
        sends.append(pltpu.make_async_copy(staged.at[part], out.at[part], out_sems.at[c]))
        sends[-1].start()
    for send in sends:
        send.wait()


def to_chips(arrays, devices, before=(), chunks=8):
    tokens, columns = arrays[0].shape
    count, chips, hd = len(arrays), devices // PAIR, columns // devices
    shape = (chips, PAIR * count // 2, tokens, 2 * hd)
    more = min(len(before), 1)
    return pl.pallas_call(
        functools.partial(pack_kernel, count=count, before=len(before), chunks=chunks),
        in_specs=[HBM] * (count + len(before)),
        out_specs=[HBM] + [SMEM] * more,
        out_shape=[pltpu.HBM(shape, jnp.bfloat16)]
        + [jax.ShapeDtypeStruct((1,), jnp.int32)] * more,
        scratch_shapes=[
            pltpu.VMEM((count, tokens, columns), jnp.bfloat16),
            pltpu.VMEM(shape, jnp.bfloat16),
            pltpu.SemaphoreType.DMA((chunks, count)),
            pltpu.SemaphoreType.DMA((chunks,)),
        ],
        compiler_params=PARAMS,
        cost_estimate=moves(4 * count * tokens * columns),
    )(*pin(*arrays, *before))


def exchange(pieces, devices):
    groups = [list(range(core, devices, PAIR)) for core in range(PAIR)]
    return lax.all_to_all(
        pieces, "heads", split_axis=0, concat_axis=0, axis_index_groups=groups, tiled=True
    )


def unpack_kernel(chip, *refs, order):
    pieces, arrays = refs[: len(order)], refs[len(order) :]
    hd = pieces[0].shape[1] // len(arrays) // PAIR
    for k, piece in zip(order, pieces):
        for h in range(PAIR):
            columns = pl.ds(pl.multiple_of(((chip[0] ^ k) * PAIR + h) * hd, hd), hd)
            for a, array in enumerate(arrays):
                source = (h * len(arrays) + a) * hd
                array[:, columns] = piece[:, source : source + hd]


def unpack(chip, pieces, count):
    tokens, width = pieces[0].shape
    columns = len(pieces) * width // count
    return pl.pallas_call(
        functools.partial(unpack_kernel, order=list(pieces)),
        in_specs=[SMEM] + [VMEM] * len(pieces),
        out_specs=[VMEM] * count,
        out_shape=[jax.ShapeDtypeStruct((tokens, columns), jnp.bfloat16)] * count,
        compiler_params=PARAMS,
        cost_estimate=moves(4 * len(pieces) * tokens * width),
    )(chip, *pieces.values())


def attend_kernel(chip, table, q_ref, *refs, sources, later, places, hd):
    tokens = q_ref.shape[2]
    if sources:
        parts, sems, kv = refs[: PAIR * sources], refs[-1], refs[-2]
        outs = refs[PAIR * sources + later : -2]
    else:
        kv, outs = refs[0], refs[1 + later :]
    groups = []
    for g in range(2 * PAIR if sources else 0):
        copies = []
        for n, ref in enumerate(parts):
            core, row = n // sources, 0 if n % sources == 0 else parts[0].shape[0]
            row += max(n % sources - 1, 0) * HB
            target = kv.at[pl.ds(row, ref.shape[0]), core, g]
            copies.append(pltpu.make_async_copy(ref.at[:, g], target, sems.at[g, n]))
        groups.append(copies)

    def start(*group):
        for g in group:
            for copy in groups[g] if sources else []:
                copy.start()

    def wait(*group):
        for g in group:
            for copy in groups[g] if sources else []:
                copy.wait()

    scale = hd ** (-0.5)
    factor = scale * math.log2(math.e)
    trans = (((1,), (1,)), ((), ()))

    def products(k, h):
        block = chip[0] ^ k
        both = q_ref[block, h]
        query = both[:, :hd]
        left = jnp.concatenate([jnp.zeros_like(query), query], axis=1)
        left = jnp.concatenate([left, both], axis=0)
        window = [table[block * WK + w] for w in range(WK)]
        scores, tans = [], []
        for index in window:
            keys = kv[index, :, 2 * h].reshape(BQ, 2 * hd)
            product = lax.dot_general(left, keys, trans, preferred_element_type=jnp.float32)
            scores.append(product[:tokens])
            tans.append(product[tokens:])
        return window, scores, tans

    def finish(k, h, window, scores, tans):
        top = functools.reduce(jnp.maximum, scores)
        top = jnp.max(top, axis=1, keepdims=True) * factor
        probs = [jnp.exp2(s * factor - top) for s in scores]
        weighted = [p * t for p, t in zip(probs, tans)]
        total = jnp.sum(functools.reduce(jnp.add, probs), axis=1, keepdims=True)
        mean = jnp.sum(functools.reduce(jnp.add, weighted), axis=1, keepdims=True)
        mixed = jnp.zeros((2 * tokens, 2 * hd), jnp.float32)
        for index, p, w in zip(window, probs, weighted):
            vals = kv[index, :, 2 * h + 1].reshape(BQ, 2 * hd)
            right = jnp.concatenate([p.astype(jnp.bfloat16), w.astype(jnp.bfloat16)], axis=0)
            mixed += jnp.dot(right, vals, preferred_element_type=jnp.float32)
        inverse = 1.0 / total
        out = mixed[:tokens, :hd] * inverse
        tan = (mixed[:tokens, hd:] + scale * mixed[tokens:, :hd]) * inverse
        tan = tan - (scale * mean * inverse) * out
        ref = outs[places.index(k)]
        ref[:, 2 * h * hd : (2 * h + 1) * hd] = out.astype(jnp.bfloat16)
        ref[:, (2 * h + 1) * hd : 2 * (h + 1) * hd] = tan.astype(jnp.bfloat16)

    units = [(k, h) for h in range(PAIR) for k in places]
    start(0, 1)
    wait(0)
    ahead = products(*units[0])
    wait(1)
    start(2, 3)
    for unit, following in zip(units, units[1:] + [None]):
        current = ahead
        if following is not None:
            if following[1] > unit[1]:
                wait(2, 3)
            ahead = products(*following)
        finish(*unit, *current)


def attend(chip, table, queries, sources, later, places):
    _, _, tokens, pair = queries.shape
    hd, joins, width = pair // 2, len(sources) > 1, PAIR * pair
    elements = len(places) * BQ * WK * BQ
    outs = [jax.ShapeDtypeStruct((tokens, width), jnp.bfloat16)] * len(places)
    scratch, total = [], 0
    if joins:
        total = sum(a.shape[0] for a in sources) // PAIR
        outs.append(jax.ShapeDtypeStruct((total, PAIR, 2 * PAIR, tokens, pair), jnp.bfloat16))
        scratch.append(pltpu.SemaphoreType.DMA((2 * PAIR, len(sources))))
    return pl.pallas_call(
        functools.partial(
            attend_kernel,
            sources=len(sources) // PAIR if joins else 0,
            later=len(later),
            places=places,
            hd=hd,
        ),
        in_specs=[SMEM, SMEM, VMEM]
        + [ANY if joins else VMEM] * len(sources)
        + [ANY] * len(later),
        out_specs=[VMEM] * len(outs),
        out_shape=outs,
        scratch_shapes=scratch,
        compiler_params=PARAMS,
        cost_estimate=pl.CostEstimate(
            flops=12 * elements * hd,
            bytes_accessed=8 * total * tokens * width,
            transcendentals=elements,
        ),
    )(chip, table, queries, *sources, *later)


def locate(neighbors, frame, blocks):
    local = neighbors - frame * blocks
    even = frame % 2 == 0
    before = blocks + jnp.where(even, HB, 0) + local + HB
    after = blocks + jnp.where(even, 0, HB) + local - blocks
    return jnp.where(local < 0, before, jnp.where(local >= blocks, after, local)).reshape(-1)


def per_device(query, keys, values, query_tan, keys_tan, values_tan, neighbors):
    devices, frames = lax.axis_size("heads"), lax.axis_size("frames")
    frame = lax.axis_index("frames")
    chip = (lax.axis_index("heads") // PAIR).reshape(1).astype(jnp.int32)
    blocks = neighbors.shape[0]
    swap = [(d, d ^ 1) for d in range(devices)]
    (kv_sent,) = to_chips([keys_tan, keys, values, values_tan], devices)
    q_sent, zero = to_chips([query, query_tan], devices, [kv_sent])
    kv = exchange(kv_sent, devices)

    mine = [kv]
    for first in (0, 1):
        pairs = [(i, i + 1) for i in range(first, frames - 1, 2)]
        if pairs:
            start = jnp.where(frame % 2 == first, blocks - HB, 0) + zero[0]
            edge = lax.dynamic_slice_in_dim(kv, start, HB, axis=0)
            mine.append(lax.ppermute(edge, "frames", pairs + [(j, i) for i, j in pairs]))
    other = [lax.ppermute(a, "heads", swap) for a in mine]

    queries = exchange(q_sent, devices)
    table = locate(neighbors, frame, blocks)
    half, middle = blocks // 2, blocks // 2 + blocks // 4
    back, later, sources = {}, [], mine + other
    for part in ([*range(half, middle), 1], [*range(middle, blocks), *range(2, half), 0]):
        pieces = attend(chip, table, queries, sources, later, part)
        for k, piece in zip(part, pieces):
            pairs = [(d, d ^ (k * PAIR)) for d in range(devices)]
            back[k] = lax.ppermute(piece, "heads", pairs) if k else piece
        later, sources = [back[1]], pieces[len(part) :]
    return unpack(chip, back, 2)


def solution(mesh):
    own = P(("frames", "heads"), None)
    return jax.shard_map(
        per_device,
        mesh=mesh,
        in_specs=(own,) * 6 + (P("frames", None),),
        out_specs=(own, own),
        check_vma=False,
    )
```

```python
import functools
import math

import jax
import jax.numpy as jnp
from jax import lax
from jax.experimental import pallas as pl
from jax.experimental.pallas import tpu as pltpu
from jax.sharding import PartitionSpec as P

BQ = 256
WK = 4
HB = 4
PAIR = 2
STEP = 2
LEAD = 16
PARAMS = pltpu.CompilerParams(vmem_limit_bytes=32 * 1024 * 1024)
ANY = pl.BlockSpec(memory_space=pl.ANY)
HBM = pl.BlockSpec(memory_space=pltpu.HBM)
VMEM = pl.BlockSpec(memory_space=pltpu.VMEM)
SMEM = pl.BlockSpec(memory_space=pltpu.SMEM)


def pin(*arrays):
    return [pltpu.with_memory_space_constraint(a, pltpu.HBM) for a in arrays]


def moves(size):
    return pl.CostEstimate(flops=0, bytes_accessed=size, transcendentals=0)


def pack_kernel(*refs, count, before):
    arrays, out = refs[:count], refs[count + before]
    held, staged, sems, out_sems = refs[-4:]
    if before:
        refs[count + before + 1][0] = 0
    chips, columns = out.shape[0], held.shape[2]
    hd = columns // chips // PAIR
    copies = [pltpu.make_async_copy(a, held.at[i], sems.at[i]) for i, a in enumerate(arrays)]
    for copy in copies:
        copy.start()
    sends = []
    for stage in range(count // 2):
        pair = (2 * stage, 2 * stage + 1)
        for a in pair:
            copies[a].wait()
        for h in range(PAIR):
            group = h * (count // 2) + stage
            for chip in range(chips):
                source = (chip * PAIR + h) * hd
                for i, a in enumerate(pair):
                    staged[group, chip, :, i * hd : (i + 1) * hd] = held[
                        a, :, source : source + hd
                    ]
            sends.append(
                pltpu.make_async_copy(staged.at[group], out.at[:, group], out_sems.at[group])
            )
            sends[-1].start()
    for send in sends:
        send.wait()


def to_chips(arrays, devices, before=()):
    tokens, columns = arrays[0].shape
    count, chips, hd = len(arrays), devices // PAIR, columns // devices
    shape = (chips, PAIR * count // 2, tokens, 2 * hd)
    more = min(len(before), 1)
    return pl.pallas_call(
        functools.partial(pack_kernel, count=count, before=len(before)),
        in_specs=[HBM] * (count + len(before)),
        out_specs=[HBM] + [SMEM] * more,
        out_shape=[pltpu.HBM(shape, jnp.bfloat16)]
        + [jax.ShapeDtypeStruct((1,), jnp.int32)] * more,
        scratch_shapes=[
            pltpu.VMEM((count, tokens, columns), jnp.bfloat16),
            pltpu.VMEM((shape[1], chips, tokens, 2 * hd), jnp.bfloat16),
            pltpu.SemaphoreType.DMA((count,)),
            pltpu.SemaphoreType.DMA((shape[1],)),
        ],
        compiler_params=PARAMS,
        cost_estimate=moves(4 * count * tokens * columns),
    )(*pin(*arrays, *before))


def exchange(pieces, devices):
    groups = [list(range(core, devices, PAIR)) for core in range(PAIR)]
    return lax.all_to_all(
        pieces, "heads", split_axis=0, concat_axis=0, axis_index_groups=groups, tiled=True
    )


def unpack_kernel(chip, *refs, order):
    pieces, arrays = refs[: len(order)], refs[len(order) :]
    hd = pieces[0].shape[1] // len(arrays) // PAIR
    for k, piece in zip(order, pieces):
        for h in range(PAIR):
            columns = pl.ds(pl.multiple_of(((chip[0] ^ k) * PAIR + h) * hd, hd), hd)
            for a, array in enumerate(arrays):
                source = (h * len(arrays) + a) * hd
                array[:, columns] = piece[:, source : source + hd]


def unpack(chip, pieces, count):
    tokens, width = pieces[0].shape
    columns = len(pieces) * width // count
    return pl.pallas_call(
        functools.partial(unpack_kernel, order=list(pieces)),
        in_specs=[SMEM] + [VMEM] * len(pieces),
        out_specs=[VMEM] * count,
        out_shape=[jax.ShapeDtypeStruct((tokens, columns), jnp.bfloat16)] * count,
        compiler_params=PARAMS,
        cost_estimate=moves(4 * len(pieces) * tokens * width),
    )(chip, *pieces.values())


def attend_kernel(chip, table, q_ref, *refs, sources, later, places, hd):
    tokens = q_ref.shape[2]
    if sources:
        parts, sems, kv = refs[: PAIR * sources], refs[-1], refs[-2]
        outs = refs[PAIR * sources + later : -3]
    else:
        kv, outs = refs[0], refs[1 + later :]
    copies = []
    for n, ref in enumerate(parts if sources else ()):
        core, row = n // sources, 0 if n % sources == 0 else parts[0].shape[0]
        row += max(n % sources - 1, 0) * HB
        for i in range(0, ref.shape[0], STEP):
            target = kv.at[pl.ds(row + i, STEP), core]
            copies.append(
                pltpu.make_async_copy(ref.at[pl.ds(i, STEP)], target, sems.at[n, i // STEP])
            )
    for copy in copies:
        copy.start()
    for copy in copies:
        copy.wait()

    scale = hd ** (-0.5)
    factor = scale * math.log2(math.e)
    trans = (((1,), (1,)), ((), ()))

    def products(k, h):
        block = chip[0] ^ k
        both = q_ref[block, h]
        query = both[:, :hd]
        left = jnp.concatenate([jnp.zeros_like(query), query], axis=1)
        left = jnp.concatenate([left, both], axis=0)
        window = [table[block * WK + w] for w in range(WK)]
        scores, tans = [], []
        for index in window:
            keys = kv[index, :, 2 * h].reshape(BQ, 2 * hd)
            product = lax.dot_general(left, keys, trans, preferred_element_type=jnp.float32)
            scores.append(product[:tokens])
            tans.append(product[tokens:])
        return window, scores, tans

    def finish(k, h, window, scores, tans):
        top = functools.reduce(jnp.maximum, scores)
        top = jnp.max(top, axis=1, keepdims=True) * factor
        probs = [jnp.exp2(s * factor - top) for s in scores]
        weighted = [p * t for p, t in zip(probs, tans)]
        total = jnp.sum(functools.reduce(jnp.add, probs), axis=1, keepdims=True)
        mean = jnp.sum(functools.reduce(jnp.add, weighted), axis=1, keepdims=True)
        mixed = jnp.zeros((2 * tokens, 2 * hd), jnp.float32)
        for index, p, w in zip(window, probs, weighted):
            vals = kv[index, :, 2 * h + 1].reshape(BQ, 2 * hd)
            right = jnp.concatenate([p.astype(jnp.bfloat16), w.astype(jnp.bfloat16)], axis=0)
            mixed += jnp.dot(right, vals, preferred_element_type=jnp.float32)
        inverse = 1.0 / total
        out = mixed[:tokens, :hd] * inverse
        tan = (mixed[:tokens, hd:] + scale * mixed[tokens:, :hd]) * inverse
        tan = tan - (scale * mean * inverse) * out
        ref = outs[places.index(k)]
        ref[:, 2 * h * hd : (2 * h + 1) * hd] = out.astype(jnp.bfloat16)
        ref[:, (2 * h + 1) * hd : 2 * (h + 1) * hd] = tan.astype(jnp.bfloat16)

    units = [(k, h) for k in places for h in range(PAIR)]
    ahead = products(*units[0])
    for unit, following in zip(units, units[1:] + [None]):
        current = ahead
        if following is not None:
            ahead = products(*following)
        finish(*unit, *current)
    if sources:
        refs[-3][...] = outs[0][:LEAD]


def attend(chip, table, queries, sources, later, places):
    _, _, tokens, pair = queries.shape
    hd, joins, width = pair // 2, len(sources) > 1, PAIR * pair
    elements = len(places) * BQ * WK * BQ
    outs = [jax.ShapeDtypeStruct((tokens, width), jnp.bfloat16)] * len(places)
    scratch, total = [], 0
    if joins:
        total = sum(a.shape[0] for a in sources) // PAIR
        outs.append(jax.ShapeDtypeStruct((LEAD, width), jnp.bfloat16))
        outs.append(jax.ShapeDtypeStruct((total, PAIR, 2 * PAIR, tokens, pair), jnp.bfloat16))
        most = max(a.shape[0] for a in sources)
        scratch.append(pltpu.SemaphoreType.DMA((len(sources), most // STEP)))
    return pl.pallas_call(
        functools.partial(
            attend_kernel,
            sources=len(sources) // PAIR if joins else 0,
            later=len(later),
            places=places,
            hd=hd,
        ),
        in_specs=[SMEM, SMEM, VMEM]
        + [ANY if joins else VMEM] * len(sources)
        + [ANY] * len(later),
        out_specs=[VMEM] * len(outs),
        out_shape=outs,
        scratch_shapes=scratch,
        compiler_params=PARAMS,
        cost_estimate=pl.CostEstimate(
            flops=12 * elements * hd,
            bytes_accessed=8 * total * tokens * width,
            transcendentals=elements,
        ),
    )(chip, table, queries, *sources, *later)


def locate(neighbors, frame, blocks):
    local = neighbors - frame * blocks
    even = frame % 2 == 0
    before = blocks + jnp.where(even, HB, 0) + local + HB
    after = blocks + jnp.where(even, 0, HB) + local - blocks
    return jnp.where(local < 0, before, jnp.where(local >= blocks, after, local)).reshape(-1)


def per_device(query, keys, values, query_tan, keys_tan, values_tan, neighbors):
    devices, frames = lax.axis_size("heads"), lax.axis_size("frames")
    frame = lax.axis_index("frames")
    chip = (lax.axis_index("heads") // PAIR).reshape(1).astype(jnp.int32)
    blocks = neighbors.shape[0]
    swap = [(d, d ^ 1) for d in range(devices)]
    (kv_sent,) = to_chips([keys_tan, keys, values, values_tan], devices)
    q_sent, zero = to_chips([query, query_tan], devices, [kv_sent])
    kv = exchange(kv_sent, devices)

    mine = [kv]
    for first in (0, 1):
        pairs = [(i, i + 1) for i in range(first, frames - 1, 2)]
        if pairs:
            start = jnp.where(frame % 2 == first, blocks - HB, 0) + zero[0]
            edge = lax.dynamic_slice_in_dim(kv, start, HB, axis=0)
            mine.append(lax.ppermute(edge, "frames", pairs + [(j, i) for i, j in pairs]))
    other = [lax.ppermute(a, "heads", swap) for a in mine]

    queries = exchange(q_sent, devices)
    table = locate(neighbors, frame, blocks)
    half, middle = blocks // 2, blocks // 2 + blocks // 4
    back, later, sources = {}, [], mine + other
    for part in (range(half, middle), [*range(middle, blocks), *range(1, half), 0]):
        pieces = attend(chip, table, queries, sources, later, list(part))
        for k, piece in zip(part, pieces):
            pairs = [(d, d ^ (k * PAIR)) for d in range(devices)]
            back[k] = lax.ppermute(piece, "heads", pairs) if k else piece
        if not later:
            later = [lax.ppermute(pieces[-2], "heads", swap)]
            sources = pieces[-1:]
    return unpack(chip, back, 2)


def solution(mesh):
    own = P(("frames", "heads"), None)
    return jax.shard_map(
        per_device,
        mesh=mesh,
        in_specs=(own,) * 6 + (P("frames", None),),
        out_specs=(own, own),
        check_vma=False,
    )
```

```python
import functools
import math

import jax
import jax.numpy as jnp
from jax import lax
from jax.experimental import pallas as pl
from jax.experimental.pallas import tpu as pltpu
from jax.sharding import PartitionSpec as P

BQ = 256
WK = 4
HB = 4
PAIR = 2
STEP = 2
LEAD = 16
PARAMS = pltpu.CompilerParams(vmem_limit_bytes=32 * 1024 * 1024)
ANY = pl.BlockSpec(memory_space=pl.ANY)
HBM = pl.BlockSpec(memory_space=pltpu.HBM)
VMEM = pl.BlockSpec(memory_space=pltpu.VMEM)
SMEM = pl.BlockSpec(memory_space=pltpu.SMEM)


def pin(*arrays):
    return [pltpu.with_memory_space_constraint(a, pltpu.HBM) for a in arrays]


def moves(size):
    return pl.CostEstimate(flops=0, bytes_accessed=size, transcendentals=0)


def pack_kernel(*refs, count, before):
    arrays, out = refs[:count], refs[count + before]
    held, staged, sems, out_sems = refs[-4:]
    if before:
        refs[count + before + 1][0] = 0
    chips, columns = out.shape[0], held.shape[2]
    hd = columns // chips // PAIR
    copies = [pltpu.make_async_copy(a, held.at[i], sems.at[i]) for i, a in enumerate(arrays)]
    for copy in copies:
        copy.start()
    sends = []
    for stage in range(count // 2):
        pair = (2 * stage, 2 * stage + 1)
        for a in pair:
            copies[a].wait()
        for h in range(PAIR):
            group = h * (count // 2) + stage
            for chip in range(chips):
                source = (chip * PAIR + h) * hd
                for i, a in enumerate(pair):
                    staged[group, chip, :, i * hd : (i + 1) * hd] = held[
                        a, :, source : source + hd
                    ]
            sends.append(
                pltpu.make_async_copy(staged.at[group], out.at[:, group], out_sems.at[group])
            )
            sends[-1].start()
    for send in sends:
        send.wait()


def to_chips(arrays, devices, before=()):
    tokens, columns = arrays[0].shape
    count, chips, hd = len(arrays), devices // PAIR, columns // devices
    shape = (chips, PAIR * count // 2, tokens, 2 * hd)
    more = min(len(before), 1)
    return pl.pallas_call(
        functools.partial(pack_kernel, count=count, before=len(before)),
        in_specs=[HBM] * (count + len(before)),
        out_specs=[HBM] + [SMEM] * more,
        out_shape=[pltpu.HBM(shape, jnp.bfloat16)]
        + [jax.ShapeDtypeStruct((1,), jnp.int32)] * more,
        scratch_shapes=[
            pltpu.VMEM((count, tokens, columns), jnp.bfloat16),
            pltpu.VMEM((shape[1], chips, tokens, 2 * hd), jnp.bfloat16),
            pltpu.SemaphoreType.DMA((count,)),
            pltpu.SemaphoreType.DMA((shape[1],)),
        ],
        compiler_params=PARAMS,
        cost_estimate=moves(4 * count * tokens * columns),
    )(*pin(*arrays, *before))


def exchange(pieces, devices):
    groups = [list(range(core, devices, PAIR)) for core in range(PAIR)]
    return lax.all_to_all(
        pieces, "heads", split_axis=0, concat_axis=0, axis_index_groups=groups, tiled=True
    )


def unpack_kernel(chip, *refs, order):
    pieces, arrays = refs[: len(order)], refs[len(order) :]
    hd = pieces[0].shape[1] // len(arrays) // PAIR
    for k, piece in zip(order, pieces):
        for h in range(PAIR):
            columns = pl.ds(pl.multiple_of(((chip[0] ^ k) * PAIR + h) * hd, hd), hd)
            for a, array in enumerate(arrays):
                source = (h * len(arrays) + a) * hd
                array[:, columns] = piece[:, source : source + hd]


def unpack(chip, pieces, count):
    tokens, width = pieces[0].shape
    columns = len(pieces) * width // count
    return pl.pallas_call(
        functools.partial(unpack_kernel, order=list(pieces)),
        in_specs=[SMEM] + [VMEM] * len(pieces),
        out_specs=[VMEM] * count,
        out_shape=[jax.ShapeDtypeStruct((tokens, columns), jnp.bfloat16)] * count,
        compiler_params=PARAMS,
        cost_estimate=moves(4 * len(pieces) * tokens * width),
    )(chip, *pieces.values())


def edge_kernel(start, kv, out, sems):
    copies = []
    for i in range(HB):
        copies.append(pltpu.make_async_copy(kv.at[start[0] + i], out.at[i], sems.at[i]))
    for copy in copies:
        copy.start()
    for copy in copies:
        copy.wait()


def edge(start, kv):
    shape = (HB, *kv.shape[1:])
    return pl.pallas_call(
        edge_kernel,
        in_specs=[SMEM, VMEM],
        out_specs=HBM,
        out_shape=pltpu.HBM(shape, jnp.bfloat16),
        scratch_shapes=[pltpu.SemaphoreType.DMA((HB,))],
        compiler_params=PARAMS,
        cost_estimate=moves(4 * math.prod(shape)),
    )(start, kv)


def attend_kernel(chip, table, q_ref, *refs, sources, halos, later, places, hd):
    tokens = q_ref.shape[2]
    own, refs = refs[0], refs[1:]
    blocks = own.shape[0]
    if sources:
        parts, sems, halo, rest = refs[:sources], refs[-1], refs[-3], refs[-2]
        outs = refs[sources + later : -4]
        copies, row = [], {0: 0, 1: 0}
        for n, ref in enumerate(parts):
            target, core = (halo, 0) if n < halos else (rest, 1)
            for i in range(0, ref.shape[0], STEP):
                place = target.at[pl.ds(row[core] + i, STEP)]
                copies.append(
                    pltpu.make_async_copy(ref.at[pl.ds(i, STEP)], place, sems.at[n, i // STEP])
                )
            row[core] += ref.shape[0]
        for copy in copies:
            copy.start()
        for copy in copies:
            copy.wait()
    else:
        halo, rest, outs = refs[0], refs[1], refs[2 + later :]

    def rows(index, group):
        here = own[jnp.minimum(index, blocks - 1), group]
        there = halo[jnp.maximum(index - blocks, 0), group]
        return jnp.concatenate([jnp.where(index < blocks, here, there), rest[index, group]], axis=0)

    scale = hd ** (-0.5)
    factor = scale * math.log2(math.e)
    trans = (((1,), (1,)), ((), ()))

    def products(k, h):
        block = chip[0] ^ k
        both = q_ref[block, h]
        query = both[:, :hd]
        left = jnp.concatenate([jnp.zeros_like(query), query], axis=1)
        left = jnp.concatenate([left, both], axis=0)
        window = [table[block * WK + w] for w in range(WK)]
        scores, tans = [], []
        for index in window:
            keys = rows(index, 2 * h)
            product = lax.dot_general(left, keys, trans, preferred_element_type=jnp.float32)
            scores.append(product[:tokens])
            tans.append(product[tokens:])
        return window, scores, tans

    def finish(k, h, window, scores, tans):
        top = functools.reduce(jnp.maximum, scores)
        top = jnp.max(top, axis=1, keepdims=True) * factor
        probs = [jnp.exp2(s * factor - top) for s in scores]
        weighted = [p * t for p, t in zip(probs, tans)]
        total = jnp.sum(functools.reduce(jnp.add, probs), axis=1, keepdims=True)
        mean = jnp.sum(functools.reduce(jnp.add, weighted), axis=1, keepdims=True)
        mixed = jnp.zeros((2 * tokens, 2 * hd), jnp.float32)
        for index, p, w in zip(window, probs, weighted):
            vals = rows(index, 2 * h + 1)
            right = jnp.concatenate([p.astype(jnp.bfloat16), w.astype(jnp.bfloat16)], axis=0)
            mixed += jnp.dot(right, vals, preferred_element_type=jnp.float32)
        inverse = 1.0 / total
        out = mixed[:tokens, :hd] * inverse
        tan = (mixed[:tokens, hd:] + scale * mixed[tokens:, :hd]) * inverse
        tan = tan - (scale * mean * inverse) * out
        ref = outs[places.index(k)]
        ref[:, 2 * h * hd : (2 * h + 1) * hd] = out.astype(jnp.bfloat16)
        ref[:, (2 * h + 1) * hd : 2 * (h + 1) * hd] = tan.astype(jnp.bfloat16)

    units = [(k, h) for k in places for h in range(PAIR)]
    ahead = products(*units[0])
    for unit, following in zip(units, units[1:] + [None]):
        current = ahead
        if following is not None:
            ahead = products(*following)
        finish(*unit, *current)
    if sources:
        refs[-4][...] = outs[0][:LEAD]


def attend(chip, table, queries, own, sources, halos, later, places, first):
    _, _, tokens, pair = queries.shape
    hd, width = pair // 2, PAIR * pair
    elements = len(places) * BQ * WK * BQ
    outs = [jax.ShapeDtypeStruct((tokens, width), jnp.bfloat16)] * len(places)
    scratch, total = [], 0
    if first:
        count = halos
        total = sum(a.shape[0] for a in sources)
        outs.append(jax.ShapeDtypeStruct((LEAD, width), jnp.bfloat16))
        for group in (sources[:count], sources[count:]):
            shape = (sum(a.shape[0] for a in group), *own.shape[1:])
            outs.append(jax.ShapeDtypeStruct(shape, jnp.bfloat16))
        most = max(a.shape[0] for a in sources)
        scratch.append(pltpu.SemaphoreType.DMA((len(sources), most // STEP)))
    return pl.pallas_call(
        functools.partial(
            attend_kernel,
            sources=len(sources) if first else 0,
            halos=halos,
            later=len(later),
            places=places,
            hd=hd,
        ),
        in_specs=[SMEM, SMEM, VMEM, VMEM]
        + [ANY if first else VMEM] * len(sources)
        + [ANY] * len(later),
        out_specs=[VMEM] * len(outs),
        out_shape=outs,
        scratch_shapes=scratch,
        compiler_params=PARAMS,
        cost_estimate=pl.CostEstimate(
            flops=12 * elements * hd,
            bytes_accessed=4 * total * tokens * width,
            transcendentals=elements,
        ),
    )(chip, table, queries, own, *sources, *later)


def locate(neighbors, frame, blocks):
    local = neighbors - frame * blocks
    even = frame % 2 == 0
    before = blocks + jnp.where(even, HB, 0) + local + HB
    after = blocks + jnp.where(even, 0, HB) + local - blocks
    return jnp.where(local < 0, before, jnp.where(local >= blocks, after, local)).reshape(-1)


def per_device(query, keys, values, query_tan, keys_tan, values_tan, neighbors):
    devices, frames = lax.axis_size("heads"), lax.axis_size("frames")
    frame = lax.axis_index("frames")
    chip = (lax.axis_index("heads") // PAIR).reshape(1).astype(jnp.int32)
    blocks = neighbors.shape[0]
    swap = [(d, d ^ 1) for d in range(devices)]
    (kv_sent,) = to_chips([keys_tan, keys, values, values_tan], devices)
    q_sent, zero = to_chips([query, query_tan], devices, [kv_sent])
    kv = exchange(kv_sent, devices)

    mine, rounds = [kv], []
    for first in (0, 1):
        pairs = [(i, i + 1) for i in range(first, frames - 1, 2)]
        if pairs:
            rounds.append(pairs + [(j, i) for i, j in pairs])
            start = jnp.where(frame % 2 == first, blocks - HB, 0).astype(jnp.int32) + zero
            mine.append(lax.ppermute(edge(start, kv), "frames", rounds[-1]))
    other = [lax.ppermute(a, "heads", swap) for a in mine]

    queries = exchange(q_sent, devices)
    table = locate(neighbors, frame, blocks)
    half, middle = blocks // 2, blocks // 2 + blocks // 4
    back, later, sources = {}, [], mine[1:] + other
    for part in (range(half, middle), [*range(middle, blocks), *range(1, half), 0]):
        pieces = attend(chip, table, queries, kv, sources, len(rounds), later, list(part), not later)
        for k, piece in zip(part, pieces):
            pairs = [(d, d ^ (k * PAIR)) for d in range(devices)]
            back[k] = lax.ppermute(piece, "heads", pairs) if k else piece
        if not later:
            later = [lax.ppermute(pieces[-3], "heads", swap)]
            sources = pieces[-2:]
    return unpack(chip, back, 2)


def solution(mesh):
    own = P(("frames", "heads"), None)
    return jax.shard_map(
        per_device,
        mesh=mesh,
        in_specs=(own,) * 6 + (P("frames", None),),
        out_specs=(own, own),
        check_vma=False,
    )
```

```python
import functools
import math

import jax
import jax.numpy as jnp
from jax import lax
from jax.experimental import pallas as pl
from jax.experimental.pallas import tpu as pltpu
from jax.sharding import PartitionSpec as P

BQ = 256
WK = 4
HB = 4
PAIR = 2
STEP = 2
LEAD = 16
PARAMS = pltpu.CompilerParams(vmem_limit_bytes=32 * 1024 * 1024)
ANY = pl.BlockSpec(memory_space=pl.ANY)
HBM = pl.BlockSpec(memory_space=pltpu.HBM)
VMEM = pl.BlockSpec(memory_space=pltpu.VMEM)
SMEM = pl.BlockSpec(memory_space=pltpu.SMEM)


def pin(*arrays):
    return [pltpu.with_memory_space_constraint(a, pltpu.HBM) for a in arrays]


def moves(size):
    return pl.CostEstimate(flops=0, bytes_accessed=size, transcendentals=0)


def pack_kernel(*refs, count, before):
    arrays, out = refs[:count], refs[count + before]
    held, staged, sems, out_sems = refs[-4:]
    if before:
        refs[count + before + 1][0] = 0
    chips, columns = out.shape[0], held.shape[2]
    hd = columns // chips // PAIR
    copies = [pltpu.make_async_copy(a, held.at[i], sems.at[i]) for i, a in enumerate(arrays)]
    for copy in copies:
        copy.start()
    sends = []
    for stage in range(count // 2):
        pair = (2 * stage, 2 * stage + 1)
        for a in pair:
            copies[a].wait()
        for h in range(PAIR):
            group = h * (count // 2) + stage
            for chip in range(chips):
                source = (chip * PAIR + h) * hd
                for i, a in enumerate(pair):
                    staged[group, chip, :, i * hd : (i + 1) * hd] = held[
                        a, :, source : source + hd
                    ]
            sends.append(
                pltpu.make_async_copy(staged.at[group], out.at[:, group], out_sems.at[group])
            )
            sends[-1].start()
    for send in sends:
        send.wait()


def to_chips(arrays, devices, before=()):
    tokens, columns = arrays[0].shape
    count, chips, hd = len(arrays), devices // PAIR, columns // devices
    shape = (chips, PAIR * count // 2, tokens, 2 * hd)
    more = min(len(before), 1)
    return pl.pallas_call(
        functools.partial(pack_kernel, count=count, before=len(before)),
        in_specs=[HBM] * (count + len(before)),
        out_specs=[HBM] + [SMEM] * more,
        out_shape=[pltpu.HBM(shape, jnp.bfloat16)]
        + [jax.ShapeDtypeStruct((1,), jnp.int32)] * more,
        scratch_shapes=[
            pltpu.VMEM((count, tokens, columns), jnp.bfloat16),
            pltpu.VMEM((shape[1], chips, tokens, 2 * hd), jnp.bfloat16),
            pltpu.SemaphoreType.DMA((count,)),
            pltpu.SemaphoreType.DMA((shape[1],)),
        ],
        compiler_params=PARAMS,
        cost_estimate=moves(4 * count * tokens * columns),
    )(*pin(*arrays, *before))


def exchange(pieces, devices):
    groups = [list(range(core, devices, PAIR)) for core in range(PAIR)]
    return lax.all_to_all(
        pieces, "heads", split_axis=0, concat_axis=0, axis_index_groups=groups, tiled=True
    )


def unpack_kernel(chip, *refs, order):
    pieces, arrays, sems = refs[: len(order)], refs[len(order) : -1], refs[-1]
    width = pieces[0].shape[1] // len(arrays)
    copies = []
    for k, piece in zip(order, pieces):
        columns = pl.ds(pl.multiple_of((chip[0] ^ k) * width, width), width)
        for a, array in enumerate(arrays):
            source = piece.at[:, a * width : (a + 1) * width]
            copies.append(pltpu.make_async_copy(source, array.at[:, columns], sems.at[k, a]))
            copies[-1].start()
    for copy in copies:
        copy.wait()


def unpack(chip, pieces, count):
    tokens, width = pieces[0].shape
    columns = len(pieces) * width // count
    return pl.pallas_call(
        functools.partial(unpack_kernel, order=list(pieces)),
        in_specs=[SMEM] + [VMEM] * len(pieces),
        out_specs=[HBM] * count,
        out_shape=[pltpu.HBM((tokens, columns), jnp.bfloat16)] * count,
        scratch_shapes=[pltpu.SemaphoreType.DMA((len(pieces), count))],
        compiler_params=PARAMS,
        cost_estimate=moves(4 * len(pieces) * tokens * width),
    )(chip, *pieces.values())


def edge_kernel(start, kv, out, sems):
    copies = []
    for i in range(HB):
        copies.append(pltpu.make_async_copy(kv.at[start[0] + i], out.at[i], sems.at[i]))
    for copy in copies:
        copy.start()
    for copy in copies:
        copy.wait()


def edge(start, kv):
    shape = (HB, *kv.shape[1:])
    return pl.pallas_call(
        edge_kernel,
        in_specs=[SMEM, VMEM],
        out_specs=HBM,
        out_shape=pltpu.HBM(shape, jnp.bfloat16),
        scratch_shapes=[pltpu.SemaphoreType.DMA((HB,))],
        compiler_params=PARAMS,
        cost_estimate=moves(4 * math.prod(shape)),
    )(start, kv)


def attend_kernel(chip, table, q_ref, *refs, sources, halos, later, places, hd):
    tokens = q_ref.shape[2]
    own, refs = refs[0], refs[1:]
    blocks = own.shape[0]
    if sources:
        parts, sems, halo, rest = refs[:sources], refs[-1], refs[-3], refs[-2]
        outs = refs[sources + later : -4]
        copies, row = [[] for _ in range(PAIR)], {0: 0, 1: 0}
        for n, ref in enumerate(parts):
            target, core = (halo, 0) if n < halos else (rest, 1)
            for i in range(0, ref.shape[0], STEP):
                for h in range(PAIR):
                    half = pl.ds(2 * h, 2)
                    place = target.at[pl.ds(row[core] + i, STEP), half]
                    source = ref.at[pl.ds(i, STEP), half]
                    copies[h].append(
                        pltpu.make_async_copy(source, place, sems.at[h, n, i // STEP])
                    )
            row[core] += ref.shape[0]
    else:
        halo, rest, outs = refs[0], refs[1], refs[2 + later :]
        copies = [[] for _ in range(PAIR)]

    def rows(index, group):
        here = own[jnp.minimum(index, blocks - 1), group]
        there = halo[jnp.maximum(index - blocks, 0), group]
        return jnp.concatenate([jnp.where(index < blocks, here, there), rest[index, group]], axis=0)

    scale = hd ** (-0.5)
    factor = scale * math.log2(math.e)
    trans = (((1,), (1,)), ((), ()))

    def products(k, h):
        block = chip[0] ^ k
        both = q_ref[block, h]
        query = both[:, :hd]
        left = jnp.concatenate([jnp.zeros_like(query), query], axis=1)
        left = jnp.concatenate([left, both], axis=0)
        window = [table[block * WK + w] for w in range(WK)]
        scores, tans = [], []
        for index in window:
            keys = rows(index, 2 * h)
            product = lax.dot_general(left, keys, trans, preferred_element_type=jnp.float32)
            scores.append(product[:tokens])
            tans.append(product[tokens:])
        return window, scores, tans

    def finish(k, h, window, scores, tans):
        top = functools.reduce(jnp.maximum, scores)
        top = jnp.max(top, axis=1, keepdims=True) * factor
        probs = [jnp.exp2(s * factor - top) for s in scores]
        weighted = [p * t for p, t in zip(probs, tans)]
        total = jnp.sum(functools.reduce(jnp.add, probs), axis=1, keepdims=True)
        mean = jnp.sum(functools.reduce(jnp.add, weighted), axis=1, keepdims=True)
        mixed = jnp.zeros((2 * tokens, 2 * hd), jnp.float32)
        for index, p, w in zip(window, probs, weighted):
            vals = rows(index, 2 * h + 1)
            right = jnp.concatenate([p.astype(jnp.bfloat16), w.astype(jnp.bfloat16)], axis=0)
            mixed += jnp.dot(right, vals, preferred_element_type=jnp.float32)
        inverse = 1.0 / total
        out = mixed[:tokens, :hd] * inverse
        tan = (mixed[:tokens, hd:] + scale * mixed[tokens:, :hd]) * inverse
        tan = tan - (scale * mean * inverse) * out
        ref = outs[places.index(k)]
        ref[:, h * hd : (h + 1) * hd] = out.astype(jnp.bfloat16)
        ref[:, (PAIR + h) * hd : (PAIR + h + 1) * hd] = tan.astype(jnp.bfloat16)

    def start(h):
        for copy in copies[h]:
            copy.start()

    def wait(h):
        for copy in copies[h]:
            copy.wait()

    units = [(k, h) for h in range(PAIR) for k in places]
    start(0)
    wait(0)
    for h in range(1, PAIR):
        start(h)
    ahead = products(*units[0])
    for unit, following in zip(units, units[1:] + [None]):
        current = ahead
        if following is not None:
            if following[1] > unit[1]:
                wait(following[1])
            ahead = products(*following)
        finish(*unit, *current)
    if sources:
        refs[-4][...] = outs[0][:LEAD]


def attend(chip, table, queries, own, sources, halos, later, places, first):
    _, _, tokens, pair = queries.shape
    hd, width = pair // 2, PAIR * pair
    elements = len(places) * BQ * WK * BQ
    outs = [jax.ShapeDtypeStruct((tokens, width), jnp.bfloat16)] * len(places)
    scratch, total = [], 0
    if first:
        count = halos
        total = sum(a.shape[0] for a in sources)
        outs.append(jax.ShapeDtypeStruct((LEAD, width), jnp.bfloat16))
        for group in (sources[:count], sources[count:]):
            shape = (sum(a.shape[0] for a in group), *own.shape[1:])
            outs.append(jax.ShapeDtypeStruct(shape, jnp.bfloat16))
        most = max(a.shape[0] for a in sources)
        scratch.append(pltpu.SemaphoreType.DMA((PAIR, len(sources), most // STEP)))
    return pl.pallas_call(
        functools.partial(
            attend_kernel,
            sources=len(sources) if first else 0,
            halos=halos,
            later=len(later),
            places=places,
            hd=hd,
        ),
        in_specs=[SMEM, SMEM, VMEM, VMEM]
        + [ANY if first else VMEM] * len(sources)
        + [ANY] * len(later),
        out_specs=[VMEM] * len(outs),
        out_shape=outs,
        scratch_shapes=scratch,
        compiler_params=PARAMS,
        cost_estimate=pl.CostEstimate(
            flops=12 * elements * hd,
            bytes_accessed=4 * total * tokens * width,
            transcendentals=elements,
        ),
    )(chip, table, queries, own, *sources, *later)


def locate(neighbors, frame, blocks):
    local = neighbors - frame * blocks
    even = frame % 2 == 0
    before = blocks + jnp.where(even, HB, 0) + local + HB
    after = blocks + jnp.where(even, 0, HB) + local - blocks
    return jnp.where(local < 0, before, jnp.where(local >= blocks, after, local)).reshape(-1)


def per_device(query, keys, values, query_tan, keys_tan, values_tan, neighbors):
    devices, frames = lax.axis_size("heads"), lax.axis_size("frames")
    frame = lax.axis_index("frames")
    chip = (lax.axis_index("heads") // PAIR).reshape(1).astype(jnp.int32)
    blocks = neighbors.shape[0]
    swap = [(d, d ^ 1) for d in range(devices)]
    (kv_sent,) = to_chips([keys_tan, keys, values, values_tan], devices)
    q_sent, zero = to_chips([query, query_tan], devices, [kv_sent])
    kv = exchange(kv_sent, devices)

    mine, rounds = [kv], []
    for first in (0, 1):
        pairs = [(i, i + 1) for i in range(first, frames - 1, 2)]
        if pairs:
            rounds.append(pairs + [(j, i) for i, j in pairs])
            start = jnp.where(frame % 2 == first, blocks - HB, 0).astype(jnp.int32) + zero
            mine.append(lax.ppermute(edge(start, kv), "frames", rounds[-1]))
    other = [lax.ppermute(a, "heads", swap) for a in mine]

    queries = exchange(q_sent, devices)
    table = locate(neighbors, frame, blocks)
    half, middle = blocks // 2, blocks // 2 + blocks // 4
    back, later, sources = {}, [], mine[1:] + other
    for part in (range(half, middle), [*range(middle, blocks), *range(1, half), 0]):
        pieces = attend(chip, table, queries, kv, sources, len(rounds), later, list(part), not later)
        for k, piece in zip(part, pieces):
            pairs = [(d, d ^ (k * PAIR)) for d in range(devices)]
            back[k] = lax.ppermute(piece, "heads", pairs) if k else piece
        if not later:
            later = [lax.ppermute(pieces[-3], "heads", swap)]
            sources = pieces[-2:]
    return unpack(chip, back, 2)


def solution(mesh):
    own = P(("frames", "heads"), None)
    return jax.shard_map(
        per_device,
        mesh=mesh,
        in_specs=(own,) * 6 + (P("frames", None),),
        out_specs=(own, own),
        check_vma=False,
    )
```

```python
import functools
import math

import jax
import jax.numpy as jnp
from jax import lax
from jax.experimental import pallas as pl
from jax.experimental.pallas import tpu as pltpu
from jax.sharding import PartitionSpec as P

BQ = 256
WK = 4
HB = 4
PAIR = 2
LEAD = 16
PARAMS = pltpu.CompilerParams(vmem_limit_bytes=32 * 1024 * 1024)
ANY = pl.BlockSpec(memory_space=pl.ANY)
HBM = pl.BlockSpec(memory_space=pltpu.HBM)
VMEM = pl.BlockSpec(memory_space=pltpu.VMEM)
SMEM = pl.BlockSpec(memory_space=pltpu.SMEM)


def pin(*arrays):
    return [pltpu.with_memory_space_constraint(a, pltpu.HBM) for a in arrays]


def moves(size):
    return pl.CostEstimate(flops=0, bytes_accessed=size, transcendentals=0)


def pack_kernel(*refs, count, before):
    arrays, out = refs[:count], refs[count + before]
    held, staged, sems, out_sems = refs[-4:]
    if before:
        refs[count + before + 1][0] = 0
    chips, columns = out.shape[0], held.shape[2]
    hd = columns // chips // PAIR
    copies = [pltpu.make_async_copy(a, held.at[i], sems.at[i]) for i, a in enumerate(arrays)]
    for copy in copies:
        copy.start()
    sends = []
    for stage in range(count // 2):
        pair = (2 * stage, 2 * stage + 1)
        for a in pair:
            copies[a].wait()
        for h in range(PAIR):
            group = h * (count // 2) + stage
            for chip in range(chips):
                source = (chip * PAIR + h) * hd
                for i, a in enumerate(pair):
                    staged[group, chip, :, i * hd : (i + 1) * hd] = held[
                        a, :, source : source + hd
                    ]
            sends.append(
                pltpu.make_async_copy(staged.at[group], out.at[:, group], out_sems.at[group])
            )
            sends[-1].start()
    for send in sends:
        send.wait()


def to_chips(arrays, devices, before=()):
    tokens, columns = arrays[0].shape
    count, chips, hd = len(arrays), devices // PAIR, columns // devices
    shape = (chips, PAIR * count // 2, tokens, 2 * hd)
    more = min(len(before), 1)
    return pl.pallas_call(
        functools.partial(pack_kernel, count=count, before=len(before)),
        in_specs=[HBM] * (count + len(before)),
        out_specs=[HBM] + [SMEM] * more,
        out_shape=[pltpu.HBM(shape, jnp.bfloat16)]
        + [jax.ShapeDtypeStruct((1,), jnp.int32)] * more,
        scratch_shapes=[
            pltpu.VMEM((count, tokens, columns), jnp.bfloat16),
            pltpu.VMEM((shape[1], chips, tokens, 2 * hd), jnp.bfloat16),
            pltpu.SemaphoreType.DMA((count,)),
            pltpu.SemaphoreType.DMA((shape[1],)),
        ],
        compiler_params=PARAMS,
        cost_estimate=moves(4 * count * tokens * columns),
    )(*pin(*arrays, *before))


def exchange(pieces, devices):
    groups = [list(range(core, devices, PAIR)) for core in range(PAIR)]
    return lax.all_to_all(
        pieces, "heads", split_axis=0, concat_axis=0, axis_index_groups=groups, tiled=True
    )


def unpack_kernel(chip, *refs, order):
    pieces, arrays, sems = refs[: len(order)], refs[len(order) : -1], refs[-1]
    width = pieces[0].shape[1] // len(arrays)
    copies = []
    for k, piece in zip(order, pieces):
        columns = pl.ds(pl.multiple_of((chip[0] ^ k) * width, width), width)
        for a, array in enumerate(arrays):
            source = piece.at[:, a * width : (a + 1) * width]
            copies.append(pltpu.make_async_copy(source, array.at[:, columns], sems.at[k, a]))
            copies[-1].start()
    for copy in copies:
        copy.wait()


def unpack(chip, pieces, count):
    tokens, width = pieces[0].shape
    columns = len(pieces) * width // count
    return pl.pallas_call(
        functools.partial(unpack_kernel, order=list(pieces)),
        in_specs=[SMEM] + [VMEM] * len(pieces),
        out_specs=[HBM] * count,
        out_shape=[pltpu.HBM((tokens, columns), jnp.bfloat16)] * count,
        scratch_shapes=[pltpu.SemaphoreType.DMA((len(pieces), count))],
        compiler_params=PARAMS,
        cost_estimate=moves(4 * len(pieces) * tokens * width),
    )(chip, *pieces.values())


def edge_kernel(start, kv, out, sems):
    copies = []
    for i in range(HB):
        copies.append(pltpu.make_async_copy(kv.at[start[0] + i], out.at[i], sems.at[i]))
    for copy in copies:
        copy.start()
    for copy in copies:
        copy.wait()


def edge(start, kv):
    shape = (HB, *kv.shape[1:])
    return pl.pallas_call(
        edge_kernel,
        in_specs=[SMEM, VMEM],
        out_specs=HBM,
        out_shape=pltpu.HBM(shape, jnp.bfloat16),
        scratch_shapes=[pltpu.SemaphoreType.DMA((HB,))],
        compiler_params=PARAMS,
        cost_estimate=moves(4 * math.prod(shape)),
    )(start, kv)


def attend_kernel(chip, table, q_ref, *refs, sources, halos, later, places, hd):
    tokens = q_ref.shape[2]
    own, refs = refs[0], refs[1:]
    blocks = own.shape[0]
    if sources:
        parts, sems, halo, rest = refs[:sources], refs[-1], refs[-3], refs[-2]
        outs = refs[sources + later : -4]
        copies, row = [], {0: 0, 1: 0}
        for n, ref in enumerate(parts):
            target, core = (halo, 0) if n < halos else (rest, 1)
            place = target.at[pl.ds(row[core], ref.shape[0])]
            copies.append(pltpu.make_async_copy(ref, place, sems.at[n]))
            row[core] += ref.shape[0]
        for copy in copies:
            copy.start()
        for copy in copies:
            copy.wait()
    else:
        halo, rest, outs = refs[0], refs[1], refs[2 + later :]

    def rows(index, group):
        here = own[jnp.minimum(index, blocks - 1), group]
        there = halo[jnp.maximum(index - blocks, 0), group]
        return jnp.concatenate([jnp.where(index < blocks, here, there), rest[index, group]], axis=0)

    scale = hd ** (-0.5)
    factor = scale * math.log2(math.e)
    trans = (((1,), (1,)), ((), ()))

    def products(k, h):
        block = chip[0] ^ k
        both = q_ref[block, h]
        query = both[:, :hd]
        left = jnp.concatenate([jnp.zeros_like(query), query], axis=1)
        left = jnp.concatenate([left, both], axis=0)
        window = [table[block * WK + w] for w in range(WK)]
        scores, tans = [], []
        for index in window:
            keys = rows(index, 2 * h)
            product = lax.dot_general(left, keys, trans, preferred_element_type=jnp.float32)
            scores.append(product[:tokens])
            tans.append(product[tokens:])
        return window, scores, tans

    def finish(k, h, window, scores, tans):
        top = functools.reduce(jnp.maximum, scores)
        top = jnp.max(top, axis=1, keepdims=True) * factor
        probs = [jnp.exp2(s * factor - top) for s in scores]
        weighted = [p * t for p, t in zip(probs, tans)]
        total = jnp.sum(functools.reduce(jnp.add, probs), axis=1, keepdims=True)
        mean = jnp.sum(functools.reduce(jnp.add, weighted), axis=1, keepdims=True)
        mixed = jnp.zeros((2 * tokens, 2 * hd), jnp.float32)
        for index, p, w in zip(window, probs, weighted):
            vals = rows(index, 2 * h + 1)
            right = jnp.concatenate([p.astype(jnp.bfloat16), w.astype(jnp.bfloat16)], axis=0)
            mixed += jnp.dot(right, vals, preferred_element_type=jnp.float32)
        inverse = 1.0 / total
        out = mixed[:tokens, :hd] * inverse
        tan = (mixed[:tokens, hd:] + scale * mixed[tokens:, :hd]) * inverse
        tan = tan - (scale * mean * inverse) * out
        ref = outs[places.index(k)]
        ref[:, h * hd : (h + 1) * hd] = out.astype(jnp.bfloat16)
        ref[:, (PAIR + h) * hd : (PAIR + h + 1) * hd] = tan.astype(jnp.bfloat16)

    units = [(k, h) for k in places for h in range(PAIR)]
    ahead = products(*units[0])
    for unit, following in zip(units, units[1:] + [None]):
        current = ahead
        if following is not None:
            ahead = products(*following)
        finish(*unit, *current)
    if sources:
        refs[-4][...] = outs[0][:LEAD]


def attend(chip, table, queries, own, sources, halos, later, places, first):
    _, _, tokens, pair = queries.shape
    hd, width = pair // 2, PAIR * pair
    elements = len(places) * BQ * WK * BQ
    outs = [jax.ShapeDtypeStruct((tokens, width), jnp.bfloat16)] * len(places)
    scratch, total = [], 0
    if first:
        count = halos
        total = sum(a.shape[0] for a in sources)
        outs.append(jax.ShapeDtypeStruct((LEAD, width), jnp.bfloat16))
        for group in (sources[:count], sources[count:]):
            shape = (sum(a.shape[0] for a in group), *own.shape[1:])
            outs.append(jax.ShapeDtypeStruct(shape, jnp.bfloat16))
        scratch.append(pltpu.SemaphoreType.DMA((len(sources),)))
    return pl.pallas_call(
        functools.partial(
            attend_kernel,
            sources=len(sources) if first else 0,
            halos=halos,
            later=len(later),
            places=places,
            hd=hd,
        ),
        in_specs=[SMEM, SMEM, VMEM, VMEM]
        + [ANY if first else VMEM] * len(sources)
        + [ANY] * len(later),
        out_specs=[VMEM] * len(outs),
        out_shape=outs,
        scratch_shapes=scratch,
        compiler_params=PARAMS,
        cost_estimate=pl.CostEstimate(
            flops=12 * elements * hd,
            bytes_accessed=4 * total * tokens * width,
            transcendentals=elements,
        ),
    )(chip, table, queries, own, *sources, *later)


def locate(neighbors, frame, blocks):
    local = neighbors - frame * blocks
    even = frame % 2 == 0
    before = blocks + jnp.where(even, HB, 0) + local + HB
    after = blocks + jnp.where(even, 0, HB) + local - blocks
    return jnp.where(local < 0, before, jnp.where(local >= blocks, after, local)).reshape(-1)


def per_device(query, keys, values, query_tan, keys_tan, values_tan, neighbors):
    devices, frames = lax.axis_size("heads"), lax.axis_size("frames")
    frame = lax.axis_index("frames")
    chip = (lax.axis_index("heads") // PAIR).reshape(1).astype(jnp.int32)
    blocks = neighbors.shape[0]
    swap = [(d, d ^ 1) for d in range(devices)]
    (kv_sent,) = to_chips([keys_tan, keys, values, values_tan], devices)
    q_sent, zero = to_chips([query, query_tan], devices, [kv_sent])
    kv = exchange(kv_sent, devices)

    mine, rounds = [kv], []
    for first in (0, 1):
        pairs = [(i, i + 1) for i in range(first, frames - 1, 2)]
        if pairs:
            rounds.append(pairs + [(j, i) for i, j in pairs])
            start = jnp.where(frame % 2 == first, blocks - HB, 0).astype(jnp.int32) + zero
            mine.append(lax.ppermute(edge(start, kv), "frames", rounds[-1]))
    other = [lax.ppermute(a, "heads", swap) for a in mine]

    queries = exchange(q_sent, devices)
    table = locate(neighbors, frame, blocks)
    half, middle = blocks // 2, blocks // 2 + blocks // 4
    back, later, sources = {}, [], mine[1:] + other
    calls = (
        range(half, half + 1),
        range(half + 1, middle + 1),
        [*range(middle + 1, blocks), *range(1, half), 0],
    )
    for n, part in enumerate(calls):
        pieces = attend(chip, table, queries, kv, sources, len(rounds), later, list(part), n == 0)
        for k, piece in zip(part, pieces):
            pairs = [(d, d ^ (k * PAIR)) for d in range(devices)]
            back[k] = lax.ppermute(piece, "heads", pairs) if k else piece
        if n == 0:
            later = [lax.ppermute(pieces[-3], "heads", swap)]
            sources = pieces[-2:]
        else:
            later = [back[half]]
    return unpack(chip, back, 2)


def solution(mesh):
    own = P(("frames", "heads"), None)
    return jax.shard_map(
        per_device,
        mesh=mesh,
        in_specs=(own,) * 6 + (P("frames", None),),
        out_specs=(own, own),
        check_vma=False,
    )
```

```python
import functools
import math

import jax
import jax.numpy as jnp
from jax import lax
from jax.experimental import pallas as pl
from jax.experimental.pallas import tpu as pltpu
from jax.sharding import PartitionSpec as P

BQ = 256
WK = 4
HB = 4
PAIR = 2
LEAD = 16
PARAMS = pltpu.CompilerParams(vmem_limit_bytes=32 * 1024 * 1024)
ANY = pl.BlockSpec(memory_space=pl.ANY)
HBM = pl.BlockSpec(memory_space=pltpu.HBM)
VMEM = pl.BlockSpec(memory_space=pltpu.VMEM)
SMEM = pl.BlockSpec(memory_space=pltpu.SMEM)


def pin(*arrays):
    return [pltpu.with_memory_space_constraint(a, pltpu.HBM) for a in arrays]


def moves(size):
    return pl.CostEstimate(flops=0, bytes_accessed=size, transcendentals=0)


def pack_kernel(*refs, count, before):
    arrays, out = refs[:count], refs[count + before]
    held, staged, sems, out_sems = refs[-4:]
    if before:
        refs[count + before + 1][0] = 0
    chips, columns = out.shape[0], held.shape[2]
    hd = columns // chips // PAIR
    copies = [pltpu.make_async_copy(a, held.at[i], sems.at[i]) for i, a in enumerate(arrays)]
    for copy in copies:
        copy.start()
    sends = []
    for stage in range(count // 2):
        pair = (2 * stage, 2 * stage + 1)
        for a in pair:
            copies[a].wait()
        for h in range(PAIR):
            group = h * (count // 2) + stage
            for chip in range(chips):
                source = (chip * PAIR + h) * hd
                for i, a in enumerate(pair):
                    staged[group, chip, :, i * hd : (i + 1) * hd] = held[
                        a, :, source : source + hd
                    ]
            sends.append(
                pltpu.make_async_copy(staged.at[group], out.at[:, group], out_sems.at[group])
            )
            sends[-1].start()
    for send in sends:
        send.wait()


def to_chips(arrays, devices, before=()):
    tokens, columns = arrays[0].shape
    count, chips, hd = len(arrays), devices // PAIR, columns // devices
    shape = (chips, PAIR * count // 2, tokens, 2 * hd)
    more = min(len(before), 1)
    return pl.pallas_call(
        functools.partial(pack_kernel, count=count, before=len(before)),
        in_specs=[HBM] * (count + len(before)),
        out_specs=[HBM] + [SMEM] * more,
        out_shape=[pltpu.HBM(shape, jnp.bfloat16)]
        + [jax.ShapeDtypeStruct((1,), jnp.int32)] * more,
        scratch_shapes=[
            pltpu.VMEM((count, tokens, columns), jnp.bfloat16),
            pltpu.VMEM((shape[1], chips, tokens, 2 * hd), jnp.bfloat16),
            pltpu.SemaphoreType.DMA((count,)),
            pltpu.SemaphoreType.DMA((shape[1],)),
        ],
        compiler_params=PARAMS,
        cost_estimate=moves(4 * count * tokens * columns),
    )(*pin(*arrays, *before))


def exchange(pieces, devices):
    groups = [list(range(core, devices, PAIR)) for core in range(PAIR)]
    return lax.all_to_all(
        pieces, "heads", split_axis=0, concat_axis=0, axis_index_groups=groups, tiled=True
    )


def unpack_kernel(chip, *refs, order):
    pieces, arrays, sems = refs[: len(order)], refs[len(order) : -1], refs[-1]
    width = pieces[0].shape[1] // len(arrays)
    copies = []
    for k, piece in zip(order, pieces):
        columns = pl.ds(pl.multiple_of((chip[0] ^ k) * width, width), width)
        for a, array in enumerate(arrays):
            source = piece.at[:, a * width : (a + 1) * width]
            copies.append(pltpu.make_async_copy(source, array.at[:, columns], sems.at[k, a]))
            copies[-1].start()
    for copy in copies:
        copy.wait()


def unpack(chip, pieces, count):
    tokens, width = pieces[0].shape
    columns = len(pieces) * width // count
    return pl.pallas_call(
        functools.partial(unpack_kernel, order=list(pieces)),
        in_specs=[SMEM] + [VMEM] * len(pieces),
        out_specs=[HBM] * count,
        out_shape=[pltpu.HBM((tokens, columns), jnp.bfloat16)] * count,
        scratch_shapes=[pltpu.SemaphoreType.DMA((len(pieces), count))],
        compiler_params=PARAMS,
        cost_estimate=moves(4 * len(pieces) * tokens * width),
    )(chip, *pieces.values())


def edge_kernel(start, kv, out, sems):
    copies = []
    for i in range(HB):
        copies.append(pltpu.make_async_copy(kv.at[start[0] + i], out.at[i], sems.at[i]))
    for copy in copies:
        copy.start()
    for copy in copies:
        copy.wait()


def edge(start, kv):
    shape = (HB, *kv.shape[1:])
    return pl.pallas_call(
        edge_kernel,
        in_specs=[SMEM, VMEM],
        out_specs=HBM,
        out_shape=pltpu.HBM(shape, jnp.bfloat16),
        scratch_shapes=[pltpu.SemaphoreType.DMA((HB,))],
        compiler_params=PARAMS,
        cost_estimate=moves(4 * math.prod(shape)),
    )(start, kv)


def fetch(parts, halos, table, place, blocks, near, wide, sems):
    for w in range(WK):
        index = table[place + w]
        low = {0: blocks, 1: 0}
        for n, ref in enumerate(parts):
            side, target = (0, near) if n < halos else (1, wide)
            first, size = low[side], ref.shape[0]
            low[side] += size

            @pl.when((index >= first) & (index < first + size))
            def copy(ref=ref, first=first, side=side, target=target, index=index, w=w):
                pltpu.make_async_copy(ref.at[index - first], target.at[w], sems.at[side, w]).start()


def arrive(part, table, place, blocks, near, wide, sems):
    for w in range(WK):
        pltpu.make_async_copy(part.at[0], wide.at[w], sems.at[1, w]).wait()

        @pl.when(table[place + w] >= blocks)
        def wait(w=w):
            pltpu.make_async_copy(part.at[0], near.at[w], sems.at[0, w]).wait()


def attend_kernel(chip, table, q_ref, *refs, sources, halos, later, places, hd):
    tokens = q_ref.shape[2]
    own, refs = refs[0], refs[1:]
    blocks = own.shape[0]
    if sources:
        parts, (halo, rest, near, wide, sems, marks) = refs[:sources], refs[-6:]
        outs = refs[sources + later : -7]
        copies, row = [], {0: 0, 1: 0}
        for n, ref in enumerate(parts):
            target, core = (halo, 0) if n < halos else (rest, 1)
            place = target.at[pl.ds(row[core], ref.shape[0])]
            copies.append(pltpu.make_async_copy(ref, place, sems.at[n]))
            row[core] += ref.shape[0]
        fetch(parts, halos, table, (chip[0] ^ places[0]) * WK, blocks, near, wide, marks)
        for copy in copies:
            copy.start()
        arrive(parts[0], table, (chip[0] ^ places[0]) * WK, blocks, near, wide, marks)
    else:
        halo, rest, outs = refs[0], refs[1], refs[2 + later :]

    def rows(w, index, group):
        here = own[jnp.minimum(index, blocks - 1), group]
        there = near[w, group] if sources else halo[jnp.maximum(index - blocks, 0), group]
        other = wide[w, group] if sources else rest[index, group]
        return jnp.concatenate([jnp.where(index < blocks, here, there), other], axis=0)

    scale = hd ** (-0.5)
    factor = scale * math.log2(math.e)
    trans = (((1,), (1,)), ((), ()))

    def products(k, h):
        block = chip[0] ^ k
        both = q_ref[block, h]
        query = both[:, :hd]
        left = jnp.concatenate([jnp.zeros_like(query), query], axis=1)
        left = jnp.concatenate([left, both], axis=0)
        window = [table[block * WK + w] for w in range(WK)]
        scores, tans = [], []
        for w, index in enumerate(window):
            keys = rows(w, index, 2 * h)
            product = lax.dot_general(left, keys, trans, preferred_element_type=jnp.float32)
            scores.append(product[:tokens])
            tans.append(product[tokens:])
        return window, scores, tans

    def finish(k, h, window, scores, tans):
        top = functools.reduce(jnp.maximum, scores)
        top = jnp.max(top, axis=1, keepdims=True) * factor
        probs = [jnp.exp2(s * factor - top) for s in scores]
        weighted = [p * t for p, t in zip(probs, tans)]
        total = jnp.sum(functools.reduce(jnp.add, probs), axis=1, keepdims=True)
        mean = jnp.sum(functools.reduce(jnp.add, weighted), axis=1, keepdims=True)
        mixed = jnp.zeros((2 * tokens, 2 * hd), jnp.float32)
        for w, (index, p, t) in enumerate(zip(window, probs, weighted)):
            vals = rows(w, index, 2 * h + 1)
            right = jnp.concatenate([p.astype(jnp.bfloat16), t.astype(jnp.bfloat16)], axis=0)
            mixed += jnp.dot(right, vals, preferred_element_type=jnp.float32)
        inverse = 1.0 / total
        out = mixed[:tokens, :hd] * inverse
        tan = (mixed[:tokens, hd:] + scale * mixed[tokens:, :hd]) * inverse
        tan = tan - (scale * mean * inverse) * out
        ref = outs[places.index(k)]
        ref[:, h * hd : (h + 1) * hd] = out.astype(jnp.bfloat16)
        ref[:, (PAIR + h) * hd : (PAIR + h + 1) * hd] = tan.astype(jnp.bfloat16)

    units = [(k, h) for k in places for h in range(PAIR)]
    ahead = products(*units[0])
    for unit, following in zip(units, units[1:] + [None]):
        current = ahead
        if following is not None:
            ahead = products(*following)
        finish(*unit, *current)
    if sources:
        refs[-7][...] = outs[0][:LEAD]
        for copy in copies:
            copy.wait()


def attend(chip, table, queries, own, sources, halos, later, places, first):
    _, _, tokens, pair = queries.shape
    hd, width = pair // 2, PAIR * pair
    elements = len(places) * BQ * WK * BQ
    outs = [jax.ShapeDtypeStruct((tokens, width), jnp.bfloat16)] * len(places)
    scratch, total = [], 0
    if first:
        count = halos
        total = sum(a.shape[0] for a in sources)
        outs.append(jax.ShapeDtypeStruct((LEAD, width), jnp.bfloat16))
        for group in (sources[:count], sources[count:]):
            shape = (sum(a.shape[0] for a in group), *own.shape[1:])
            outs.append(jax.ShapeDtypeStruct(shape, jnp.bfloat16))
        scratch += [pltpu.VMEM((WK, *own.shape[1:]), jnp.bfloat16)] * 2
        scratch += [pltpu.SemaphoreType.DMA((len(sources),)), pltpu.SemaphoreType.DMA((2, WK))]
    return pl.pallas_call(
        functools.partial(
            attend_kernel,
            sources=len(sources) if first else 0,
            halos=halos,
            later=len(later),
            places=places,
            hd=hd,
        ),
        in_specs=[SMEM, SMEM, VMEM, VMEM]
        + [ANY if first else VMEM] * len(sources)
        + [ANY] * len(later),
        out_specs=[VMEM] * len(outs),
        out_shape=outs,
        scratch_shapes=scratch,
        compiler_params=PARAMS,
        cost_estimate=pl.CostEstimate(
            flops=12 * elements * hd,
            bytes_accessed=4 * total * tokens * width,
            transcendentals=elements,
        ),
    )(chip, table, queries, own, *sources, *later)


def locate(neighbors, frame, blocks):
    local = neighbors - frame * blocks
    even = frame % 2 == 0
    before = blocks + jnp.where(even, HB, 0) + local + HB
    after = blocks + jnp.where(even, 0, HB) + local - blocks
    return jnp.where(local < 0, before, jnp.where(local >= blocks, after, local)).reshape(-1)


def per_device(query, keys, values, query_tan, keys_tan, values_tan, neighbors):
    devices, frames = lax.axis_size("heads"), lax.axis_size("frames")
    frame = lax.axis_index("frames")
    chip = (lax.axis_index("heads") // PAIR).reshape(1).astype(jnp.int32)
    blocks = neighbors.shape[0]
    swap = [(d, d ^ 1) for d in range(devices)]
    (kv_sent,) = to_chips([keys_tan, keys, values, values_tan], devices)
    q_sent, zero = to_chips([query, query_tan], devices, [kv_sent])
    kv = exchange(kv_sent, devices)

    mine, rounds = [kv], []
    for first in (0, 1):
        pairs = [(i, i + 1) for i in range(first, frames - 1, 2)]
        if pairs:
            rounds.append(pairs + [(j, i) for i, j in pairs])
            start = jnp.where(frame % 2 == first, blocks - HB, 0).astype(jnp.int32) + zero
            mine.append(lax.ppermute(edge(start, kv), "frames", rounds[-1]))
    other = [lax.ppermute(a, "heads", swap) for a in mine]

    queries = exchange(q_sent, devices)
    table = locate(neighbors, frame, blocks)
    half, middle = blocks // 2, blocks // 2 + blocks // 4
    back, later, sources = {}, [], mine[1:] + other
    calls = (
        range(half, half + 1),
        range(half + 1, middle + 1),
        [*range(middle + 1, blocks), *range(1, half), 0],
    )
    for n, part in enumerate(calls):
        pieces = attend(chip, table, queries, kv, sources, len(rounds), later, list(part), n == 0)
        for k, piece in zip(part, pieces):
            pairs = [(d, d ^ (k * PAIR)) for d in range(devices)]
            back[k] = lax.ppermute(piece, "heads", pairs) if k else piece
        if n == 0:
            later = [lax.ppermute(pieces[-3], "heads", swap)]
            sources = pieces[-2:]
        else:
            later = [back[half]]
    return unpack(chip, back, 2)


def solution(mesh):
    own = P(("frames", "heads"), None)
    return jax.shard_map(
        per_device,
        mesh=mesh,
        in_specs=(own,) * 6 + (P("frames", None),),
        out_specs=(own, own),
        check_vma=False,
    )
```

```python
import functools
import math

import jax
import jax.numpy as jnp
from jax import lax
from jax.experimental import pallas as pl
from jax.experimental.pallas import tpu as pltpu
from jax.sharding import PartitionSpec as P

BQ = 256
WK = 4
HB = 4
PAIR = 2
LEAD = 16
PARAMS = pltpu.CompilerParams(vmem_limit_bytes=32 * 1024 * 1024)
ANY = pl.BlockSpec(memory_space=pl.ANY)
HBM = pl.BlockSpec(memory_space=pltpu.HBM)
VMEM = pl.BlockSpec(memory_space=pltpu.VMEM)
SMEM = pl.BlockSpec(memory_space=pltpu.SMEM)


def pin(*arrays):
    return [pltpu.with_memory_space_constraint(a, pltpu.HBM) for a in arrays]


def moves(size):
    return pl.CostEstimate(flops=0, bytes_accessed=size, transcendentals=0)


def pack_kernel(*refs, count, before):
    arrays, out = refs[:count], refs[count + before]
    held, staged, sems, out_sems = refs[-4:]
    if before:
        refs[count + before + 1][0] = 0
    chips, columns = out.shape[0], held.shape[2]
    hd = columns // chips // PAIR
    copies = [pltpu.make_async_copy(a, held.at[i], sems.at[i]) for i, a in enumerate(arrays)]
    for copy in copies:
        copy.start()
    sends = []
    for stage in range(count // 2):
        pair = (2 * stage, 2 * stage + 1)
        for a in pair:
            copies[a].wait()
        for h in range(PAIR):
            group = h * (count // 2) + stage
            for chip in range(chips):
                source = (chip * PAIR + h) * hd
                for i, a in enumerate(pair):
                    staged[group, chip, :, i * hd : (i + 1) * hd] = held[
                        a, :, source : source + hd
                    ]
            sends.append(
                pltpu.make_async_copy(staged.at[group], out.at[:, group], out_sems.at[group])
            )
            sends[-1].start()
    for send in sends:
        send.wait()


def to_chips(arrays, devices, before=()):
    tokens, columns = arrays[0].shape
    count, chips, hd = len(arrays), devices // PAIR, columns // devices
    shape = (chips, PAIR * count // 2, tokens, 2 * hd)
    more = min(len(before), 1)
    return pl.pallas_call(
        functools.partial(pack_kernel, count=count, before=len(before)),
        in_specs=[HBM] * (count + len(before)),
        out_specs=[HBM] + [SMEM] * more,
        out_shape=[pltpu.HBM(shape, jnp.bfloat16)]
        + [jax.ShapeDtypeStruct((1,), jnp.int32)] * more,
        scratch_shapes=[
            pltpu.VMEM((count, tokens, columns), jnp.bfloat16),
            pltpu.VMEM((shape[1], chips, tokens, 2 * hd), jnp.bfloat16),
            pltpu.SemaphoreType.DMA((count,)),
            pltpu.SemaphoreType.DMA((shape[1],)),
        ],
        compiler_params=PARAMS,
        cost_estimate=moves(4 * count * tokens * columns),
    )(*pin(*arrays, *before))


def exchange(pieces, devices):
    groups = [list(range(core, devices, PAIR)) for core in range(PAIR)]
    return lax.all_to_all(
        pieces, "heads", split_axis=0, concat_axis=0, axis_index_groups=groups, tiled=True
    )


def unpack_kernel(chip, *refs, order):
    pieces, arrays, sems = refs[: len(order)], refs[len(order) : -1], refs[-1]
    width = pieces[0].shape[1] // len(arrays)
    copies = []
    for k, piece in zip(order, pieces):
        columns = pl.ds(pl.multiple_of((chip[0] ^ k) * width, width), width)
        for a, array in enumerate(arrays):
            source = piece.at[:, a * width : (a + 1) * width]
            copies.append(pltpu.make_async_copy(source, array.at[:, columns], sems.at[k, a]))
            copies[-1].start()
    for copy in copies:
        copy.wait()


def unpack(chip, pieces, count):
    tokens, width = pieces[0].shape
    columns = len(pieces) * width // count
    return pl.pallas_call(
        functools.partial(unpack_kernel, order=list(pieces)),
        in_specs=[SMEM] + [VMEM] * len(pieces),
        out_specs=[HBM] * count,
        out_shape=[pltpu.HBM((tokens, columns), jnp.bfloat16)] * count,
        scratch_shapes=[pltpu.SemaphoreType.DMA((len(pieces), count))],
        compiler_params=PARAMS,
        cost_estimate=moves(4 * len(pieces) * tokens * width),
    )(chip, *pieces.values())


def edge_kernel(start, kv, out, sems):
    copies = []
    for i in range(HB):
        copies.append(pltpu.make_async_copy(kv.at[start[0] + i], out.at[i], sems.at[i]))
    for copy in copies:
        copy.start()
    for copy in copies:
        copy.wait()


def edge(start, kv):
    shape = (HB, *kv.shape[1:])
    return pl.pallas_call(
        edge_kernel,
        in_specs=[SMEM, VMEM],
        out_specs=HBM,
        out_shape=pltpu.HBM(shape, jnp.bfloat16),
        scratch_shapes=[pltpu.SemaphoreType.DMA((HB,))],
        compiler_params=PARAMS,
        cost_estimate=moves(4 * math.prod(shape)),
    )(start, kv)


def fetch(parts, halos, table, place, blocks, near, wide, sems):
    for w in range(WK):
        index = table[place + w]
        low = {0: blocks, 1: 0}
        for n, ref in enumerate(parts):
            side, target = (0, near) if n < halos else (1, wide)
            first, size = low[side], ref.shape[0]
            low[side] += size

            @pl.when((index >= first) & (index < first + size))
            def copy(ref=ref, first=first, side=side, target=target, index=index, w=w):
                pltpu.make_async_copy(ref.at[index - first], target.at[w], sems.at[side, w]).start()


def arrive(part, table, place, blocks, near, wide, sems):
    for w in range(WK):
        pltpu.make_async_copy(part.at[0], wide.at[w], sems.at[1, w]).wait()

        @pl.when(table[place + w] >= blocks)
        def wait(w=w):
            pltpu.make_async_copy(part.at[0], near.at[w], sems.at[0, w]).wait()


def attend_kernel(chip, table, q_ref, *refs, sources, halos, later, places, hd):
    tokens = q_ref.shape[2]
    own, refs = refs[0], refs[1:]
    blocks = own.shape[0]
    if sources:
        parts, (halo, rest, near, wide, sems, marks) = refs[:sources], refs[-6:]
        outs = refs[sources + later : -7]
        copies, row = [], {0: 0, 1: 0}
        for n, ref in enumerate(parts):
            target, core = (halo, 0) if n < halos else (rest, 1)
            place = target.at[pl.ds(row[core], ref.shape[0])]
            copies.append(pltpu.make_async_copy(ref, place, sems.at[n]))
            row[core] += ref.shape[0]
        fetch(parts, halos, table, (chip[0] ^ places[0]) * WK, blocks, near, wide, marks)
        for copy in copies:
            copy.start()
        arrive(parts[0], table, (chip[0] ^ places[0]) * WK, blocks, near, wide, marks)
    else:
        halo, rest, outs = refs[0], refs[1], refs[2 + later :]

    def rows(w, index, group):
        here = own[jnp.minimum(index, blocks - 1), group]
        there = near[w, group] if sources else halo[jnp.maximum(index - blocks, 0), group]
        other = wide[w, group] if sources else rest[index, group]
        return jnp.concatenate([jnp.where(index < blocks, here, there), other], axis=0)

    scale = hd ** (-0.5)
    factor = scale * math.log2(math.e)
    trans = (((1,), (1,)), ((), ()))

    def products(k, h):
        block = chip[0] ^ k
        both = q_ref[block, h]
        query = both[:, :hd]
        left = jnp.concatenate([jnp.zeros_like(query), query], axis=1)
        left = jnp.concatenate([left, both], axis=0)
        window = [table[block * WK + w] for w in range(WK)]
        scores, tans = [], []
        for w, index in enumerate(window):
            keys = rows(w, index, 2 * h)
            product = lax.dot_general(left, keys, trans, preferred_element_type=jnp.float32)
            scores.append(product[:tokens])
            tans.append(product[tokens:])
        return window, scores, tans

    def finish(k, h, window, scores, tans):
        top = functools.reduce(jnp.maximum, scores)
        top = jnp.max(top, axis=1, keepdims=True) * factor
        probs = [jnp.exp2(s * factor - top) for s in scores]
        weighted = [p * t for p, t in zip(probs, tans)]
        total = jnp.sum(functools.reduce(jnp.add, probs), axis=1, keepdims=True)
        mean = jnp.sum(functools.reduce(jnp.add, weighted), axis=1, keepdims=True)
        mixed = jnp.zeros((2 * tokens, 2 * hd), jnp.float32)
        for w, (index, p, t) in enumerate(zip(window, probs, weighted)):
            vals = rows(w, index, 2 * h + 1)
            right = jnp.concatenate([p.astype(jnp.bfloat16), t.astype(jnp.bfloat16)], axis=0)
            mixed += jnp.dot(right, vals, preferred_element_type=jnp.float32)
        inverse = 1.0 / total
        out = mixed[:tokens, :hd] * inverse
        tan = (mixed[:tokens, hd:] + scale * mixed[tokens:, :hd]) * inverse
        tan = tan - (scale * mean * inverse) * out
        ref = outs[places.index(k)]
        ref[:, h * hd : (h + 1) * hd] = out.astype(jnp.bfloat16)
        ref[:, (PAIR + h) * hd : (PAIR + h + 1) * hd] = tan.astype(jnp.bfloat16)

    units = [(k, h) for k in places for h in range(PAIR)]
    ahead = products(*units[0])
    for unit, following in zip(units, units[1:] + [None]):
        current = ahead
        if following is not None:
            ahead = products(*following)
        finish(*unit, *current)
    if sources:
        refs[-7][...] = outs[0][:LEAD]
        for copy in copies:
            copy.wait()


def attend(chip, table, queries, own, sources, halos, later, places, first):
    _, _, tokens, pair = queries.shape
    hd, width = pair // 2, PAIR * pair
    elements = len(places) * BQ * WK * BQ
    outs = [jax.ShapeDtypeStruct((tokens, width), jnp.bfloat16)] * len(places)
    scratch, total = [], 0
    if first:
        count = halos
        total = sum(a.shape[0] for a in sources)
        outs.append(jax.ShapeDtypeStruct((LEAD, width), jnp.bfloat16))
        for group in (sources[:count], sources[count:]):
            shape = (sum(a.shape[0] for a in group), *own.shape[1:])
            outs.append(jax.ShapeDtypeStruct(shape, jnp.bfloat16))
        scratch += [pltpu.VMEM((WK, *own.shape[1:]), jnp.bfloat16)] * 2
        scratch += [pltpu.SemaphoreType.DMA((len(sources),)), pltpu.SemaphoreType.DMA((2, WK))]
    return pl.pallas_call(
        functools.partial(
            attend_kernel,
            sources=len(sources) if first else 0,
            halos=halos,
            later=len(later),
            places=places,
            hd=hd,
        ),
        in_specs=[SMEM, SMEM, VMEM, VMEM]
        + [ANY if first else VMEM] * len(sources)
        + [ANY] * len(later),
        out_specs=[VMEM] * len(outs),
        out_shape=outs,
        scratch_shapes=scratch,
        compiler_params=PARAMS,
        cost_estimate=pl.CostEstimate(
            flops=12 * elements * hd,
            bytes_accessed=4 * total * tokens * width,
            transcendentals=elements,
        ),
    )(chip, table, queries, own, *sources, *later)


def locate(neighbors, frame, blocks):
    local = neighbors - frame * blocks
    even = frame % 2 == 0
    before = blocks + jnp.where(even, HB, 0) + local + HB
    after = blocks + jnp.where(even, 0, HB) + local - blocks
    return jnp.where(local < 0, before, jnp.where(local >= blocks, after, local)).reshape(-1)


def per_device(query, keys, values, query_tan, keys_tan, values_tan, neighbors):
    devices, frames = lax.axis_size("heads"), lax.axis_size("frames")
    frame = lax.axis_index("frames")
    chip = (lax.axis_index("heads") // PAIR).reshape(1).astype(jnp.int32)
    blocks = neighbors.shape[0]
    swap = [(d, d ^ 1) for d in range(devices)]
    (kv_sent,) = to_chips([keys_tan, keys, values, values_tan], devices)
    q_sent, zero = to_chips([query, query_tan], devices, [kv_sent])
    kv = exchange(kv_sent, devices)

    mine, rounds = [kv], []
    for first in (0, 1):
        pairs = [(i, i + 1) for i in range(first, frames - 1, 2)]
        if pairs:
            rounds.append(pairs + [(j, i) for i, j in pairs])
            start = jnp.where(frame % 2 == first, blocks - HB, 0).astype(jnp.int32) + zero
            mine.append(lax.ppermute(edge(start, kv), "frames", rounds[-1]))
    other = [lax.ppermute(a, "heads", swap) for a in mine]

    queries = exchange(q_sent, devices)
    table = locate(neighbors, frame, blocks)
    half, middle = blocks // 2, blocks // 2 + blocks // 4
    back, later, sources = {}, [], mine[1:] + other
    far = [*range(middle, blocks), *range(half, middle)]
    cut = 1 + (middle - half)
    calls = (far[:1], far[1:cut], [*far[cut:], *range(1, half), 0])
    for n, part in enumerate(calls):
        pieces = attend(chip, table, queries, kv, sources, len(rounds), later, list(part), n == 0)
        for k, piece in zip(part, pieces):
            pairs = [(d, d ^ (k * PAIR)) for d in range(devices)]
            back[k] = lax.ppermute(piece, "heads", pairs) if k else piece
        if n == 0:
            later = [lax.ppermute(pieces[-3], "heads", swap)]
            sources = pieces[-2:]
        else:
            later = [back[far[0]]]
    return unpack(chip, back, 2)


def solution(mesh):
    own = P(("frames", "heads"), None)
    return jax.shard_map(
        per_device,
        mesh=mesh,
        in_specs=(own,) * 6 + (P("frames", None),),
        out_specs=(own, own),
        check_vma=False,
    )
```

```python
import functools
import math

import jax
import jax.numpy as jnp
from jax import lax
from jax.experimental import pallas as pl
from jax.experimental.pallas import tpu as pltpu
from jax.sharding import PartitionSpec as P

BQ = 256
WK = 4
HB = 4
PAIR = 2
LEAD = 16
PARAMS = pltpu.CompilerParams(vmem_limit_bytes=32 * 1024 * 1024)
ANY = pl.BlockSpec(memory_space=pl.ANY)
HBM = pl.BlockSpec(memory_space=pltpu.HBM)
VMEM = pl.BlockSpec(memory_space=pltpu.VMEM)
SMEM = pl.BlockSpec(memory_space=pltpu.SMEM)


def pin(*arrays):
    return [pltpu.with_memory_space_constraint(a, pltpu.HBM) for a in arrays]


def moves(size):
    return pl.CostEstimate(flops=0, bytes_accessed=size, transcendentals=0)


def pack_kernel(*refs, count, before):
    arrays, out = refs[:count], refs[count + before]
    held, staged, sems, out_sems = refs[-4:]
    if before:
        refs[count + before + 1][0] = 0
    chips, columns = out.shape[0], held.shape[2]
    hd = columns // chips // PAIR
    copies = [pltpu.make_async_copy(a, held.at[i], sems.at[i]) for i, a in enumerate(arrays)]
    for copy in copies:
        copy.start()
    sends = []
    for stage in range(count // 2):
        pair = (2 * stage, 2 * stage + 1)
        for a in pair:
            copies[a].wait()
        for h in range(PAIR):
            group = h * (count // 2) + stage
            for chip in range(chips):
                source = (chip * PAIR + h) * hd
                for i, a in enumerate(pair):
                    staged[group, chip, :, i * hd : (i + 1) * hd] = held[
                        a, :, source : source + hd
                    ]
            sends.append(
                pltpu.make_async_copy(staged.at[group], out.at[:, group], out_sems.at[group])
            )
            sends[-1].start()
    for send in sends:
        send.wait()


def to_chips(arrays, devices, before=()):
    tokens, columns = arrays[0].shape
    count, chips, hd = len(arrays), devices // PAIR, columns // devices
    shape = (chips, PAIR * count // 2, tokens, 2 * hd)
    more = min(len(before), 1)
    return pl.pallas_call(
        functools.partial(pack_kernel, count=count, before=len(before)),
        in_specs=[HBM] * (count + len(before)),
        out_specs=[HBM] + [SMEM] * more,
        out_shape=[pltpu.HBM(shape, jnp.bfloat16)]
        + [jax.ShapeDtypeStruct((1,), jnp.int32)] * more,
        scratch_shapes=[
            pltpu.VMEM((count, tokens, columns), jnp.bfloat16),
            pltpu.VMEM((shape[1], chips, tokens, 2 * hd), jnp.bfloat16),
            pltpu.SemaphoreType.DMA((count,)),
            pltpu.SemaphoreType.DMA((shape[1],)),
        ],
        compiler_params=PARAMS,
        cost_estimate=moves(4 * count * tokens * columns),
    )(*pin(*arrays, *before))


def exchange(pieces, devices):
    groups = [list(range(core, devices, PAIR)) for core in range(PAIR)]
    return lax.all_to_all(
        pieces, "heads", split_axis=0, concat_axis=0, axis_index_groups=groups, tiled=True
    )


def unpack_kernel(chip, *refs, order):
    pieces, arrays, sems = refs[: len(order)], refs[len(order) : -1], refs[-1]
    width = pieces[0].shape[1] // len(arrays)
    copies = []
    for k, piece in zip(order, pieces):
        columns = pl.ds(pl.multiple_of((chip[0] ^ k) * width, width), width)
        for a, array in enumerate(arrays):
            source = piece.at[:, a * width : (a + 1) * width]
            copies.append(pltpu.make_async_copy(source, array.at[:, columns], sems.at[k, a]))
            copies[-1].start()
    for copy in copies:
        copy.wait()


def unpack(chip, pieces, count):
    tokens, width = pieces[0].shape
    columns = len(pieces) * width // count
    return pl.pallas_call(
        functools.partial(unpack_kernel, order=list(pieces)),
        in_specs=[SMEM] + [VMEM] * len(pieces),
        out_specs=[HBM] * count,
        out_shape=[pltpu.HBM((tokens, columns), jnp.bfloat16)] * count,
        scratch_shapes=[pltpu.SemaphoreType.DMA((len(pieces), count))],
        compiler_params=PARAMS,
        cost_estimate=moves(4 * len(pieces) * tokens * width),
    )(chip, *pieces.values())


def edge_kernel(start, kv, out, sems):
    copies = []
    for i in range(HB):
        copies.append(pltpu.make_async_copy(kv.at[start[0] + i], out.at[i], sems.at[i]))
    for copy in copies:
        copy.start()
    for copy in copies:
        copy.wait()


def edge(start, kv):
    shape = (HB, *kv.shape[1:])
    return pl.pallas_call(
        edge_kernel,
        in_specs=[SMEM, VMEM],
        out_specs=HBM,
        out_shape=pltpu.HBM(shape, jnp.bfloat16),
        scratch_shapes=[pltpu.SemaphoreType.DMA((HB,))],
        compiler_params=PARAMS,
        cost_estimate=moves(4 * math.prod(shape)),
    )(start, kv)


def fetch(parts, halos, table, place, blocks, near, wide, sems):
    for w in range(WK):
        index = table[place + w]
        low = {0: blocks, 1: 0}
        for n, ref in enumerate(parts):
            side, target = (0, near) if n < halos else (1, wide)
            first, size = low[side], ref.shape[0]
            low[side] += size

            @pl.when((index >= first) & (index < first + size))
            def copy(ref=ref, first=first, side=side, target=target, index=index, w=w):
                pltpu.make_async_copy(ref.at[index - first], target.at[w], sems.at[side, w]).start()


def arrive(part, table, place, blocks, near, wide, sems):
    for w in range(WK):
        pltpu.make_async_copy(part.at[0], wide.at[w], sems.at[1, w]).wait()

        @pl.when(table[place + w] >= blocks)
        def wait(w=w):
            pltpu.make_async_copy(part.at[0], near.at[w], sems.at[0, w]).wait()


def attend_kernel(chip, table, q_ref, *refs, sources, halos, later, places, hd):
    tokens = q_ref.shape[2]
    own, refs = refs[0], refs[1:]
    blocks = own.shape[0]
    if sources:
        parts, (halo, rest, near, wide, sems, marks) = refs[:sources], refs[-6:]
        outs = refs[sources + later : -7]
        copies, row = [], {0: 0, 1: 0}
        for n, ref in enumerate(parts):
            target, core = (halo, 0) if n < halos else (rest, 1)
            place = target.at[pl.ds(row[core], ref.shape[0])]
            copies.append(pltpu.make_async_copy(ref, place, sems.at[n]))
            row[core] += ref.shape[0]
        fetch(parts, halos, table, (chip[0] ^ places[0]) * WK, blocks, near, wide, marks)
        for copy in copies:
            copy.start()
        arrive(parts[0], table, (chip[0] ^ places[0]) * WK, blocks, near, wide, marks)
    else:
        halo, rest, outs = refs[0], refs[1], refs[2 + later :]

    def rows(w, index, group):
        here = own[jnp.minimum(index, blocks - 1), group]
        there = near[w, group] if sources else halo[jnp.maximum(index - blocks, 0), group]
        other = wide[w, group] if sources else rest[index, group]
        return jnp.concatenate([jnp.where(index < blocks, here, there), other], axis=0)

    scale = hd ** (-0.5)
    factor = scale * math.log2(math.e)
    trans = (((1,), (1,)), ((), ()))

    def products(k, h):
        block = chip[0] ^ k
        both = q_ref[block, h]
        query = both[:, :hd]
        left = jnp.concatenate([jnp.zeros_like(query), query], axis=1)
        left = jnp.concatenate([left, both], axis=0)
        window = [table[block * WK + w] for w in range(WK)]
        scores, tans = [], []
        for w, index in enumerate(window):
            keys = rows(w, index, 2 * h)
            product = lax.dot_general(left, keys, trans, preferred_element_type=jnp.float32)
            scores.append(product[:tokens])
            tans.append(product[tokens:])
        return window, scores, tans

    def finish(k, h, window, scores, tans):
        top = functools.reduce(jnp.maximum, scores)
        top = jnp.max(top, axis=1, keepdims=True) * factor
        probs = [jnp.exp2(s * factor - top) for s in scores]
        weighted = [p * t for p, t in zip(probs, tans)]
        total = jnp.sum(functools.reduce(jnp.add, probs), axis=1, keepdims=True)
        mean = jnp.sum(functools.reduce(jnp.add, weighted), axis=1, keepdims=True)
        mixed = jnp.zeros((2 * tokens, 2 * hd), jnp.float32)
        for w, (index, p, t) in enumerate(zip(window, probs, weighted)):
            vals = rows(w, index, 2 * h + 1)
            right = jnp.concatenate([p.astype(jnp.bfloat16), t.astype(jnp.bfloat16)], axis=0)
            mixed += jnp.dot(right, vals, preferred_element_type=jnp.float32)
        inverse = 1.0 / total
        out = mixed[:tokens, :hd] * inverse
        tan = (mixed[:tokens, hd:] + scale * mixed[tokens:, :hd]) * inverse
        tan = tan - (scale * mean * inverse) * out
        ref = outs[places.index(k)]
        ref[:, h * hd : (h + 1) * hd] = out.astype(jnp.bfloat16)
        ref[:, (PAIR + h) * hd : (PAIR + h + 1) * hd] = tan.astype(jnp.bfloat16)

    units = [(k, h) for k in places for h in range(PAIR)]
    ahead = products(*units[0])
    for unit, following in zip(units, units[1:] + [None]):
        current = ahead
        if following is not None:
            ahead = products(*following)
        finish(*unit, *current)
    if sources:
        refs[-7][...] = outs[0][:LEAD]
        for copy in copies:
            copy.wait()


def attend(chip, table, queries, own, sources, halos, later, places, first):
    _, _, tokens, pair = queries.shape
    hd, width = pair // 2, PAIR * pair
    elements = len(places) * BQ * WK * BQ
    outs = [jax.ShapeDtypeStruct((tokens, width), jnp.bfloat16)] * len(places)
    scratch, total = [], 0
    if first:
        count = halos
        total = sum(a.shape[0] for a in sources)
        outs.append(jax.ShapeDtypeStruct((LEAD, width), jnp.bfloat16))
        for group in (sources[:count], sources[count:]):
            shape = (sum(a.shape[0] for a in group), *own.shape[1:])
            outs.append(jax.ShapeDtypeStruct(shape, jnp.bfloat16))
        scratch += [pltpu.VMEM((WK, *own.shape[1:]), jnp.bfloat16)] * 2
        scratch += [pltpu.SemaphoreType.DMA((len(sources),)), pltpu.SemaphoreType.DMA((2, WK))]
    return pl.pallas_call(
        functools.partial(
            attend_kernel,
            sources=len(sources) if first else 0,
            halos=halos,
            later=len(later),
            places=places,
            hd=hd,
        ),
        in_specs=[SMEM, SMEM, VMEM, VMEM]
        + [ANY if first else VMEM] * len(sources)
        + [ANY] * len(later),
        out_specs=[VMEM] * len(outs),
        out_shape=outs,
        scratch_shapes=scratch,
        compiler_params=PARAMS,
        cost_estimate=pl.CostEstimate(
            flops=12 * elements * hd,
            bytes_accessed=4 * total * tokens * width,
            transcendentals=elements,
        ),
    )(chip, table, queries, own, *sources, *later)


def locate(neighbors, frame, blocks):
    local = neighbors - frame * blocks
    even = frame % 2 == 0
    before = blocks + jnp.where(even, HB, 0) + local + HB
    after = blocks + jnp.where(even, 0, HB) + local - blocks
    return jnp.where(local < 0, before, jnp.where(local >= blocks, after, local)).reshape(-1)


def per_device(query, keys, values, query_tan, keys_tan, values_tan, neighbors):
    devices, frames = lax.axis_size("heads"), lax.axis_size("frames")
    frame = lax.axis_index("frames")
    chip = (lax.axis_index("heads") // PAIR).reshape(1).astype(jnp.int32)
    blocks = neighbors.shape[0]
    swap = [(d, d ^ 1) for d in range(devices)]
    (kv_sent,) = to_chips([keys_tan, keys, values, values_tan], devices)
    q_sent, zero = to_chips([query, query_tan], devices, [kv_sent])
    kv = exchange(kv_sent, devices)

    mine, rounds = [kv], []
    for first in (0, 1):
        pairs = [(i, i + 1) for i in range(first, frames - 1, 2)]
        if pairs:
            rounds.append(pairs + [(j, i) for i, j in pairs])
            start = jnp.where(frame % 2 == first, blocks - HB, 0).astype(jnp.int32) + zero
            mine.append(lax.ppermute(edge(start, kv), "frames", rounds[-1]))
    other = [lax.ppermute(a, "heads", swap) for a in mine]

    queries = exchange(q_sent, devices)
    table = locate(neighbors, frame, blocks)
    half, middle = blocks // 2, blocks // 2 + blocks // 4
    back, later, sources = {}, [], mine[1:] + other
    calls = (
        range(half, half + 1),
        range(half + 1, middle + 1),
        [*range(middle + 1, blocks), *range(half - 1, 0, -1), 0],
    )
    for n, part in enumerate(calls):
        pieces = attend(chip, table, queries, kv, sources, len(rounds), later, list(part), n == 0)
        for k, piece in zip(part, pieces):
            pairs = [(d, d ^ (k * PAIR)) for d in range(devices)]
            back[k] = lax.ppermute(piece, "heads", pairs) if k else piece
        if n == 0:
            later = [lax.ppermute(pieces[-3], "heads", swap)]
            sources = pieces[-2:]
        else:
            later = [back[half]]
    return unpack(chip, back, 2)


def solution(mesh):
    own = P(("frames", "heads"), None)
    return jax.shard_map(
        per_device,
        mesh=mesh,
        in_specs=(own,) * 6 + (P("frames", None),),
        out_specs=(own, own),
        check_vma=False,
    )
```

```python
import functools
import math

import jax
import jax.numpy as jnp
from jax import lax
from jax.experimental import pallas as pl
from jax.experimental.pallas import tpu as pltpu
from jax.sharding import PartitionSpec as P

BQ = 256
WK = 4
HB = 4
PAIR = 2
LEAD = 16
PARAMS = pltpu.CompilerParams(vmem_limit_bytes=32 * 1024 * 1024)
ANY = pl.BlockSpec(memory_space=pl.ANY)
HBM = pl.BlockSpec(memory_space=pltpu.HBM)
VMEM = pl.BlockSpec(memory_space=pltpu.VMEM)
SMEM = pl.BlockSpec(memory_space=pltpu.SMEM)


def pin(*arrays):
    return [pltpu.with_memory_space_constraint(a, pltpu.HBM) for a in arrays]


def moves(size):
    return pl.CostEstimate(flops=0, bytes_accessed=size, transcendentals=0)


def pack_kernel(*refs, count, before):
    arrays, out = refs[:count], refs[count + before]
    held, staged, sems, out_sems = refs[-4:]
    if before:
        refs[count + before + 1][0] = 0
    chips, columns = out.shape[0], held.shape[2]
    hd = columns // chips // PAIR
    copies = [pltpu.make_async_copy(a, held.at[i], sems.at[i]) for i, a in enumerate(arrays)]
    for copy in copies:
        copy.start()
    sends = []
    for stage in range(count // 2):
        pair = (2 * stage, 2 * stage + 1)
        for a in pair:
            copies[a].wait()
        for h in range(PAIR):
            group = h * (count // 2) + stage
            for chip in range(chips):
                source = (chip * PAIR + h) * hd
                for i, a in enumerate(pair):
                    staged[group, chip, :, i * hd : (i + 1) * hd] = held[
                        a, :, source : source + hd
                    ]
            sends.append(
                pltpu.make_async_copy(staged.at[group], out.at[:, group], out_sems.at[group])
            )
            sends[-1].start()
    for send in sends:
        send.wait()


def to_chips(arrays, devices, before=()):
    tokens, columns = arrays[0].shape
    count, chips, hd = len(arrays), devices // PAIR, columns // devices
    shape = (chips, PAIR * count // 2, tokens, 2 * hd)
    more = min(len(before), 1)
    return pl.pallas_call(
        functools.partial(pack_kernel, count=count, before=len(before)),
        in_specs=[HBM] * (count + len(before)),
        out_specs=[HBM] + [SMEM] * more,
        out_shape=[pltpu.HBM(shape, jnp.bfloat16)]
        + [jax.ShapeDtypeStruct((1,), jnp.int32)] * more,
        scratch_shapes=[
            pltpu.VMEM((count, tokens, columns), jnp.bfloat16),
            pltpu.VMEM((shape[1], chips, tokens, 2 * hd), jnp.bfloat16),
            pltpu.SemaphoreType.DMA((count,)),
            pltpu.SemaphoreType.DMA((shape[1],)),
        ],
        compiler_params=PARAMS,
        cost_estimate=moves(4 * count * tokens * columns),
    )(*pin(*arrays, *before))


def exchange(pieces, devices):
    groups = [list(range(core, devices, PAIR)) for core in range(PAIR)]
    return lax.all_to_all(
        pieces, "heads", split_axis=0, concat_axis=0, axis_index_groups=groups, tiled=True
    )


def unpack_kernel(chip, *refs, order):
    pieces, arrays, sems = refs[: len(order)], refs[len(order) : -1], refs[-1]
    width = pieces[0].shape[1] // len(arrays)
    copies = []
    for k, piece in zip(order, pieces):
        columns = pl.ds(pl.multiple_of((chip[0] ^ k) * width, width), width)
        for a, array in enumerate(arrays):
            source = piece.at[:, a * width : (a + 1) * width]
            copies.append(pltpu.make_async_copy(source, array.at[:, columns], sems.at[k, a]))
            copies[-1].start()
    for copy in copies:
        copy.wait()


def unpack(chip, pieces, count):
    tokens, width = pieces[0].shape
    columns = len(pieces) * width // count
    return pl.pallas_call(
        functools.partial(unpack_kernel, order=list(pieces)),
        in_specs=[SMEM] + [VMEM] * len(pieces),
        out_specs=[HBM] * count,
        out_shape=[pltpu.HBM((tokens, columns), jnp.bfloat16)] * count,
        scratch_shapes=[pltpu.SemaphoreType.DMA((len(pieces), count))],
        compiler_params=PARAMS,
        cost_estimate=moves(4 * len(pieces) * tokens * width),
    )(chip, *pieces.values())


def edge_kernel(start, kv, out, sems):
    copies = []
    for i in range(HB):
        copies.append(pltpu.make_async_copy(kv.at[start[0] + i], out.at[i], sems.at[i]))
    for copy in copies:
        copy.start()
    for copy in copies:
        copy.wait()


def edge(start, kv):
    shape = (HB, *kv.shape[1:])
    return pl.pallas_call(
        edge_kernel,
        in_specs=[SMEM, VMEM],
        out_specs=HBM,
        out_shape=pltpu.HBM(shape, jnp.bfloat16),
        scratch_shapes=[pltpu.SemaphoreType.DMA((HB,))],
        compiler_params=PARAMS,
        cost_estimate=moves(4 * math.prod(shape)),
    )(start, kv)


def fetch(parts, halos, table, place, blocks, near, wide, sems):
    for w in range(WK):
        index = table[place + w]
        low = {0: blocks, 1: 0}
        for n, ref in enumerate(parts):
            side, target = (0, near) if n < halos else (1, wide)
            first, size = low[side], ref.shape[0]
            low[side] += size

            @pl.when((index >= first) & (index < first + size))
            def copy(ref=ref, first=first, side=side, target=target, index=index, w=w):
                pltpu.make_async_copy(ref.at[index - first], target.at[w], sems.at[side, w]).start()


def arrive(part, table, place, blocks, near, wide, sems):
    for w in range(WK):
        pltpu.make_async_copy(part.at[0], wide.at[w], sems.at[1, w]).wait()

        @pl.when(table[place + w] >= blocks)
        def wait(w=w):
            pltpu.make_async_copy(part.at[0], near.at[w], sems.at[0, w]).wait()


def attend_kernel(chip, table, q_ref, *refs, sources, halos, later, places, hd):
    tokens = q_ref.shape[2]
    own, refs = refs[0], refs[1:]
    blocks = own.shape[0]
    if sources:
        parts, (halo, rest, near, wide, sems, marks) = refs[:sources], refs[-6:]
        outs = refs[sources + later : -7]
        copies, row = [], {0: 0, 1: 0}
        for n, ref in enumerate(parts):
            target, core = (halo, 0) if n < halos else (rest, 1)
            place = target.at[pl.ds(row[core], ref.shape[0])]
            copies.append(pltpu.make_async_copy(ref, place, sems.at[n]))
            row[core] += ref.shape[0]
        fetch(parts, halos, table, (chip[0] ^ places[0]) * WK, blocks, near, wide, marks)
        for copy in copies:
            copy.start()
        arrive(parts[0], table, (chip[0] ^ places[0]) * WK, blocks, near, wide, marks)
    else:
        halo, rest, outs = refs[0], refs[1], refs[2 + later :]

    def rows(w, index, group):
        here = own[jnp.minimum(index, blocks - 1), group]
        there = near[w, group] if sources else halo[jnp.maximum(index - blocks, 0), group]
        other = wide[w, group] if sources else rest[index, group]
        return jnp.concatenate([jnp.where(index < blocks, here, there), other], axis=0)

    scale = hd ** (-0.5)
    factor = scale * math.log2(math.e)
    trans = (((1,), (1,)), ((), ()))

    def products(k, h):
        block = chip[0] ^ k
        both = q_ref[block, h]
        query = both[:, :hd]
        left = jnp.concatenate([jnp.zeros_like(query), query], axis=1)
        left = jnp.concatenate([left, both], axis=0)
        window = [table[block * WK + w] for w in range(WK)]
        scores, tans = [], []
        for w, index in enumerate(window):
            keys = rows(w, index, 2 * h)
            product = lax.dot_general(left, keys, trans, preferred_element_type=jnp.float32)
            scores.append(product[:tokens])
            tans.append(product[tokens:])
        return window, scores, tans

    def finish(k, h, window, scores, tans):
        top = functools.reduce(jnp.maximum, scores)
        top = jnp.max(top, axis=1, keepdims=True) * factor
        probs = [jnp.exp2(s * factor - top) for s in scores]
        weighted = [p * t for p, t in zip(probs, tans)]
        total = jnp.sum(functools.reduce(jnp.add, probs), axis=1, keepdims=True)
        mean = jnp.sum(functools.reduce(jnp.add, weighted), axis=1, keepdims=True)
        mixed = jnp.zeros((2 * tokens, 2 * hd), jnp.float32)
        for w, (index, p, t) in enumerate(zip(window, probs, weighted)):
            vals = rows(w, index, 2 * h + 1)
            right = jnp.concatenate([p.astype(jnp.bfloat16), t.astype(jnp.bfloat16)], axis=0)
            mixed += jnp.dot(right, vals, preferred_element_type=jnp.float32)
        inverse = 1.0 / total
        out = mixed[:tokens, :hd] * inverse
        tan = (mixed[:tokens, hd:] + scale * mixed[tokens:, :hd]) * inverse
        tan = tan - (scale * mean * inverse) * out
        ref = outs[places.index(k)]
        ref[:, h * hd : (h + 1) * hd] = out.astype(jnp.bfloat16)
        ref[:, (PAIR + h) * hd : (PAIR + h + 1) * hd] = tan.astype(jnp.bfloat16)

    units = [(k, h) for k in places for h in range(PAIR)]
    ahead = products(*units[0])
    for unit, following in zip(units, units[1:] + [None]):
        current = ahead
        if following is not None:
            ahead = products(*following)
        finish(*unit, *current)
    if sources:
        refs[-7][...] = outs[0][:LEAD]
        for copy in copies:
            copy.wait()


def attend(chip, table, queries, own, sources, halos, later, places, first):
    _, _, tokens, pair = queries.shape
    hd, width = pair // 2, PAIR * pair
    elements = len(places) * BQ * WK * BQ
    outs = [jax.ShapeDtypeStruct((tokens, width), jnp.bfloat16)] * len(places)
    scratch, total = [], 0
    if first:
        count = halos
        total = sum(a.shape[0] for a in sources)
        outs.append(jax.ShapeDtypeStruct((LEAD, width), jnp.bfloat16))
        for group in (sources[:count], sources[count:]):
            shape = (sum(a.shape[0] for a in group), *own.shape[1:])
            outs.append(jax.ShapeDtypeStruct(shape, jnp.bfloat16))
        scratch += [pltpu.VMEM((WK, *own.shape[1:]), jnp.bfloat16)] * 2
        scratch += [pltpu.SemaphoreType.DMA((len(sources),)), pltpu.SemaphoreType.DMA((2, WK))]
    return pl.pallas_call(
        functools.partial(
            attend_kernel,
            sources=len(sources) if first else 0,
            halos=halos,
            later=len(later),
            places=places,
            hd=hd,
        ),
        in_specs=[SMEM, SMEM, VMEM, VMEM]
        + [ANY if first else VMEM] * len(sources)
        + [ANY] * len(later),
        out_specs=[VMEM] * len(outs),
        out_shape=outs,
        scratch_shapes=scratch,
        compiler_params=PARAMS,
        cost_estimate=pl.CostEstimate(
            flops=12 * elements * hd,
            bytes_accessed=4 * total * tokens * width,
            transcendentals=elements,
        ),
    )(chip, table, queries, own, *sources, *later)


def locate(neighbors, frame, blocks):
    local = neighbors - frame * blocks
    even = frame % 2 == 0
    before = blocks + jnp.where(even, HB, 0) + local + HB
    after = blocks + jnp.where(even, 0, HB) + local - blocks
    return jnp.where(local < 0, before, jnp.where(local >= blocks, after, local)).reshape(-1)


def per_device(query, keys, values, query_tan, keys_tan, values_tan, neighbors):
    devices, frames = lax.axis_size("heads"), lax.axis_size("frames")
    frame = lax.axis_index("frames")
    chip = (lax.axis_index("heads") // PAIR).reshape(1).astype(jnp.int32)
    blocks = neighbors.shape[0]
    swap = [(d, d ^ 1) for d in range(devices)]
    (kv_sent,) = to_chips([keys_tan, keys, values, values_tan], devices)
    q_sent, zero = to_chips([query, query_tan], devices, [kv_sent])
    kv = exchange(kv_sent, devices)

    mine, rounds = [kv], []
    for first in (0, 1):
        pairs = [(i, i + 1) for i in range(first, frames - 1, 2)]
        if pairs:
            rounds.append(pairs + [(j, i) for i, j in pairs])
            start = jnp.where(frame % 2 == first, blocks - HB, 0).astype(jnp.int32) + zero
            mine.append(lax.ppermute(edge(start, kv), "frames", rounds[-1]))
    other = [lax.ppermute(a, "heads", swap) for a in mine]

    queries = exchange(q_sent, devices)
    table = locate(neighbors, frame, blocks)
    half, middle = blocks // 2, blocks // 2 + blocks // 4
    back, later, sources = {}, [], mine[1:] + other
    calls = (
        range(half, half + 1),
        [*range(half + 1, middle + 1), half - 1],
        [*range(middle + 1, blocks), *range(half - 2, 0, -1), 0],
    )
    for n, part in enumerate(calls):
        pieces = attend(chip, table, queries, kv, sources, len(rounds), later, list(part), n == 0)
        for k, piece in zip(part, pieces):
            pairs = [(d, d ^ (k * PAIR)) for d in range(devices)]
            back[k] = lax.ppermute(piece, "heads", pairs) if k else piece
        if n == 0:
            later = [lax.ppermute(pieces[-3], "heads", swap)]
            sources = pieces[-2:]
        else:
            later = [back[half]]
    return unpack(chip, back, 2)


def solution(mesh):
    own = P(("frames", "heads"), None)
    return jax.shard_map(
        per_device,
        mesh=mesh,
        in_specs=(own,) * 6 + (P("frames", None),),
        out_specs=(own, own),
        check_vma=False,
    )
```

```python
import functools
import math

import jax
import jax.numpy as jnp
from jax import lax
from jax.experimental import pallas as pl
from jax.experimental.pallas import tpu as pltpu
from jax.sharding import PartitionSpec as P

BQ = 256
WK = 4
HB = 4
PAIR = 2
LEAD = 16
PARAMS = pltpu.CompilerParams(vmem_limit_bytes=32 * 1024 * 1024)
ANY = pl.BlockSpec(memory_space=pl.ANY)
HBM = pl.BlockSpec(memory_space=pltpu.HBM)
VMEM = pl.BlockSpec(memory_space=pltpu.VMEM)
SMEM = pl.BlockSpec(memory_space=pltpu.SMEM)


def pin(*arrays):
    return [pltpu.with_memory_space_constraint(a, pltpu.HBM) for a in arrays]


def moves(size):
    return pl.CostEstimate(flops=0, bytes_accessed=size, transcendentals=0)


def pack_kernel(*refs, count, before):
    arrays, out = refs[:count], refs[count + before]
    held, staged, sems, out_sems = refs[-4:]
    if before:
        refs[count + before + 1][0] = 0
    chips, columns = out.shape[0], held.shape[2]
    hd = columns // chips // PAIR
    copies = [pltpu.make_async_copy(a, held.at[i], sems.at[i]) for i, a in enumerate(arrays)]
    for copy in copies:
        copy.start()
    sends = []
    for stage in range(count // 2):
        pair = (2 * stage, 2 * stage + 1)
        for a in pair:
            copies[a].wait()
        for h in range(PAIR):
            group = h * (count // 2) + stage
            for chip in range(chips):
                source = (chip * PAIR + h) * hd
                for i, a in enumerate(pair):
                    staged[group, chip, :, i * hd : (i + 1) * hd] = held[
                        a, :, source : source + hd
                    ]
            sends.append(
                pltpu.make_async_copy(staged.at[group], out.at[:, group], out_sems.at[group])
            )
            sends[-1].start()
    for send in sends:
        send.wait()


def to_chips(arrays, devices, before=()):
    tokens, columns = arrays[0].shape
    count, chips, hd = len(arrays), devices // PAIR, columns // devices
    shape = (chips, PAIR * count // 2, tokens, 2 * hd)
    more = min(len(before), 1)
    return pl.pallas_call(
        functools.partial(pack_kernel, count=count, before=len(before)),
        in_specs=[HBM] * (count + len(before)),
        out_specs=[HBM] + [SMEM] * more,
        out_shape=[pltpu.HBM(shape, jnp.bfloat16)]
        + [jax.ShapeDtypeStruct((1,), jnp.int32)] * more,
        scratch_shapes=[
            pltpu.VMEM((count, tokens, columns), jnp.bfloat16),
            pltpu.VMEM((shape[1], chips, tokens, 2 * hd), jnp.bfloat16),
            pltpu.SemaphoreType.DMA((count,)),
            pltpu.SemaphoreType.DMA((shape[1],)),
        ],
        compiler_params=PARAMS,
        cost_estimate=moves(4 * count * tokens * columns),
    )(*pin(*arrays, *before))


def exchange(pieces, devices):
    groups = [list(range(core, devices, PAIR)) for core in range(PAIR)]
    return lax.all_to_all(
        pieces, "heads", split_axis=0, concat_axis=0, axis_index_groups=groups, tiled=True
    )


def unpack_kernel(chip, *refs, order):
    pieces, arrays, sems = refs[: len(order)], refs[len(order) : -1], refs[-1]
    width = pieces[0].shape[1] // len(arrays)
    copies = []
    for k, piece in zip(order, pieces):
        columns = pl.ds(pl.multiple_of((chip[0] ^ k) * width, width), width)
        for a, array in enumerate(arrays):
            source = piece.at[:, a * width : (a + 1) * width]
            copies.append(pltpu.make_async_copy(source, array.at[:, columns], sems.at[k, a]))
            copies[-1].start()
    for copy in copies:
        copy.wait()


def unpack(chip, pieces, count):
    tokens, width = pieces[0].shape
    columns = len(pieces) * width // count
    return pl.pallas_call(
        functools.partial(unpack_kernel, order=list(pieces)),
        in_specs=[SMEM] + [VMEM] * len(pieces),
        out_specs=[HBM] * count,
        out_shape=[pltpu.HBM((tokens, columns), jnp.bfloat16)] * count,
        scratch_shapes=[pltpu.SemaphoreType.DMA((len(pieces), count))],
        compiler_params=PARAMS,
        cost_estimate=moves(4 * len(pieces) * tokens * width),
    )(chip, *pieces.values())


def edge_kernel(start, kv, out, sems):
    copies = []
    for i in range(HB):
        copies.append(pltpu.make_async_copy(kv.at[start[0] + i], out.at[i], sems.at[i]))
    for copy in copies:
        copy.start()
    for copy in copies:
        copy.wait()


def edge(start, kv):
    shape = (HB, *kv.shape[1:])
    return pl.pallas_call(
        edge_kernel,
        in_specs=[SMEM, VMEM],
        out_specs=HBM,
        out_shape=pltpu.HBM(shape, jnp.bfloat16),
        scratch_shapes=[pltpu.SemaphoreType.DMA((HB,))],
        compiler_params=PARAMS,
        cost_estimate=moves(4 * math.prod(shape)),
    )(start, kv)


def fetch(parts, halos, table, place, blocks, near, wide, sems):
    for w in range(WK):
        index = table[place + w]
        low = {0: blocks, 1: 0}
        for n, ref in enumerate(parts):
            side, target = (0, near) if n < halos else (1, wide)
            first, size = low[side], ref.shape[0]
            low[side] += size

            @pl.when((index >= first) & (index < first + size))
            def copy(ref=ref, first=first, side=side, target=target, index=index, w=w):
                pltpu.make_async_copy(ref.at[index - first], target.at[w], sems.at[side, w]).start()


def arrive(part, table, place, blocks, near, wide, sems):
    for w in range(WK):
        pltpu.make_async_copy(part.at[0], wide.at[w], sems.at[1, w]).wait()

        @pl.when(table[place + w] >= blocks)
        def wait(w=w):
            pltpu.make_async_copy(part.at[0], near.at[w], sems.at[0, w]).wait()


def attend_kernel(chip, table, q_ref, *refs, sources, halos, later, places, hd):
    tokens = q_ref.shape[2]
    own, refs = refs[0], refs[1:]
    blocks = own.shape[0]
    if sources:
        parts, (halo, rest, near, wide, sems, marks) = refs[:sources], refs[-6:]
        outs = refs[sources + later : -7]
        copies, row = [], {0: 0, 1: 0}
        for n, ref in enumerate(parts):
            target, core = (halo, 0) if n < halos else (rest, 1)
            place = target.at[pl.ds(row[core], ref.shape[0])]
            copies.append(pltpu.make_async_copy(ref, place, sems.at[n]))
            row[core] += ref.shape[0]
        fetch(parts, halos, table, (chip[0] ^ places[0]) * WK, blocks, near, wide, marks)
        for copy in copies:
            copy.start()
        arrive(parts[0], table, (chip[0] ^ places[0]) * WK, blocks, near, wide, marks)
    else:
        halo, rest, outs = refs[0], refs[1], refs[2 + later :]

    def rows(w, index, group):
        here = own[jnp.minimum(index, blocks - 1), group]
        there = near[w, group] if sources else halo[jnp.maximum(index - blocks, 0), group]
        other = wide[w, group] if sources else rest[index, group]
        return jnp.concatenate([jnp.where(index < blocks, here, there), other], axis=0)

    scale = hd ** (-0.5)
    factor = scale * math.log2(math.e)
    trans = (((1,), (1,)), ((), ()))

    def products(k, h):
        block = chip[0] ^ k
        both = q_ref[block, h]
        query = both[:, :hd]
        left = jnp.concatenate([jnp.zeros_like(query), query], axis=1)
        left = jnp.concatenate([left, both], axis=0)
        window = [table[block * WK + w] for w in range(WK)]
        scores, tans = [], []
        for w, index in enumerate(window):
            keys = rows(w, index, 2 * h)
            product = lax.dot_general(left, keys, trans, preferred_element_type=jnp.float32)
            scores.append(product[:tokens])
            tans.append(product[tokens:])
        return window, scores, tans

    def finish(k, h, window, scores, tans):
        top = functools.reduce(jnp.maximum, scores)
        top = jnp.max(top, axis=1, keepdims=True) * factor
        probs = [jnp.exp2(s * factor - top) for s in scores]
        weighted = [p * t for p, t in zip(probs, tans)]
        total = jnp.sum(functools.reduce(jnp.add, probs), axis=1, keepdims=True)
        mean = jnp.sum(functools.reduce(jnp.add, weighted), axis=1, keepdims=True)
        mixed = jnp.zeros((2 * tokens, 2 * hd), jnp.float32)
        for w, (index, p, t) in enumerate(zip(window, probs, weighted)):
            vals = rows(w, index, 2 * h + 1)
            right = jnp.concatenate([p.astype(jnp.bfloat16), t.astype(jnp.bfloat16)], axis=0)
            mixed += jnp.dot(right, vals, preferred_element_type=jnp.float32)
        inverse = 1.0 / total
        out = mixed[:tokens, :hd] * inverse
        tan = (mixed[:tokens, hd:] + scale * mixed[tokens:, :hd]) * inverse
        tan = tan - (scale * mean * inverse) * out
        ref = outs[places.index(k)]
        ref[:, h * hd : (h + 1) * hd] = out.astype(jnp.bfloat16)
        ref[:, (PAIR + h) * hd : (PAIR + h + 1) * hd] = tan.astype(jnp.bfloat16)

    units = [(k, h) for k in places for h in range(PAIR)]
    ahead = products(*units[0])
    for unit, following in zip(units, units[1:] + [None]):
        current = ahead
        if following is not None:
            ahead = products(*following)
        finish(*unit, *current)
    if sources:
        refs[-7][...] = outs[0][:LEAD]
        for copy in copies:
            copy.wait()


def attend(chip, table, queries, own, sources, halos, later, places, first):
    _, _, tokens, pair = queries.shape
    hd, width = pair // 2, PAIR * pair
    elements = len(places) * BQ * WK * BQ
    outs = [jax.ShapeDtypeStruct((tokens, width), jnp.bfloat16)] * len(places)
    scratch, total = [], 0
    if first:
        count = halos
        total = sum(a.shape[0] for a in sources)
        outs.append(jax.ShapeDtypeStruct((LEAD, width), jnp.bfloat16))
        for group in (sources[:count], sources[count:]):
            shape = (sum(a.shape[0] for a in group), *own.shape[1:])
            outs.append(jax.ShapeDtypeStruct(shape, jnp.bfloat16))
        scratch += [pltpu.VMEM((WK, *own.shape[1:]), jnp.bfloat16)] * 2
        scratch += [pltpu.SemaphoreType.DMA((len(sources),)), pltpu.SemaphoreType.DMA((2, WK))]
    return pl.pallas_call(
        functools.partial(
            attend_kernel,
            sources=len(sources) if first else 0,
            halos=halos,
            later=len(later),
            places=places,
            hd=hd,
        ),
        in_specs=[SMEM, SMEM, VMEM, VMEM]
        + [ANY if first else VMEM] * len(sources)
        + [ANY] * len(later),
        out_specs=[VMEM] * len(outs),
        out_shape=outs,
        scratch_shapes=scratch,
        compiler_params=PARAMS,
        cost_estimate=pl.CostEstimate(
            flops=12 * elements * hd,
            bytes_accessed=4 * total * tokens * width,
            transcendentals=elements,
        ),
    )(chip, table, queries, own, *sources, *later)


def locate(neighbors, frame, blocks):
    local = neighbors - frame * blocks
    even = frame % 2 == 0
    before = blocks + jnp.where(even, HB, 0) + local + HB
    after = blocks + jnp.where(even, 0, HB) + local - blocks
    return jnp.where(local < 0, before, jnp.where(local >= blocks, after, local)).reshape(-1)


def per_device(query, keys, values, query_tan, keys_tan, values_tan, neighbors):
    devices, frames = lax.axis_size("heads"), lax.axis_size("frames")
    frame = lax.axis_index("frames")
    chip = (lax.axis_index("heads") // PAIR).reshape(1).astype(jnp.int32)
    blocks = neighbors.shape[0]
    swap = [(d, d ^ 1) for d in range(devices)]
    (kv_sent,) = to_chips([keys_tan, keys, values, values_tan], devices)
    q_sent, zero = to_chips([query, query_tan], devices, [kv_sent])
    kv = exchange(kv_sent, devices)

    mine, rounds = [kv], []
    for first in (0, 1):
        pairs = [(i, i + 1) for i in range(first, frames - 1, 2)]
        if pairs:
            rounds.append(pairs + [(j, i) for i, j in pairs])
            start = jnp.where(frame % 2 == first, blocks - HB, 0).astype(jnp.int32) + zero
            mine.append(lax.ppermute(edge(start, kv), "frames", rounds[-1]))
    other = [lax.ppermute(a, "heads", swap) for a in mine]

    queries = exchange(q_sent, devices)
    table = locate(neighbors, frame, blocks)
    half, middle = blocks // 2, blocks // 2 + blocks // 4
    back, later, sources = {}, [], mine[1:] + other
    calls = (
        range(half, half + 1),
        [*range(half + 1, middle + 1), *range(half - 1, half // 2 - 1, -1)],
        [*range(middle + 1, blocks), *range(half // 2 - 1, 0, -1), 0],
    )
    for n, part in enumerate(calls):
        pieces = attend(chip, table, queries, kv, sources, len(rounds), later, list(part), n == 0)
        for k, piece in zip(part, pieces):
            pairs = [(d, d ^ (k * PAIR)) for d in range(devices)]
            back[k] = lax.ppermute(piece, "heads", pairs) if k else piece
        if n == 0:
            later = [lax.ppermute(pieces[-3], "heads", swap)]
            sources = pieces[-2:]
        else:
            later = [back[half]]
    return unpack(chip, back, 2)


def solution(mesh):
    own = P(("frames", "heads"), None)
    return jax.shard_map(
        per_device,
        mesh=mesh,
        in_specs=(own,) * 6 + (P("frames", None),),
        out_specs=(own, own),
        check_vma=False,
    )
```
